32 devices in a mesh: wide: 8 (over z, y), narrow: 4 (over x, core).
Axes of the slice: x: 2, y: 2, z: 4, core: 2. Of those that a mesh axis runs over, the one named last changes fastest.
Arguments:
- hidden: bfloat16 [128, 512, 768], P(('wide', 'narrow')), may hold values from -6 to 6
- lengths: int32 [128], P(('wide', 'narrow')), may hold values from 1 to 512, 22528 in all
- cotangent: bfloat16 [128, 256, 768], P(('wide', 'narrow')), may hold values from -6 to 6
- inflow: bfloat16 [3, 768, 768], P(None, ('wide', 'narrow')), may hold values from -0.21875 to 0.21875
- outflow: bfloat16 [768, 768], P(('wide', 'narrow')), may hold values from -1.75 to 1.75
- widener: bfloat16 [768, 3072], P(('wide', 'narrow')), may hold values from -0.21875 to 0.21875
- narrower: bfloat16 [3072, 768], P(('wide', 'narrow')), may hold values from -0.109375 to 0.109375
- shifts: bfloat16 [8, 768], P(None, ('wide', 'narrow')), may hold values from -1.5 to 1.5, as said below
- offsets: bfloat16 [3072], P(('wide', 'narrow')), may hold values from -3 to 3
- distance: bfloat16 [384], P(('wide', 'narrow')), may hold values from -4 to 4
- intake: bfloat16 [3, 768, 768], P(None, ('wide', 'narrow')), may hold values from -0.21875 to 0.21875
- outtake: bfloat16 [768, 768], P(('wide', 'narrow')), may hold values from -1.75 to 1.75
- expander: bfloat16 [768, 3072], P(('wide', 'narrow')), may hold values from -0.21875 to 0.21875
- squeezer: bfloat16 [3072, 768], P(('wide', 'narrow')), may hold values from -0.109375 to 0.109375
- adjusts: bfloat16 [8, 768], P(None, ('wide', 'narrow')), may hold values from -1.5 to 1.5, as said below
- leanings: bfloat16 [3072], P(('wide', 'narrow')), may hold values from -3 to 3
- spacing: bfloat16 [384], P(('wide', 'narrow')), may hold values from -4 to 4
Outputs:
- pooled_layer: bfloat16 [128, 256, 768], P(('wide', 'narrow'))
- full_layer: bfloat16 [128, 256, 768], P(('wide', 'narrow'))
- hidden_grad: float32 [128, 512, 768], P(('wide', 'narrow'))
- inflow_grad: float32 [3, 768, 768], P(None, ('wide', 'narrow'))
- outflow_grad: float32 [768, 768], P(('wide', 'narrow'))
- widener_grad: float32 [768, 3072], P(('wide', 'narrow'))
- narrower_grad: float32 [3072, 768], P(('wide', 'narrow'))
- shifts_grad: float32 [8, 768], P(None, ('wide', 'narrow'))
- offsets_grad: float32 [3072], P(('wide', 'narrow'))
- distance_grad: float32 [384], P(('wide', 'narrow'))
- intake_grad: float32 [3, 768, 768], P(None, ('wide', 'narrow'))
- outtake_grad: float32 [768, 768], P(('wide', 'narrow'))
- expander_grad: float32 [768, 3072], P(('wide', 'narrow'))
- squeezer_grad: float32 [3072, 768], P(('wide', 'narrow'))
- adjusts_grad: float32 [7, 768], P(None, ('wide', 'narrow'))
- leanings_grad: float32 [3072], P(('wide', 'narrow'))
- spacing_grad: float32 [384], P(('wide', 'narrow'))
- query_bias_grad: float32 [768], P(('wide', 'narrow'))
The draws below stay inside these ranges and needn't reach their ends.
Inputs may be any that keep to these rules, and one draw needn't show every extreme that they name: `lengths`: the longest row has exactly 512 real tokens. `shifts`: rows 3 and 6 are norm gains between 0.6 and 1.4; the other rows are biases. `adjusts`: rows 3 and 6 are norm gains between 0.6 and 1.4; the other rows are biases.
All inputs are finite; a program needn't handle non-finite values. No bound on the sum of `lengths` on one device may be relied on, other than what follows from the above.
Results may differ from the reference program's by a relative error of at most 0.035.
Values may be sent and summed in bfloat16 or wider, within the bound.
No kernel may reach another device: no remote copies, remote signals or barrier semaphores. Data moves between devices by JAX's collectives and lax.ppermute only.
A program may use at most 320 MiB of HBM per device.

```python
import math
from functools import partial
import jax
import jax.numpy as jnp
import numpy as np
from jax import lax

D = 768
H = 12
HD = 64
FF = 3072
NB = 32
LEN = 512
LQ = 256
ROWS = 128


def vector_bank(key):
    base = jnp.clip(jax.random.normal(jax.random.fold_in(key, 1), (8, D), jnp.float32) * 0.5, -1.5, 1.5)
    gains = jax.random.uniform(jax.random.fold_in(key, 2), (8, D), jnp.float32, 0.6, 1.4)
    row = jnp.arange(8)[:, None]
    pick = (row == 3) | (row == 6)
    return jnp.where(pick, gains, base).astype(jnp.bfloat16)


def draw_shifts(key, part):
    return vector_bank(jax.random.fold_in(key, 11))


def draw_adjusts(key, part):
    return vector_bank(jax.random.fold_in(key, 23))


def block_scale(rng, dims, cuts, smallest, largest):
    def one(position, blocks):
        heights = jax.random.uniform(jax.random.fold_in(jax.random.fold_in(rng, 6), position), (blocks,), jnp.float32, smallest / len(cuts), largest / len(cuts))
        return jnp.repeat(jnp.exp(heights), dims[position] // blocks).reshape((-1,) + (1,) * (len(dims) - position - 1))

    level = one(*cuts[0])
    for cut in cuts[1:]:
        level = level * one(*cut)
    return level


def length_profile(amount, total, reach, slope):
    loads = [(1 << 20) // math.isqrt(rank ** slope) + 1 for rank in range(2, amount + 1)]
    rest, holding = total - reach - (amount - 1), [1] * (amount - 1)
    while rest > 0:
        candidates = [i for i in range(amount - 1) if holding[i] < reach]
        mass, budget = sum([loads[i] for i in candidates]), rest
        for i in candidates:
            extra = min(reach - holding[i], max(1, budget * loads[i] // mass), rest)
            holding[i] = holding[i] + extra
            rest = rest - extra
    return np.array([reach] + holding)


def ragged(rng, number_of, total, most, slope):
    if number_of == 2:
        one = jax.random.randint(rng, (), max(1, total - most), min(most, total - 1) + 1)
        return jnp.stack([one, total - one])
    sizes = jnp.asarray(length_profile(number_of, total, most, slope), jnp.int32)
    pairs = (number_of - 1) // 2
    donor, taker = sizes[1:1 + 2 * pairs:2], sizes[2:2 + 2 * pairs:2]
    slack = jnp.minimum(donor - 1, most - taker)
    passed = jax.random.randint(jax.random.fold_in(rng, 1), (pairs,), 0, 1 << 20) % (slack + 1)
    sizes = sizes.at[1:1 + 2 * pairs:2].set(donor - passed).at[2:2 + 2 * pairs:2].set(taker + passed)
    return sizes[jax.random.permutation(jax.random.fold_in(rng, 2), number_of)]


def noise(rng, extent, scale, limit, pieces=(), kind=jnp.bfloat16):
    values = jax.random.normal(rng, extent, jnp.float32) * scale
    if len(pieces) > 0:
        values = block_scale(rng, extent, pieces, -0.22, 0.18) * values
    return jnp.clip(values, min=-limit, max=limit).astype(kind)


def setup_inputs(seed: int = 0) -> dict:
    seeds = jax.random.split(jax.random.key(seed), 18)
    return {
        "hidden": noise(seeds[0], (ROWS, LEN, D), 1.0, 6.0, ((0, 32),)),
        "lengths": ragged(seeds[1], ROWS, ROWS * LEN * 11 // 32, LEN, 2).astype(jnp.int32),
        "cotangent": noise(seeds[2], (ROWS, LQ, D), 1.0, 6.0, ((0, 32),)),
        "inflow": noise(seeds[3], (3, D, D), D ** -0.5, 0.21875, ((1, 32),)),
        "outflow": noise(seeds[4], (D, D), (D // 64) ** -0.5, 1.75, ((0, 32),)),
        "widener": noise(seeds[5], (D, FF), D ** -0.5, 0.21875, ((0, 32),)),
        "narrower": noise(seeds[6], (FF, D), FF ** -0.5, 0.109375, ((0, 32),)),
        "shifts": draw_shifts(jax.random.fold_in(seeds[17], 71), 0),
        "offsets": noise(seeds[8], (FF,), 0.5, 3.0, ((0, 32),)),
        "distance": noise(seeds[9], (H * NB,), 1.0, 4.0, ((0, 32),)),
        "intake": noise(seeds[10], (3, D, D), D ** -0.5, 0.21875, ((1, 32),)),
        "outtake": noise(seeds[11], (D, D), (D // 64) ** -0.5, 1.75, ((0, 32),)),
        "expander": noise(seeds[12], (D, FF), D ** -0.5, 0.21875, ((0, 32),)),
        "squeezer": noise(seeds[13], (FF, D), FF ** -0.5, 0.109375, ((0, 32),)),
        "adjusts": draw_adjusts(jax.random.fold_in(seeds[17], 71), 0),
        "leanings": noise(seeds[15], (FF,), 0.5, 3.0, ((0, 32),)),
        "spacing": noise(seeds[16], (H * NB,), 1.0, 4.0, ((0, 32),)),
    }


EPS = 1e-06
HIGH = lax.Precision.HIGHEST

@jax.custom_vjp
def low(v):
    return lax.optimization_barrier(v.astype(jnp.bfloat16)).astype(jnp.float32)

@jax.custom_vjp
def low_back(v):
    return v

def low_keep(v):
    return (low(v), None)

def low_pass(kept, grad):
    return (grad,)

def back_keep(v):
    return (v, None)

def back_low(kept, grad):
    return (low(grad),)
low.defvjp(low_keep, low_pass)
low_back.defvjp(back_keep, back_low)

def layer_norm(u, gain, shift):
    mean = lax.optimization_barrier(jnp.mean(u, axis=-1, keepdims=True))
    centred = u - mean
    spread = lax.optimization_barrier(jnp.mean(centred * centred, axis=-1, keepdims=True))
    return centred * lax.rsqrt(spread + EPS) * gain + shift

def dense(left, weight):
    return jnp.einsum('rtd,de->rte', left, weight, precision=HIGH)

def bucket_onehot(queries, keys, stride):
    place = jnp.arange(keys, dtype=jnp.int32)[None, :] - stride * jnp.arange(queries, dtype=jnp.int32)[:, None]
    bucket = jnp.clip(place, -(NB // 2), NB // 2 - 1) + NB // 2
    return (bucket[:, :, None] == jnp.arange(NB, dtype=jnp.int32)[None, None, :]).astype(jnp.float32)

def attend_row(query, key, value, key_len, bias):
    queries = query.shape[0]
    keys = key.shape[0]
    qh = query.reshape(queries, H, HD)
    kh = key.reshape(keys, H, HD)
    vh = value.reshape(keys, H, HD)
    scores = jnp.einsum('qhd,khd->hqk', qh, kh, precision=HIGH) * HD ** (-0.5) + bias
    scores = low_back(scores)
    valid = jnp.arange(keys, dtype=jnp.int32)[None, None, :] < key_len
    scores = jnp.where(valid, scores, -1e+30)
    total = jax.nn.logsumexp(scores, axis=-1, keepdims=True)
    probs = low(jnp.exp(scores - total))
    context = jnp.einsum('hqk,khd->qhd', probs, vh, precision=HIGH)
    return context.reshape(queries, H * HD)

def layer(query_in, key_in, resid, key_len, weights, stride):
    entry, leave, widen, narrow, vectors, wide_bias, table = weights
    queries = query_in.shape[1]
    keys = key_in.shape[1]
    onehot = bucket_onehot(queries, keys, stride)
    bias = jnp.einsum('hb,qkb->hqk', table.reshape(H, NB), onehot, precision=HIGH)
    query = low(low_back(dense(query_in, entry[0]) + vectors[0]))
    key = low(low_back(dense(key_in, entry[1])))
    value = low(low_back(dense(key_in, entry[2]) + vectors[1]))
    attend = jax.checkpoint(partial(attend_row, bias=bias))
    context = lax.map(lambda item: attend(item[0], item[1], item[2], item[3]), (query, key, value, key_len))
    context = low(low_back(context))
    attended = low_back(dense(context, leave) + vectors[2])
    mixed = layer_norm(resid + attended, vectors[3], vectors[4])
    hidden_units = low_back(dense(low(mixed), widen) + wide_bias)
    activation = low(jax.nn.gelu(hidden_units, approximate=True))
    back = low_back(dense(activation, narrow) + vectors[5])
    return layer_norm(mixed + back, vectors[6], vectors[7])

def forward(inputs, lengths, first, second):
    pooled = 0.5 * (inputs[:, 0::2] + inputs[:, 1::2])
    pooled_out = low(layer(low(pooled), inputs, pooled, lengths, first, 2))
    full_out = layer(pooled_out, pooled_out, pooled_out, (lengths + 1) // 2, second, 1)
    return (pooled_out, full_out)

def reference(hidden, lengths, cotangent, inflow, outflow, widener, narrower, shifts, offsets, distance, intake, outtake, expander, squeezer, adjusts, leanings, spacing):
    first = tuple((a.astype(jnp.float32) for a in (inflow, outflow, widener, narrower, shifts, offsets, distance)))
    second = tuple((a.astype(jnp.float32) for a in (intake, outtake, expander, squeezer, adjusts, leanings, spacing)))
    group = math.gcd(ROWS, max(1, 4096 // LEN))
    count = ROWS // group
    inputs = hidden.astype(jnp.float32).reshape(count, group, LEN, D)
    counts = lengths.reshape(count, group)
    cots = cotangent.astype(jnp.float32).reshape(count, group, LQ, D)

    def visit(carry, item):
        block, block_len, block_cot = item

        def run(x, one, two):
            return forward(x, block_len, one, two)
        (pooled_out, full_out), pull = jax.vjp(run, block, first, second)
        block_grad, grad_one, grad_two = pull((jnp.zeros_like(pooled_out), block_cot))
        carry = jax.tree.map(jnp.add, carry, (grad_one, grad_two))
        return (carry, (pooled_out, full_out, block_grad))
    zeros = jax.tree.map(jnp.zeros_like, (first, second))
    totals, (pooled_all, full_all, grad_all) = lax.scan(visit, zeros, (inputs, counts, cots))
    grad_one, grad_two = totals
    return (pooled_all.reshape(ROWS, LQ, D).astype(jnp.bfloat16), full_all.reshape(ROWS, LQ, D).astype(jnp.bfloat16), grad_all.reshape(ROWS, LEN, D), grad_one[0], grad_one[1], grad_one[2], grad_one[3], grad_one[4], grad_one[5], grad_one[6], grad_two[0], grad_two[1], grad_two[2], grad_two[3], grad_two[4][1:], grad_two[5], grad_two[6], grad_two[4][0])
```

```python
from functools import partial

import jax
import jax.numpy as jnp
from jax import lax
from jax.experimental import pallas as pl
from jax.experimental.pallas import tpu as pltpu
from jax.sharding import PartitionSpec as P

H = 12
HD = 64
NB = 32
D = 768
FF = 3072
HALF = 384
EPS = 1e-06
AX = ("wide", "narrow")
CORE, XBIT, YBIT, Z0, Z1 = 1, 2, 4, 8, 16
UNITS = 16
F32 = jnp.float32
BF16 = jnp.bfloat16
GELU_A = 0.7978845608028654
GELU_B = 0.044715
NN = (((1,), (0,)), ((), ()))
NT = (((1,), (1,)), ((), ()))
TN = (((0,), (0,)), ((), ()))
VMEM_LIMIT = 60 * 1024 * 1024
ANY = pl.BlockSpec(memory_space=pl.ANY)


def mm(left, right, dims=NN):
    return lax.dot_general(left, right, dims, preferred_element_type=F32)


def wide(value):
    return value.astype(F32)


def low(value):
    return value.astype(BF16)


def swap(value, mask):
    return lax.ppermute(value, AX, [(i, i ^ mask) for i in range(32)])


def pick(core, first, second):
    return jnp.where(core == 0, first, second)


def pair_units(core, value, group):
    rows, _, width = value.shape
    keep = pick(core, value[:, 0], value[:, 1]).reshape(-1, group, width)
    send = pick(core, value[:, 1], value[:, 0]).reshape(-1, group, width)
    return keep, send


def join_units(core, keep, recv):
    return jnp.concatenate([pick(core, keep, recv), pick(core, recv, keep)], axis=1)


def gather_slab(slab):
    own = jnp.stack([slab, swap(slab, Z0), swap(slab, Z1), swap(slab, Z0 | Z1)])
    across_y = swap(own, YBIT)
    across_x = swap(own, XBIT)
    diag_low = swap(across_y[:2], XBIT)
    diag_high = swap(across_x[2:], YBIT)
    mine = (own, across_y, across_x, diag_low, diag_high)
    return mine + tuple(swap(piece, CORE) for piece in mine)


def flip_bit(bit, value, axis):
    return jnp.where(bit == 0, value, jnp.flip(value, axis))


def gather_vectors(index, flat):
    pieces = gather_slab(flat)
    sides = []
    for side in range(2):
        own, across_y, across_x, diag_low, diag_high = pieces[5 * side : 5 * side + 5]
        diag = jnp.concatenate([diag_low, diag_high], axis=0)
        sides.append(jnp.stack([own, across_x, across_y, diag], axis=1))
    full = jnp.stack(sides, axis=2)
    full = full.reshape(2, 2, 2, 2, 2, -1)
    for axis, mask in enumerate((Z1, Z0, YBIT, XBIT, CORE)):
        full = flip_bit((index // mask) % 2, full, axis)
    return full.reshape(32, -1)


def gather_layers(index, layers):
    core = index % 2
    packed = []
    for entry, leave, widen, narrow in layers:
        eo = jnp.concatenate([entry, leave[None]]).reshape(96, 2, HALF)
        packed.append(pair_units(core, eo, 24))
        packed.append(pair_units(core, widen.reshape(24, 2, FF // 2), 24))
        packed.append(pair_units(core, narrow.reshape(96, 2, HALF), 96))
    result = []
    for keep, send in packed:
        slab = join_units(core, keep, swap(send, CORE))
        slab = slab if slab.shape[0] == 4 else slab[0]
        result.append(gather_slab(slab))
    return result[:3], result[3:]


def reduce_units(send, keep):
    shape = (4, 4) + keep.shape[1:]
    keep = keep.reshape(shape)
    recv = swap(send, CORE).reshape(shape)
    diag = low(wide(keep[3]) + wide(recv[3]))
    diag_low = wide(swap(diag[:2], XBIT))
    diag_high = wide(swap(diag[2:], YBIT))
    to_y = wide(keep[2]) + wide(recv[2])
    to_x = wide(keep[1]) + wide(recv[1])
    to_y = jnp.concatenate([low(to_y[:2] + diag_low), low(to_y[2:])])
    to_x = jnp.concatenate([low(to_x[:2]), low(to_x[2:] + diag_high)])
    total = wide(keep[0]) + wide(recv[0])
    total = total + wide(swap(to_y, YBIT)) + wide(swap(to_x, XBIT))
    sent = low(total[1:])
    return (
        total[0] + wide(swap(sent[0], Z0)) + wide(swap(sent[1], Z1)) + wide(swap(sent[2], Z0 | Z1))
    )


def unpair(core, slab, group):
    keep = pick(core, slab[:, :group], slab[:, group:])
    recv = swap(pick(core, slab[:, group:], slab[:, :group]), CORE)
    return jnp.concatenate([pick(core, keep, recv), pick(core, recv, keep)], axis=-1)


def vector_units(vectors, wide_bias, table, parts):
    flat = jnp.concatenate(
        [
            vectors.reshape(8, parts, -1).transpose(1, 0, 2).reshape(parts, -1),
            wide_bias.reshape(parts, -1),
            table.reshape(parts, -1),
        ],
        axis=1,
    )
    return flat


def split_vectors(flat, parts):
    cut = 8 * D // parts
    mid = cut + FF // parts
    return flat[:cut].reshape(8, -1), flat[cut:mid], flat[mid : mid + H * NB // parts]


def position(chip, unit):
    rel = jnp.bitwise_xor(chip, unit)
    return jnp.bitwise_and(rel, 3) * 4 + lax.shift_right_logical(rel, 2)


def start_load(me, refs, dst, sem, place):
    if len(refs) == 1:
        pltpu.make_async_copy(refs[0], dst, sem).start()
        return
    chip = lax.shift_right_logical(me, 1)
    for side in range(2):
        half = jnp.bitwise_xor(jnp.bitwise_and(me, 1), side)
        own, across_y, across_x, diag_low, diag_high = refs[5 * side : 5 * side + 5]
        for k in range(4):
            for step, ref, at in (
                (0, own, k),
                (1, across_x, k),
                (2, across_y, k),
                (3, diag_low if k < 2 else diag_high, k % 2),
            ):
                unit = jnp.bitwise_xor(chip, 4 * k + step)
                source, target = place(ref.at[at], dst, unit, half)
                pltpu.make_async_copy(source, target, sem).start()


def wait_load(dst, sem):
    pltpu.make_async_copy(dst, dst, sem).wait()


def place_entry(src, dst, unit, half):
    rows, cols = pl.multiple_of(unit * 48, 16), pl.multiple_of(half * HALF, 128)
    return src.at[0:3], dst.at[:, pl.ds(rows, 48), pl.ds(cols, HALF)]


def place_leave(src, dst, unit, half):
    rows, cols = pl.multiple_of(unit * 48, 16), pl.multiple_of(half * HALF, 128)
    return src.at[3], dst.at[pl.ds(rows, 48), pl.ds(cols, HALF)]


def place_widen(src, dst, unit, half):
    rows, cols = pl.multiple_of(unit * 48, 16), pl.multiple_of(half * FF // 2, 128)
    return src, dst.at[pl.ds(rows, 48), pl.ds(cols, FF // 2)]


def place_narrow(src, dst, unit, half):
    rows, cols = pl.multiple_of(unit * 192, 16), pl.multiple_of(half * HALF, 128)
    return src, dst.at[pl.ds(rows, 192), pl.ds(cols, HALF)]


def build_bias(tab_ref, bias, stride):
    keys = bias.shape[1]
    for part in range(bias.shape[2] // 128):
        row = lax.broadcasted_iota(jnp.int32, (keys, 128), 0)
        col = lax.broadcasted_iota(jnp.int32, (keys, 128), 1) + 128 * part
        bucket = jnp.clip(row - stride * col, -(NB // 2), NB // 2 - 1) + NB // 2
        for h in range(H):
            table = jnp.broadcast_to(tab_ref[h : h + 1, :], (keys, 128))
            bias[h, :, 128 * part : 128 * part + 128] = jnp.take_along_axis(
                table, bucket, axis=1, mode="promise_in_bounds"
            )


def lane_masks(value):
    lane = lax.broadcasted_iota(jnp.int32, value.shape, 1)
    zero = jnp.zeros_like(value)
    return jnp.where(lane < HD, value, zero), jnp.where(lane < HD, zero, value)


def masked_scores(keys, query, bias, count):
    scores = mm(keys, query, NT) + bias
    size = scores.shape[0]
    head, tail = scores[: size - 128], scores[size - 128 :]
    row = lax.broadcasted_iota(jnp.int32, tail.shape, 0) + (size - 128)
    tail = jnp.where(row < count, tail, -1e30)
    return tail if size == 128 else jnp.concatenate([head, tail], axis=0)


def statistics(value):
    mean = jnp.mean(value, axis=-1, keepdims=True)
    centred = value - mean
    spread = jnp.mean(centred * centred, axis=-1, keepdims=True)
    rstd = lax.rsqrt(spread + EPS)
    return centred * rstd, rstd


def norm_pull(grad, unit, rstd):
    return rstd * (
        grad
        - jnp.mean(grad, axis=-1, keepdims=True)
        - unit * jnp.mean(grad * unit, axis=-1, keepdims=True)
    )


def column_sum(value):
    return jnp.sum(value, axis=0, keepdims=True)


def attend_kernel(stride, count, len_ref, me_ref, x_ref, vec_ref, tab_ref, *refs):
    sources = refs[:count]
    refs = refs[count:]
    if stride == 2:
        pooled_ref, pooled_low_ref, *refs = refs
    q_ref, k_ref, v_ref, ctx_ref, lse_ref, entry, bias, turned, sem = refs
    row = pl.program_id(0)
    keys = x_ref.shape[1]
    queries = q_ref.shape[1]

    @pl.when(row == 0)
    def _():
        start_load(me_ref[0], sources, entry, sem.at[0], place_entry)
        build_bias(tab_ref, bias, stride)
        wait_load(entry, sem.at[0])

    length = len_ref[row]
    if stride == 2:
        place = lax.broadcasted_iota(jnp.int32, (queries, keys), 1)
        mine = lax.broadcasted_iota(jnp.int32, (queries, keys), 0)
        pair = jnp.where(lax.shift_right_logical(place, 1) == mine, 0.5, 0.0).astype(BF16)
        pooled = mm(pair, x_ref[0])
        pooled_ref[0] = pooled
        query_in = low(pooled)
        pooled_low_ref[0] = query_in
    else:
        query_in = x_ref[0]
    q_ref[0] = low(wide(low(mm(query_in, entry[0]) + vec_ref[0:1, :])) * HD**-0.5)
    for block in range(keys // 256):

        @pl.when(block * 256 < length)
        def _():
            rows = pl.ds(block * 256, 256)
            x = x_ref[0, rows, :]
            k_ref[0, rows, :] = low(mm(x, entry[1]))
            v_ref[0, rows, :] = low(mm(x, entry[2]) + vec_ref[1:2, :])

    def pair_step(size, step, carry):
        lanes = pl.ds(pl.multiple_of(step * 128, 128), 128)
        queries_low = lane_masks(q_ref[0, :, lanes])
        key = k_ref[0, :size, lanes]
        value = v_ref[0, :size, lanes].T
        for i in range(2):
            h = 2 * step + i
            scores = masked_scores(key, queries_low[i], bias[h, :size, :], length)
            top = jnp.max(scores, axis=0, keepdims=True)
            probs = jnp.exp(scores - top)
            total = jnp.sum(probs, axis=0, keepdims=True)
            lse_ref[0, h] = jnp.broadcast_to(top + jnp.log(total), lse_ref.shape[2:])
            context = mm(value[HD * i : HD * i + HD], low(probs)) / total
            turned[pl.ds(pl.multiple_of(step * 128 + HD * i, HD), HD), :] = context
        return carry

    blocks = lax.div(length + 127, 128)
    for w in range(1, keys // 128 + 1):

        @pl.when(blocks == w)
        def _():
            lax.fori_loop(0, H // 2, partial(pair_step, 128 * w), 0)

    ctx_ref[0] = low(turned[...].T)


def attend(stride, index, lengths, x, vectors, table, sources):
    rows, keys, _ = x.shape
    queries = keys // stride
    blk = lambda *shape: pl.BlockSpec((1,) + shape, lambda r, *_: (r,) + (0,) * len(shape))
    full = lambda *shape: pl.BlockSpec(shape, lambda r, *_: (0,) * len(shape))
    sds = jax.ShapeDtypeStruct
    outs = [
        (sds((rows, queries, D), BF16), blk(queries, D)),
        (sds((rows, keys, D), BF16), blk(keys, D)),
        (sds((rows, keys, D), BF16), blk(keys, D)),
        (sds((rows, queries, D), BF16), blk(queries, D)),
        (sds((rows, H, 8, queries), F32), blk(H, 8, queries)),
    ]
    if stride == 2:
        outs = [
            (sds((rows, queries, D), F32), blk(queries, D)),
            (sds((rows, queries, D), BF16), blk(queries, D)),
        ] + outs
    return pl.pallas_call(
        partial(attend_kernel, stride, len(sources)),
        grid_spec=pltpu.PrefetchScalarGridSpec(
            num_scalar_prefetch=2,
            grid=(rows,),
            in_specs=[blk(keys, D), full(8, D), full(16, 128)] + [ANY] * len(sources),
            out_specs=[o[1] for o in outs],
            scratch_shapes=[
                pltpu.VMEM((3, D, D), BF16),
                pltpu.VMEM((H, keys, queries), F32),
                pltpu.VMEM((D, queries), F32),
                pltpu.SemaphoreType.DMA((1,)),
            ],
        ),
        out_shape=[o[0] for o in outs],
        compiler_params=pltpu.CompilerParams(vmem_limit_bytes=VMEM_LIMIT),
        cost_estimate=pl.CostEstimate(
            flops=rows * keys * D * D * 8, bytes_accessed=20_000_000, transcendentals=rows * H * keys * queries
        ),
        name="attend",
    )(lengths, index, x, vectors, table, *sources)


def expand_kernel(counts, me_ref, ctx_ref, resid_ref, vec_ref, bias_ref, *refs):
    c1, c2, c3 = counts
    leave_src, widen_src, narrow_src = refs[:c1], refs[c1 : c1 + c2], refs[c1 + c2 : c1 + c2 + c3]
    u_ref, h_ref, before_ref, out_ref, leave, widen, narrow, sem = refs[c1 + c2 + c3 :]
    first = pl.program_id(0) == 0

    @pl.when(first)
    def _():
        start_load(me_ref[0], leave_src, leave, sem.at[0], place_leave)
        start_load(me_ref[0], widen_src, widen, sem.at[1], place_widen)
        start_load(me_ref[0], narrow_src, narrow, sem.at[2], place_narrow)
        wait_load(leave, sem.at[0])

    u = wide(resid_ref[...]) + mm(ctx_ref[...], leave[...]) + vec_ref[2:3, :]
    u_ref[...] = u
    unit, _ = statistics(u)
    mixed = unit * vec_ref[3:4, :] + vec_ref[4:5, :]
    mixed_low = low(mixed)

    @pl.when(first)
    def _():
        wait_load(widen, sem.at[1])
        wait_load(narrow, sem.at[2])

    total = mixed + vec_ref[5:6, :]
    for j in range(6):
        cols = slice(512 * j, 512 * j + 512)
        h = mm(mixed_low, widen[:, cols]) + bias_ref[0:1, cols]
        h_ref[:, cols] = low(h)
        act = 0.5 * h * (1.0 + jnp.tanh(GELU_A * (h + GELU_B * h * h * h)))
        total = total + mm(low(act), narrow[cols, :])
    before_ref[...] = total
    unit, _ = statistics(total)
    out_ref[...] = low(unit * vec_ref[6:7, :] + vec_ref[7:8, :])


def expand(index, ctx, resid, vectors, wide_bias, leave, widen, narrow):
    tokens = ctx.shape[0]
    tile = 512 if tokens % 512 == 0 else 256
    blk = lambda width: pl.BlockSpec((tile, width), lambda r, *_: (r, 0))
    full = lambda *shape: pl.BlockSpec(shape, lambda r, *_: (0,) * len(shape))
    sds = jax.ShapeDtypeStruct
    sources = tuple(leave) + tuple(widen) + tuple(narrow)
    return pl.pallas_call(
        partial(expand_kernel, (len(leave), len(widen), len(narrow))),
        grid_spec=pltpu.PrefetchScalarGridSpec(
            num_scalar_prefetch=1,
            grid=(tokens // tile,),
            in_specs=[blk(D), blk(D), full(8, D), full(1, FF)] + [ANY] * len(sources),
            out_specs=[blk(D), blk(FF), blk(D), blk(D)],
            scratch_shapes=[
                pltpu.VMEM((D, D), BF16),
                pltpu.VMEM((D, FF), BF16),
                pltpu.VMEM((FF, D), BF16),
                pltpu.SemaphoreType.DMA((3,)),
            ],
        ),
        out_shape=[
            sds((tokens, D), F32),
            sds((tokens, FF), BF16),
            sds((tokens, D), F32),
            sds((tokens, D), BF16),
        ],
        compiler_params=pltpu.CompilerParams(vmem_limit_bytes=VMEM_LIMIT),
        cost_estimate=pl.CostEstimate(
            flops=2 * tokens * D * (D + 2 * FF), bytes_accessed=30_000_000, transcendentals=tokens * FF
        ),
        name="expand",
    )(index, ctx, resid, vectors, wide_bias, *sources)


def contract_kernel(counts, me_ref, dz_ref, before_ref, h_ref, u_ref, vec_ref, *refs):
    c1, c2, c3 = counts
    leave_src, widen_src, narrow_src = refs[:c1], refs[c1 : c1 + c2], refs[c1 + c2 : c1 + c2 + c3]
    refs = refs[c1 + c2 + c3 :]
    dback_ref, mixed_ref, act_ref, dhid_ref, dattn_ref, du_ref, dctx_ref, dvec_ref, dbias_ref = refs[:9]
    leave, widen, narrow, sem = refs[9:]
    first = pl.program_id(0) == 0

    @pl.when(first)
    def _():
        start_load(me_ref[0], narrow_src, narrow, sem.at[2], place_narrow)
        start_load(me_ref[0], widen_src, widen, sem.at[1], place_widen)
        start_load(me_ref[0], leave_src, leave, sem.at[0], place_leave)
        dvec_ref[...] = jnp.zeros_like(dvec_ref)
        dbias_ref[...] = jnp.zeros_like(dbias_ref)

    dz = wide(dz_ref[...])
    unit, rstd = statistics(before_ref[...])
    dvec_ref[6:7, :] += column_sum(dz * unit)
    dvec_ref[7:8, :] += column_sum(dz)
    dpre = norm_pull(dz * vec_ref[6:7, :], unit, rstd)
    dback = low(dpre)
    dback_ref[...] = dback
    dvec_ref[5:6, :] += column_sum(wide(dback))
    unit, rstd = statistics(u_ref[...])
    mixed_ref[...] = low(unit * vec_ref[3:4, :] + vec_ref[4:5, :])

    @pl.when(first)
    def _():
        wait_load(narrow, sem.at[2])
        wait_load(widen, sem.at[1])
        wait_load(leave, sem.at[0])

    dmixed = dpre
    for j in range(6):
        cols = slice(512 * j, 512 * j + 512)
        dact = mm(dback, narrow[cols, :], NT)
        h = wide(h_ref[:, cols])
        square = h * h
        tanh = jnp.tanh(GELU_A * h * (1.0 + GELU_B * square))
        gate = 0.5 + 0.5 * tanh
        act_ref[:, cols] = low(h * gate)
        slope = gate + 0.5 * h * (1.0 - tanh * tanh) * (GELU_A + (3.0 * GELU_A * GELU_B) * square)
        dhid = low(dact * slope)
        dhid_ref[:, cols] = dhid
        dbias_ref[:, cols] += column_sum(wide(dhid))
        dmixed = dmixed + mm(dhid, widen[:, cols], NT)
    dvec_ref[3:4, :] += column_sum(dmixed * unit)
    dvec_ref[4:5, :] += column_sum(dmixed)
    du = norm_pull(dmixed * vec_ref[3:4, :], unit, rstd)
    du_ref[...] = du
    dattn = low(du)
    dattn_ref[...] = dattn
    dvec_ref[2:3, :] += column_sum(wide(dattn))
    dctx_ref[...] = low(mm(dattn, leave[...], NT))


def contract(index, dz, before, hidden_units, u, vectors, leave, widen, narrow):
    tokens = dz.shape[0]
    tile = 256
    blk = lambda width: pl.BlockSpec((tile, width), lambda r, *_: (r, 0))
    full = lambda *shape: pl.BlockSpec(shape, lambda r, *_: (0,) * len(shape))
    sds = jax.ShapeDtypeStruct
    sources = tuple(leave) + tuple(widen) + tuple(narrow)
    return pl.pallas_call(
        partial(contract_kernel, (len(leave), len(widen), len(narrow))),
        grid_spec=pltpu.PrefetchScalarGridSpec(
            num_scalar_prefetch=1,
            grid=(tokens // tile,),
            in_specs=[blk(D), blk(D), blk(FF), blk(D), full(8, D)] + [ANY] * len(sources),
            out_specs=[blk(D), blk(D), blk(FF), blk(FF), blk(D), blk(D), blk(D), full(8, D), full(1, FF)],
            scratch_shapes=[
                pltpu.VMEM((D, D), BF16),
                pltpu.VMEM((D, FF), BF16),
                pltpu.VMEM((FF, D), BF16),
                pltpu.SemaphoreType.DMA((3,)),
            ],
        ),
        out_shape=[
            sds((tokens, D), BF16),
            sds((tokens, D), BF16),
            sds((tokens, FF), BF16),
            sds((tokens, FF), BF16),
            sds((tokens, D), BF16),
            sds((tokens, D), F32),
            sds((tokens, D), BF16),
            sds((8, D), F32),
            sds((1, FF), F32),
        ],
        compiler_params=pltpu.CompilerParams(vmem_limit_bytes=VMEM_LIMIT),
        cost_estimate=pl.CostEstimate(
            flops=2 * tokens * D * (D + 2 * FF), bytes_accessed=50_000_000, transcendentals=tokens * FF
        ),
        name="contract",
    )(index, dz, before, hidden_units, u, vectors, *sources)


def halves(core, value, width):
    left, right = value[:, :width], value[:, width:]
    first = core == 0
    return jnp.where(first, right, left), jnp.where(first, left, right)


def narrow_grad_kernel(me_ref, act_ref, dback_ref, ctx_ref, dattn_ref, send_ref, keep_ref):
    step = pl.program_id(0)
    core = jnp.bitwise_and(me_ref[0], 1)
    chip = lax.shift_right_logical(me_ref[0], 1)

    @pl.when(step < 4)
    def _():
        send, keep = halves(core, mm(act_ref[...], dback_ref[...], TN), HALF)
        for i in range(4):
            at = position(chip, step * 4 + i)
            send_ref[at, 0:192, :] = low(send[192 * i : 192 * i + 192])
            keep_ref[at, 0:192, :] = low(keep[192 * i : 192 * i + 192])

    @pl.when(step == 4)
    def _():
        send, keep = halves(core, mm(ctx_ref[...], dattn_ref[...], TN), HALF)
        for i in range(UNITS):
            at = position(chip, i)
            send_ref[at, 192:240, :] = low(send[48 * i : 48 * i + 48])
            keep_ref[at, 192:240, :] = low(keep[48 * i : 48 * i + 48])


def narrow_grad(index, act, dback, ctx, dattn):
    tokens = act.shape[0]
    full = lambda *shape: pl.BlockSpec(shape, lambda r, *_: (0,) * len(shape))
    out = jax.ShapeDtypeStruct((UNITS, 240, HALF), BF16)
    return pl.pallas_call(
        narrow_grad_kernel,
        grid_spec=pltpu.PrefetchScalarGridSpec(
            num_scalar_prefetch=1,
            grid=(5,),
            in_specs=[
                pl.BlockSpec((tokens, D), lambda r, *_: (0, jnp.minimum(r, 3))),
                full(tokens, D),
                full(tokens, D),
                full(tokens, D),
            ],
            out_specs=[full(UNITS, 240, HALF)] * 2,
        ),
        out_shape=[out, out],
        compiler_params=pltpu.CompilerParams(vmem_limit_bytes=VMEM_LIMIT),
        cost_estimate=pl.CostEstimate(
            flops=2 * tokens * D * (D + FF), bytes_accessed=16_000_000, transcendentals=0
        ),
        name="narrow_grad",
    )(index, act, dback, ctx, dattn)


def widen_grad_kernel(me_ref, mixed_ref, dhid_ref, send_ref, keep_ref, turned):
    step = pl.program_id(0)
    core = jnp.bitwise_and(me_ref[0], 1)
    chip = lax.shift_right_logical(me_ref[0], 1)

    @pl.when(step == 0)
    def _():
        turned[...] = mixed_ref[...].T

    grad = low(mm(turned[...], dhid_ref[...]))
    mine = lax.div(step, 2) == core
    for part in range(2):

        @pl.when(lax.rem(step, 2) == part)
        def _():
            for wanted, out_ref in ((True, keep_ref), (False, send_ref)):

                @pl.when(mine == wanted)
                def _():
                    for i in range(UNITS):
                        at = position(chip, i)
                        out_ref[at, :, D * part : D * part + D] = grad[48 * i : 48 * i + 48]


def widen_grad(index, mixed_low, dhid):
    tokens = mixed_low.shape[0]
    full = lambda *shape: pl.BlockSpec(shape, lambda r, *_: (0,) * len(shape))
    out = jax.ShapeDtypeStruct((UNITS, 48, FF // 2), BF16)
    return pl.pallas_call(
        widen_grad_kernel,
        grid_spec=pltpu.PrefetchScalarGridSpec(
            num_scalar_prefetch=1,
            grid=(4,),
            in_specs=[full(tokens, D), pl.BlockSpec((tokens, D), lambda r, *_: (0, r))],
            out_specs=[full(UNITS, 48, FF // 2)] * 2,
            scratch_shapes=[pltpu.VMEM((D, tokens), BF16)],
        ),
        out_shape=[out, out],
        compiler_params=pltpu.CompilerParams(vmem_limit_bytes=VMEM_LIMIT),
        cost_estimate=pl.CostEstimate(
            flops=2 * tokens * D * FF, bytes_accessed=13_000_000, transcendentals=0
        ),
        name="widen_grad",
    )(index, mixed_low, dhid)


def entry_grad_kernel(len_ref, me_ref, a_ref, b_ref, dq_ref, dk_ref, dv_ref, vec_ref, send_ref, keep_ref, total):
    row = pl.program_id(0)
    core = jnp.bitwise_and(me_ref[0], 1)
    chip = lax.shift_right_logical(me_ref[0], 1)
    keys = b_ref.shape[1]

    @pl.when(row == 0)
    def _():
        total[...] = jnp.zeros_like(total)

    total[0] += mm(a_ref[0], dq_ref[0], TN)
    for block in range(keys // 256):

        @pl.when(block * 256 < len_ref[row])
        def _():
            rows = pl.ds(block * 256, 256)
            b = b_ref[0, rows, :].T
            total[1] += mm(b, dk_ref[0, rows, :])
            total[2] += mm(b, dv_ref[0, rows, :])

    @pl.when(row == pl.num_programs(0) - 1)
    def _():
        for m in range(3):
            send, keep = halves(core, total[m], HALF)
            for i in range(UNITS):
                at = position(chip, i)
                send_ref[at, 48 * m : 48 * m + 48, :] = low(send[48 * i : 48 * i + 48])
                keep_ref[at, 48 * m : 48 * m + 48, :] = low(keep[48 * i : 48 * i + 48])
        for i in range(UNITS):
            at = position(chip, i)
            send_ref[at, 144:160, :] = vec_ref[i, 1 - core]
            keep_ref[at, 144:160, :] = vec_ref[i, core]


def entry_grad(index, lengths, a, b, dq, dk, dv, vec):
    rows, keys, _ = b.shape
    queries = a.shape[1]
    blk = lambda *shape: pl.BlockSpec((1,) + shape, lambda r, *_: (r,) + (0,) * len(shape))
    full = lambda *shape: pl.BlockSpec(shape, lambda r, *_: (0,) * len(shape))
    out = jax.ShapeDtypeStruct((UNITS, 160, HALF), BF16)
    return pl.pallas_call(
        entry_grad_kernel,
        grid_spec=pltpu.PrefetchScalarGridSpec(
            num_scalar_prefetch=2,
            grid=(rows,),
            in_specs=[
                blk(queries, D),
                blk(keys, D),
                blk(queries, D),
                blk(keys, D),
                blk(keys, D),
                full(UNITS, 2, 16, HALF),
            ],
            out_specs=[full(UNITS, 160, HALF)] * 2,
            scratch_shapes=[pltpu.VMEM((3, D, D), F32)],
        ),
        out_shape=[out, out],
        compiler_params=pltpu.CompilerParams(vmem_limit_bytes=VMEM_LIMIT),
        cost_estimate=pl.CostEstimate(
            flops=2 * rows * (queries + keys) * D * D, bytes_accessed=20_000_000, transcendentals=0
        ),
        name="entry_grad",
    )(lengths, index, a, b, dq, dk, dv, vec)


def retrace_kernel(stride, len_ref, q_ref, k_ref, v_ref, dctx_ref, lse_ref, tab_ref, *refs):
    dq_ref, dk_ref, dv_ref, dvec_ref, diag_ref, ends_ref, bias, bias_sum, turned = refs
    row = pl.program_id(0)
    keys = k_ref.shape[1]
    queries = q_ref.shape[1]
    length = len_ref[row]

    @pl.when(row == 0)
    def _():
        build_bias(tab_ref, bias, stride)
        bias_sum[...] = jnp.zeros_like(bias_sum)
        dvec_ref[...] = jnp.zeros_like(dvec_ref)

    def pair_step(size, step, carry):
        lanes = pl.ds(pl.multiple_of(step * 128, 128), 128)
        queries_low = lane_masks(q_ref[0, :, lanes])
        dctx = lane_masks(dctx_ref[0, :, lanes])
        key = k_ref[0, :size, lanes]
        value = v_ref[0, :size, lanes]
        key_turned = key.T
        kept_probs, kept_grads = [], []
        for i in range(2):
            h = 2 * step + i
            scores = masked_scores(key, queries_low[i], bias[h, :size, :], length)
            probs = jnp.exp(scores - lse_ref[0, h, 0:1, :])
            dprobs = mm(value, dctx[i], NT)
            inner = jnp.sum(probs * dprobs, axis=0, keepdims=True)
            grads = low(probs * (dprobs - inner))
            kept_probs.append(low(probs))
            kept_grads.append(grads)
            for lane in range(queries // 128):
                bias_sum[lane, h, :size, :] += wide(grads[:, 128 * lane : 128 * lane + 128])
            turned[pl.ds(pl.multiple_of(step * 128 + HD * i, HD), HD), :] = (
                mm(key_turned[HD * i : HD * i + HD], grads) * HD**-0.5
            )
        dv_ref[0, :size, lanes] = low(
            mm(jnp.concatenate(kept_probs, axis=1), jnp.concatenate(dctx, axis=0))
        )
        dk_ref[0, :size, lanes] = low(
            mm(jnp.concatenate(kept_grads, axis=1), jnp.concatenate(queries_low, axis=0))
        )
        return carry

    blocks = lax.div(length + 127, 128)
    for w in range(1, keys // 128 + 1):

        @pl.when(blocks == w)
        def _():
            size = 128 * w
            lax.fori_loop(0, H // 2, partial(pair_step, size), 0)
            if size < keys:
                dk_ref[0, size:, :] = jnp.zeros((keys - size, D), BF16)
                dv_ref[0, size:, :] = jnp.zeros((keys - size, D), BF16)
            dvec_ref[1:2, :] += column_sum(wide(dv_ref[0, :size, :]))

    dquery = low(turned[...].T)
    dq_ref[0] = dquery
    dvec_ref[0:1, :] += column_sum(wide(dquery))

    @pl.when(row == pl.num_programs(0) - 1)
    def _():
        ends_ref[...] = jnp.zeros_like(ends_ref)

        def collect(h, carry):
            below = above = jnp.zeros((1, queries), F32)
            for part in range(stride):
                block = jnp.concatenate(
                    [
                        bias_sum[lane, h, pl.ds(part, queries, stride=stride), :]
                        for lane in range(queries // 128)
                    ],
                    axis=1,
                )
                col = lax.broadcasted_iota(jnp.int32, block.shape, 1)
                line = lax.broadcasted_iota(jnp.int32, block.shape, 0)
                place = stride * (line - col) + part
                zero = jnp.zeros_like(block)
                below = below + column_sum(jnp.where(place <= -(NB // 2), block, zero))
                above = above + column_sum(jnp.where(place >= NB // 2 - 1, block, zero))
                inside = jnp.where((place > -(NB // 2)) & (place < NB // 2 - 1), block, zero)
                partial_sum = inside[:8]
                for a in range(1, queries // 8):
                    partial_sum = partial_sum + pltpu.roll(inside[8 * a : 8 * a + 8], queries - 8 * a, 1)
                sub = lax.broadcasted_iota(jnp.int32, partial_sum.shape, 0)
                lined = jnp.where(sub == 0, partial_sum, 0.0)
                for b in range(1, 8):
                    lined = lined + jnp.where(sub == b, pltpu.roll(partial_sum, queries - b, 1), 0.0)
                diag_ref[h, part] = jnp.broadcast_to(column_sum(lined), (8, queries))
            ends_ref[h, 0] = jnp.broadcast_to(below, (8, queries))
            ends_ref[h, 1] = jnp.broadcast_to(above, (8, queries))
            return carry

        lax.fori_loop(0, H, collect, 0)


def retrace(stride, lengths, q, k, v, dctx, lse, table):
    rows, keys, _ = k.shape
    queries = q.shape[1]
    blk = lambda *shape: pl.BlockSpec((1,) + shape, lambda r, *_: (r,) + (0,) * len(shape))
    full = lambda *shape: pl.BlockSpec(shape, lambda r, *_: (0,) * len(shape))
    sds = jax.ShapeDtypeStruct
    return pl.pallas_call(
        partial(retrace_kernel, stride),
        grid_spec=pltpu.PrefetchScalarGridSpec(
            num_scalar_prefetch=1,
            grid=(rows,),
            in_specs=[
                blk(queries, D),
                blk(keys, D),
                blk(keys, D),
                blk(queries, D),
                blk(H, 8, queries),
                full(16, 128),
            ],
            out_specs=[
                blk(queries, D),
                blk(keys, D),
                blk(keys, D),
                full(8, D),
                full(H, stride, 8, queries),
                full(H, 2, 8, queries),
            ],
            scratch_shapes=[
                pltpu.VMEM((H, keys, queries), F32),
                pltpu.VMEM((queries // 128, H, keys, 128), F32),
                pltpu.VMEM((D, queries), F32),
            ],
        ),
        out_shape=[
            sds((rows, queries, D), BF16),
            sds((rows, keys, D), BF16),
            sds((rows, keys, D), BF16),
            sds((8, D), F32),
            sds((H, stride, 8, queries), F32),
            sds((H, 2, 8, queries), F32),
        ],
        compiler_params=pltpu.CompilerParams(vmem_limit_bytes=VMEM_LIMIT),
        cost_estimate=pl.CostEstimate(
            flops=rows * keys * queries * D * 10, bytes_accessed=20_000_000, transcendentals=rows * H * keys * queries
        ),
        name="retrace",
    )(lengths, q, k, v, dctx, lse, table)


def table_grad(stride, diag, ends):
    queries = diag.shape[-1]
    columns = []
    for bucket in range(NB):
        place = bucket - NB // 2
        if bucket == 0:
            columns.append(jnp.sum(ends[:, 0, 0], axis=-1))
        elif bucket == NB - 1:
            columns.append(jnp.sum(ends[:, 1, 0], axis=-1))
        else:
            part = place % stride
            columns.append(diag[:, part, 0, ((part - place) // stride) % queries])
    return jnp.stack(columns, axis=1).reshape(-1)


def inputs_kernel(stride, count, len_ref, me_ref, dq_ref, dk_ref, dv_ref, du_ref, *refs):
    sources = refs[:count]
    out_ref, entry, sem = refs[count:]
    row = pl.program_id(0)
    keys = dk_ref.shape[1]
    queries = dq_ref.shape[1]

    @pl.when(row == 0)
    def _():
        start_load(me_ref[0], sources, entry, sem.at[0], place_entry)
        wait_load(entry, sem.at[0])

    total = mm(dq_ref[0], entry[0], NT) + du_ref[0]
    if stride == 1:
        out_ref[0] = total + mm(dk_ref[0], entry[1], NT) + mm(dv_ref[0], entry[2], NT)
        return
    total = 0.5 * total
    upper = low(total)
    lower = low(total - wide(upper))
    for block in range(keys // 256):
        rows = pl.ds(block * 256, 256)
        place = lax.broadcasted_iota(jnp.int32, (256, queries), 0) + 256 * block
        mine = lax.broadcasted_iota(jnp.int32, (256, queries), 1)
        pair = jnp.where(lax.shift_right_logical(place, 1) == mine, 1.0, 0.0).astype(BF16)
        spread = mm(pair, upper) + mm(pair, lower)

        @pl.when(block * 256 < len_ref[row])
        def _():
            out_ref[0, rows, :] = (
                spread + mm(dk_ref[0, rows, :], entry[1], NT) + mm(dv_ref[0, rows, :], entry[2], NT)
            )

        @pl.when(block * 256 >= len_ref[row])
        def _():
            out_ref[0, rows, :] = spread


def input_grads(stride, index, lengths, dq, dk, dv, du, sources):
    rows, keys, _ = dk.shape
    queries = dq.shape[1]
    blk = lambda *shape: pl.BlockSpec((1,) + shape, lambda r, *_: (r,) + (0,) * len(shape))
    return pl.pallas_call(
        partial(inputs_kernel, stride, len(sources)),
        grid_spec=pltpu.PrefetchScalarGridSpec(
            num_scalar_prefetch=2,
            grid=(rows,),
            in_specs=[blk(queries, D), blk(keys, D), blk(keys, D), blk(queries, D)] + [ANY] * len(sources),
            out_specs=blk(keys, D),
            scratch_shapes=[pltpu.VMEM((3, D, D), BF16), pltpu.SemaphoreType.DMA((1,))],
        ),
        out_shape=jax.ShapeDtypeStruct((rows, keys, D), F32),
        compiler_params=pltpu.CompilerParams(vmem_limit_bytes=VMEM_LIMIT),
        cost_estimate=pl.CostEstimate(
            flops=2 * rows * (queries + keys) * D * D, bytes_accessed=20_000_000, transcendentals=0
        ),
        name="input_grads",
    )(lengths, index, dq, dk, dv, du, *sources)


def forward(stride, index, lengths, x, resid, weights, small):
    entry_leave, widen, narrow = weights
    entry, leave = entry_leave if len(widen) == 1 else (entry_leave, entry_leave)
    vectors, wide_bias, table = small
    made = attend(stride, index, lengths, x, vectors, table, entry)
    if stride == 2:
        resid, query_in, *made = made
    else:
        query_in = x
    q, k, v, ctx, lse = made
    tokens = ctx.shape[0] * ctx.shape[1]
    flat = lambda value: value.reshape(tokens, D)
    u, hidden_units, before, out = expand(
        index, flat(ctx), flat(resid), vectors, wide_bias, leave, widen, narrow
    )
    return out, (query_in, q, k, v, ctx, lse, u, hidden_units, before)


def backward(stride, index, lengths, dz, x, kept, weights, small, reduce):
    entry_leave, widen, narrow = weights
    entry, leave = entry_leave if len(widen) == 1 else (entry_leave, entry_leave)
    vectors, wide_bias, table = small
    query_in, q, k, v, ctx, lse, u, hidden_units, before = kept
    rows, queries, _ = q.shape
    dback, mixed_low, act, dhid, dattn, du, dctx, dvec, dbias = contract(
        index, dz, before, hidden_units, u, vectors, leave, widen, narrow
    )
    shape = q.shape
    sums = [narrow_grad(index, act, dback, ctx.reshape(-1, D), dattn)]
    sums.append(widen_grad(index, mixed_low, dhid))
    dq, dk, dv, dvec_top, diag, ends = retrace(
        stride, lengths, q, k, v, dctx.reshape(shape), lse, table
    )
    dvec = dvec + dvec_top
    dtable = table_grad(stride, diag, ends)
    flat = vector_units(dvec, dbias, dtable, 32)
    flat = jnp.pad(low(flat), ((0, 0), (0, 16 * HALF - flat.shape[1]))).reshape(UNITS, 2, 16, HALF)
    sums.append(entry_grad(index, lengths, query_in, x, dq, dk, dv, flat))
    dx = input_grads(stride, index, lengths, dq, dk, dv, du.reshape(shape), entry)
    return dx, [reduce(*pair) for pair in sums]


def shards(index, sums):
    core = index % 2
    narrow_leave, widen, entry = sums
    narrow = unpair(core, narrow_leave[None, :192], 96)[0]
    leave = unpair(core, narrow_leave[None, 192:], 24)[0]
    widen = unpair(core, widen[None], 24)[0]
    vectors = split_vectors(entry[144:].reshape(-1), 32)
    entry = unpair(core, entry[:144].reshape(3, 48, HALF), 24)
    return (entry, leave, widen, narrow) + vectors


def absolute_units(pair):
    send, keep = pair
    merged = jnp.concatenate([keep[:, :, None], send[:, :, None]], axis=2)
    rest = merged.shape[1:]
    merged = merged.reshape((4, 4) + rest).transpose(1, 0, 2, 3, 4)
    return wide(merged.reshape((UNITS,) + rest))


def plain_shards(sums):
    narrow_leave, widen, entry = [absolute_units(pair) for pair in sums]
    vectors = entry[:, 144:].transpose(0, 2, 1, 3).reshape(32, -1)
    narrow = narrow_leave[:, :192].reshape(FF, D)
    leave = narrow_leave[:, 192:].reshape(D, D)
    widen = widen.reshape(D, FF)
    entry = entry[:, :144].reshape(UNITS, 3, 48, D).transpose(1, 0, 2, 3).reshape(3, D, D)
    scatter = lambda value, dim: lax.psum_scatter(value, AX, scatter_dimension=dim, tiled=True)
    rows = vectors.shape[0]
    cut, mid = 8 * D // rows, 8 * D // rows + FF // rows
    last = mid + H * NB // rows
    vec = vectors[:, :cut].reshape(rows, 8, -1).transpose(1, 0, 2).reshape(8, D)
    return (
        scatter(entry, 1),
        scatter(leave, 0),
        scatter(widen, 0),
        scatter(narrow, 0),
        scatter(vec, 1),
        scatter(vectors[:, cut:mid].reshape(-1), 0),
        scatter(vectors[:, mid:last].reshape(-1), 0),
    )


def plain_gather(entry, leave, widen, narrow):
    gather = lambda value, dim: lax.all_gather(value, AX, axis=dim, tiled=True)
    return (
        ((gather(entry, 1),), (gather(leave, 0),)),
        (gather(widen, 0),),
        (gather(narrow, 0),),
    )


def small_parts(vectors, wide_bias, table):
    tab = jnp.pad(wide(table).reshape(H, NB), ((0, 16 - H), (0, 128 - NB)))
    return wide(vectors), wide(wide_bias).reshape(1, FF), tab


def unpack_small(full, parts):
    cut, mid = 8 * D // parts, (8 * D + FF) // parts
    vectors = full[:, :cut].reshape(parts, 8, -1).transpose(1, 0, 2).reshape(8, D)
    last = (8 * D + FF + H * NB) // parts
    return small_parts(vectors, full[:, cut:mid].reshape(-1), full[:, mid:last].reshape(-1))


def on_device(
    devices,
    hidden,
    lengths,
    cotangent,
    inflow,
    outflow,
    widener,
    narrower,
    shifts,
    offsets,
    distance,
    intake,
    outtake,
    expander,
    squeezer,
    adjusts,
    leanings,
    spacing,
):
    rows, seq, width = hidden.shape
    half = seq // 2
    fast = devices == 32
    index = lax.axis_index(AX)
    flat = jnp.concatenate(
        [shifts.reshape(-1), offsets, distance, adjusts.reshape(-1), leanings, spacing]
    )
    count = flat.shape[0] // 2
    if fast:
        flat = jnp.pad(flat, (0, 1024 - flat.shape[0])).reshape(8, 128)
        small = gather_vectors(index, flat)
        first, second = gather_layers(
            index, ((inflow, outflow, widener, narrower), (intake, outtake, expander, squeezer))
        )
        me = index.astype(jnp.int32).reshape(1)
    else:
        small = lax.all_gather(flat, AX, axis=0)
        first = plain_gather(inflow, outflow, widener, narrower)
        second = plain_gather(intake, outtake, expander, squeezer)
        me = jnp.zeros((1,), jnp.int32)
    small_one = unpack_small(small[:, :count], devices)
    small_two = unpack_small(small[:, count : 2 * count], devices)
    reduce = reduce_units if fast else (lambda *pair: pair)
    halved = (lengths + 1) // 2
    first_out, first_kept = forward(2, me, lengths, hidden, None, first, small_one)
    pooled_layer = first_out.reshape(rows, half, width)
    second_out, second_kept = forward(1, me, halved, pooled_layer, pooled_layer, second, small_two)
    dlayer, sums_two = backward(
        1, me, halved, cotangent.reshape(-1, width), pooled_layer, second_kept, second, small_two, reduce
    )
    hidden_grad, sums_one = backward(
        2, me, lengths, dlayer.reshape(-1, width), hidden, first_kept, first, small_one, reduce
    )
    if fast:
        shards_one, shards_two = shards(index, sums_one), shards(index, sums_two)
    else:
        shards_one, shards_two = plain_shards(sums_one), plain_shards(sums_two)
    return (
        pooled_layer,
        second_out.reshape(rows, half, width),
        hidden_grad,
        *shards_one,
        *shards_two[:4],
        shards_two[4][1:],
        shards_two[5],
        shards_two[6],
        shards_two[4][0],
    )


def solution(mesh):
    both = ("wide", "narrow")
    rows = P(both, None, None)
    weights = (
        P(None, both, None),
        P(both, None),
        P(both, None),
        P(both, None),
        P(None, both),
        P(both),
        P(both),
    )
    return jax.shard_map(
        partial(on_device, mesh.size),
        mesh=mesh,
        in_specs=(rows, P(both), rows) + weights + weights,
        out_specs=(rows, rows, rows) + weights + weights + (P(both),),
        check_vma=False,
    )
```

```python
from functools import partial

import jax
import jax.numpy as jnp
from jax import lax
from jax.experimental import pallas as pl
from jax.experimental.pallas import tpu as pltpu
from jax.sharding import PartitionSpec as P

H = 12
HD = 64
NB = 32
D = 768
FF = 3072
HALF = 384
EPS = 1e-06
AX = ("wide", "narrow")
CORE, XBIT, YBIT, Z0, Z1 = 1, 2, 4, 8, 16
UNITS = 16
F32 = jnp.float32
BF16 = jnp.bfloat16
GELU_A = 0.7978845608028654
GELU_B = 0.044715
NN = (((1,), (0,)), ((), ()))
NT = (((1,), (1,)), ((), ()))
TN = (((0,), (0,)), ((), ()))
GROUPS = (6, 3, 2, 2)
TILE_A = 256
TILE_B = 256
VMEM_LIMIT = 60 * 1024 * 1024
ANY = pl.BlockSpec(memory_space=pl.ANY)


def mm(left, right, dims=NN):
    return lax.dot_general(left, right, dims, preferred_element_type=F32)


def wide(value):
    return value.astype(F32)


def low(value):
    return value.astype(BF16)


SENT = []


def swap(value, mask):
    SENT.append(value)
    return lax.ppermute(value, AX, [(i, i ^ mask) for i in range(32)])


def pick(core, first, second):
    return jnp.where(core == 0, first, second)


class Job:
    def __init__(self, stages, *operands):
        self.stages = stages(*operands)
        self.operands = next(self.stages)
        self.result = None

    def step(self, operands):
        try:
            self.operands = self.stages.send(operands)
        except StopIteration as stop:
            self.result = stop.value
            self.operands = ()


class Ticks:
    def __init__(self, me):
        self.me = me
        self.last = ()
        self.flying = []

    def run(self, jobs, kernel=None):
        jobs = [job for job in jobs if job.result is None]
        tied = jobs + [job for job in self.flying if job not in jobs]
        operands = [job.operands if job.result is None else job.result for job in tied]
        self.me, operands, self.last = lax.optimization_barrier((self.me, operands, self.last))
        SENT.clear()
        for job, value in zip(tied, operands):
            if job in jobs:
                job.step(value)
            elif job.result is None:
                job.operands = value
            else:
                job.result = value
        self.flying = jobs
        if kernel is None:
            return None
        self.me = lax.optimization_barrier((self.me, list(SENT)))[0]
        out = kernel(self.me)
        self.last = jax.tree.leaves(out)[-1]
        return out


def gather_stages(pair, direct, keep, send):
    keep, send = yield keep, send
    core = lax.axis_index(AX) % 2
    recv = swap(send, CORE)
    slab = pair(pick(core, keep, recv), pick(core, recv, keep))
    slab = yield slab
    if direct:
        own = jnp.stack([slab, swap(slab, Z0), swap(slab, Z1), swap(slab, Z0 | Z1)])
    else:
        two = jnp.stack([slab, swap(slab, Z0)])
        two = yield two
        own = jnp.concatenate([two, swap(two, Z1)])
    own = yield own
    across_y = swap(own, YBIT)
    across_x = swap(own, XBIT)
    far = (swap(own, CORE),)
    own, across_y, across_x, far = yield own, across_y, across_x, far
    diag = (swap(across_y[:2], XBIT), swap(across_x[2:], YBIT))
    far = far + (swap(across_x, CORE), swap(across_y, CORE))
    mine, far = yield (own, across_x, across_y) + diag, far
    return mine + far + tuple(swap(piece, CORE) for piece in mine[3:])


def vector_stages(slab):
    slab = yield slab
    own = jnp.stack([slab, swap(slab, Z0), swap(slab, Z1), swap(slab, Z0 | Z1)])
    own = yield own
    across = [own, swap(own, XBIT), swap(own, YBIT), swap(own, XBIT | YBIT)]
    across = yield across
    near = jnp.concatenate(across)
    return near, swap(near, CORE)


def pair_entry(first, second):
    return jnp.concatenate([first.reshape(4, 24, HALF), second.reshape(4, 24, HALF)], axis=1)


def pair_wide(first, second):
    widen = jnp.concatenate([first[:96].reshape(4, 24, HALF), second[:96].reshape(4, 24, HALF)], axis=1)
    widen = widen.reshape(2, 2, 48, HALF).transpose(0, 2, 1, 3).reshape(2, 48, D)
    narrow = jnp.concatenate([first[96:].reshape(2, 48, HALF), second[96:].reshape(2, 48, HALF)], axis=2)
    return jnp.concatenate([widen, narrow], axis=0)


def gather_jobs(core, direct, entry, leave, widen, narrow):
    def halved(value):
        return pick(core, value[0], value[1]), pick(core, value[1], value[0])

    eo = jnp.concatenate([entry, leave[None]]).reshape(96, 2, HALF).transpose(1, 0, 2)
    widen = widen.reshape(24, 2, 4, HALF).transpose(1, 2, 0, 3).reshape(2, 96, HALF)
    narrow = narrow.reshape(96, 2, HALF).transpose(1, 0, 2)
    both = jnp.concatenate([widen, narrow], axis=1)
    return (
        Job(gather_stages, pair_entry, direct, *halved(eo)),
        Job(gather_stages, pair_wide, False, *halved(both)),
    )


def reduce_stages(core, cuts, send, keep):
    shape = (4, 4) + keep.shape[1:]
    send, keep = yield send, keep
    keep = keep.reshape(shape)
    recv = swap(send, CORE).reshape(shape)
    keep, recv = yield keep, recv
    diag_low = swap(low(wide(keep[3, :2]) + wide(recv[3, :2])), XBIT)
    diag_high = swap(low(wide(keep[3, 2:]) + wide(recv[3, 2:])), YBIT)
    keep, recv, diag_low, diag_high = yield keep, recv, diag_low, diag_high
    to_y = wide(keep[2]) + wide(recv[2])
    to_x = wide(keep[1]) + wide(recv[1])
    rest = [(0, 0)] * 2
    to_y = low(to_y + jnp.pad(wide(diag_low), [(0, 2)] + rest))
    to_x = low(to_x + jnp.pad(wide(diag_high), [(2, 0)] + rest))
    from_y, from_x = swap(to_y, YBIT), swap(to_x, XBIT)
    keep, recv, from_y, from_x = yield keep, recv, from_y, from_x

    def part(k):
        return (wide(keep[0, k]) + wide(recv[0, k])) + (wide(from_y[k]) + wide(from_x[k]))

    far = swap(jnp.stack([low(part(2)), low(part(3))]), Z1)
    keep, recv, from_y, from_x, far = yield keep, recv, from_y, from_x, far
    near = swap(low(part(1) + wide(far[1])), Z0)
    keep, recv, from_y, from_x, far, near = yield keep, recv, from_y, from_x, far, near
    total = part(0) + wide(far[0]) + wide(near)
    keeps, sends = [], []
    start = 0
    for rows, group in cuts:
        slab = total[start : start + rows].reshape(-1, 2, group, HALF)
        start += rows
        keeps.append(pick(core, slab[:, 0], slab[:, 1]).reshape(-1, HALF))
        sends.append(pick(core, slab[:, 1], slab[:, 0]).reshape(-1, HALF))
    rest = total[start:]
    keep, send = jnp.concatenate(keeps), jnp.concatenate(sends)
    recv = swap(send, CORE)
    return pick(core, keep, recv), pick(core, recv, keep), rest


def vector_units(vectors, wide_bias, table, parts):
    flat = jnp.concatenate(
        [
            vectors.reshape(8, parts, -1).transpose(1, 0, 2).reshape(parts, -1),
            wide_bias.reshape(parts, -1),
            table.reshape(parts, -1),
        ],
        axis=1,
    )
    return flat


def split_vectors(flat, parts):
    cut = 8 * D // parts
    mid = cut + FF // parts
    return flat[:cut].reshape(8, -1), flat[cut:mid], flat[mid : mid + H * NB // parts]


def position(chip, unit):
    rel = jnp.bitwise_xor(chip, unit)
    return jnp.bitwise_and(rel, 3) * 4 + lax.shift_right_logical(rel, 2)


def start_load(me, refs, dst, sem, place):
    if len(refs) == 1:
        pltpu.make_async_copy(refs[0], dst, sem).start()
        return
    chip = lax.shift_right_logical(me, 1)
    for side in range(2):
        half = jnp.bitwise_xor(jnp.bitwise_and(me, 1), side)
        own, across_x, across_y, diag_low, diag_high = refs[5 * side : 5 * side + 5]
        for k in range(4):
            for step, ref, at in (
                (0, own, k),
                (1, across_x, k),
                (2, across_y, k),
                (3, diag_low if k < 2 else diag_high, k % 2),
            ):
                unit = jnp.bitwise_xor(chip, 4 * k + step)
                for source, target in place(ref.at[at], dst, unit, half):
                    pltpu.make_async_copy(source, target, sem).start()


def wait_load(dst, sem):
    pltpu.make_async_copy(dst, dst, sem).wait()


def place_entry(src, dst, unit, half):
    rows, cols = pl.multiple_of(unit * 48, 16), pl.multiple_of(half * HALF, 128)
    return [(src.at[0:3], dst.at[:, pl.ds(rows, 48), pl.ds(cols, HALF)])]


def place_leave(src, dst, unit, half):
    rows, cols = pl.multiple_of(unit * 48, 16), pl.multiple_of(half * HALF, 128)
    return [(src.at[3], dst.at[pl.ds(rows, 48), pl.ds(cols, HALF)])]


def place_widen(src, dst, unit, half):
    rows = pl.multiple_of(unit * 48, 16)
    return [(src.at[0:2], dst.at[pl.ds(half * 2, 2), pl.ds(rows, 48), :])]


def place_narrow(src, dst, unit, half):
    cols = pl.multiple_of(half * HALF, 128)
    return [
        (
            src.at[2:4, :, HALF * g : HALF * g + HALF],
            dst.at[pl.ds(unit * 4 + 2 * g, 2), :, pl.ds(cols, HALF)],
        )
        for g in range(2)
    ]


def build_bias(table, bias, stride):
    keys = bias.shape[1]
    for part in range(bias.shape[2] // 128):
        row = lax.broadcasted_iota(jnp.int32, (keys, 128), 0)
        col = lax.broadcasted_iota(jnp.int32, (keys, 128), 1) + 128 * part
        bucket = jnp.clip(row - stride * col, -(NB // 2), NB // 2 - 1) + NB // 2
        for h in range(H):
            values = jnp.broadcast_to(table[h : h + 1, :], (keys, 128))
            bias[h, :, 128 * part : 128 * part + 128] = low(
                jnp.take_along_axis(values, bucket, axis=1, mode="promise_in_bounds")
            )


def prepare_kernel(me_ref, near_ref, far_ref, *refs):
    outs, tables = refs[:6], refs[6:]
    core = jnp.bitwise_and(me_ref[0], 1)
    chip = lax.shift_right_logical(me_ref[0], 1)
    for table in tables:
        table[...] = jnp.zeros_like(table)
    for d in range(32):
        at = position(chip, d // 2)
        slab = jnp.where(core == d % 2, wide(near_ref[at]), wide(far_ref[at]))
        for layer in range(2):
            vec_ref, wide_ref = outs[3 * layer], outs[3 * layer + 1]
            rows = slab[8 * layer : 8 * layer + 8]
            vec_ref[:, 24 * d : 24 * d + 24] = rows[:, :24]
            wide_ref[:, 96 * d : 96 * d + 96] = rows[0:1, 32:128]
            h, start = 12 * d // NB, 12 * d % NB
            count = min(12, NB - start)
            tables[layer][h : h + 1, start : start + count] = rows[1:2, 32 : 32 + count]
            if count < 12:
                tables[layer][h + 1 : h + 2, 0 : 12 - count] = rows[1:2, 32 + count : 44]
    build_bias(tables[0], outs[2], 2)
    build_bias(tables[1], outs[5], 1)


def prepare(index, near, far, keys, queries):
    sds = jax.ShapeDtypeStruct
    shapes = []
    for length in (keys, queries):
        shapes += [sds((8, D), F32), sds((1, FF), F32), sds((H, length, queries), BF16)]
    return pl.pallas_call(
        prepare_kernel,
        grid_spec=pltpu.PrefetchScalarGridSpec(
            num_scalar_prefetch=1,
            grid=(1,),
            in_specs=[whole(UNITS, 16, 128)] * 2,
            out_specs=[whole(*shape.shape) for shape in shapes],
            scratch_shapes=[pltpu.VMEM((16, 128), F32)] * 2,
        ),
        out_shape=shapes,
        compiler_params=pltpu.CompilerParams(vmem_limit_bytes=VMEM_LIMIT),
        cost_estimate=pl.CostEstimate(flops=10_000_000, bytes_accessed=10_000_000, transcendentals=0),
        name="prepare",
    )(index, near, far)


def vector_slab(vectors_one, wide_one, table_one, vectors_two, wide_two, table_two):
    lead = wide_one.shape[:-1]
    left = jnp.concatenate([vectors_one, vectors_two], axis=-2)
    left = jnp.pad(left, [(0, 0)] * (left.ndim - 1) + [(0, 8)])
    rows = []
    for wide_bias, table in ((wide_one, table_one), (wide_two, table_two)):
        table = jnp.pad(table, [(0, 0)] * len(lead) + [(0, 84)])
        pair = jnp.stack([wide_bias, table], axis=-2)
        rows.append(jnp.pad(pair, [(0, 0)] * len(lead) + [(0, 6), (0, 0)]))
    return jnp.concatenate([left, jnp.concatenate(rows, axis=-2)], axis=-1)


def whole(*shape):
    return pl.BlockSpec(shape, lambda r, *_: (0,) * len(shape))


def lane_masks(value):
    lane = lax.broadcasted_iota(jnp.int32, value.shape, 1)
    zero = jnp.zeros_like(value)
    return jnp.where(lane < HD, value, zero), jnp.where(lane < HD, zero, value)


def masked_scores(keys, query, bias, count):
    scores = mm(keys, query, NT) + wide(bias)
    size = scores.shape[0]
    head, tail = scores[: size - 128], scores[size - 128 :]
    row = lax.broadcasted_iota(jnp.int32, tail.shape, 0) + (size - 128)
    tail = jnp.where(row < count, tail, -1e30)
    return tail if size == 128 else jnp.concatenate([head, tail], axis=0)


def statistics(value):
    mean = jnp.mean(value, axis=-1, keepdims=True)
    centred = value - mean
    spread = jnp.mean(centred * centred, axis=-1, keepdims=True)
    rstd = lax.rsqrt(spread + EPS)
    return centred * rstd, rstd


def norm_pull(grad, unit, rstd):
    return rstd * (
        grad
        - jnp.mean(grad, axis=-1, keepdims=True)
        - unit * jnp.mean(grad * unit, axis=-1, keepdims=True)
    )


def column_sum(value):
    return jnp.sum(value, axis=0, keepdims=True)


def project_kernel(stride, count, len_ref, me_ref, x_ref, vec_ref, *refs):
    sources = refs[:count]
    refs = refs[count:]
    if stride == 2:
        pooled_ref, pooled_low_ref, *refs = refs
    q_ref, k_ref, v_ref, entry, sem = refs
    row = pl.program_id(0)
    keys = x_ref.shape[1]
    queries = q_ref.shape[1]

    @pl.when(row == 0)
    def _():
        start_load(me_ref[0], sources, entry, sem.at[0], place_entry)
        wait_load(entry, sem.at[0])

    length = len_ref[row]
    if stride == 2:
        place = lax.broadcasted_iota(jnp.int32, (queries, keys), 1)
        mine = lax.broadcasted_iota(jnp.int32, (queries, keys), 0)
        pair = jnp.where(lax.shift_right_logical(place, 1) == mine, 0.5, 0.0).astype(BF16)
        pooled = mm(pair, x_ref[0])
        pooled_ref[0] = pooled
        query_in = low(pooled)
        pooled_low_ref[0] = query_in
    else:
        query_in = x_ref[0]
    q_ref[0] = low(wide(low(mm(query_in, entry[0]) + vec_ref[0:1, :])) * HD**-0.5)
    for block in range(keys // 256):

        @pl.when(block * 256 < length)
        def _():
            rows = pl.ds(block * 256, 256)
            x = x_ref[0, rows, :]
            k_ref[0, rows, :] = low(mm(x, entry[1]))
            v_ref[0, rows, :] = low(mm(x, entry[2]) + vec_ref[1:2, :])


def project(stride, index, lengths, x, vectors, sources):
    rows, keys, _ = x.shape
    queries = keys // stride
    blk = lambda *shape: pl.BlockSpec((1,) + shape, lambda r, *_: (r,) + (0,) * len(shape))
    full = lambda *shape: pl.BlockSpec(shape, lambda r, *_: (0,) * len(shape))
    sds = jax.ShapeDtypeStruct
    outs = [
        (sds((rows, queries, D), BF16), blk(queries, D)),
        (sds((rows, keys, D), BF16), blk(keys, D)),
        (sds((rows, keys, D), BF16), blk(keys, D)),
    ]
    if stride == 2:
        outs = [
            (sds((rows, queries, D), F32), blk(queries, D)),
            (sds((rows, queries, D), BF16), blk(queries, D)),
        ] + outs
    return pl.pallas_call(
        partial(project_kernel, stride, len(sources)),
        grid_spec=pltpu.PrefetchScalarGridSpec(
            num_scalar_prefetch=2,
            grid=(rows,),
            in_specs=[blk(keys, D), full(8, D)] + [ANY] * len(sources),
            out_specs=[o[1] for o in outs],
            scratch_shapes=[pltpu.VMEM((3, D, D), BF16), pltpu.SemaphoreType.DMA((1,))],
        ),
        out_shape=[o[0] for o in outs],
        compiler_params=pltpu.CompilerParams(vmem_limit_bytes=VMEM_LIMIT),
        cost_estimate=pl.CostEstimate(
            flops=rows * keys * D * D * 4, bytes_accessed=20_000_000, transcendentals=0
        ),
        name="project",
    )(lengths, index, x, vectors, *sources)


def attend_kernel(base, len_ref, me_ref, q_ref, k_ref, v_ref, bias, *refs):
    ctx_ref, probs_ref, turned = refs[-3:]
    row = pl.program_id(0)
    keys = k_ref.shape[1]
    length = len_ref[row + base]

    def group_step(size, pairs, step, carry):
        made = []
        for p in range(pairs):
            lanes = pl.ds(pl.multiple_of((step * pairs + p) * 128, 128), 128)
            queries_low = lane_masks(q_ref[0, :, lanes])
            key = k_ref[0, :size, lanes]
            value = v_ref[0, :size, lanes].T
            for i in range(2):
                h = 2 * (step * pairs + p) + i
                scores = masked_scores(key, queries_low[i], bias[h, :size, :], length)
                made.append((h, scores, value[HD * i : HD * i + HD]))
        kept = []
        for h, scores, value in made:
            top = jnp.max(scores, axis=0, keepdims=True)
            probs = jnp.exp(scores - top)
            probs = low(probs * (1.0 / jnp.sum(probs, axis=0, keepdims=True)))
            probs_ref[0, h, :size, :] = probs
            kept.append((h, probs, value))
        for h, probs, value in kept:
            turned[pl.ds(pl.multiple_of(HD * h, HD), HD), :] = mm(value, probs)
        return carry

    blocks = lax.div(length + 127, 128)
    for w in range(1, keys // 128 + 1):

        @pl.when(blocks == w)
        def _():
            pairs = GROUPS[w - 1]
            lax.fori_loop(0, H // 2 // pairs, partial(group_step, 128 * w, pairs), 0)

    ctx_ref[0] = low(turned[...].T)


def attend(stride, index, lengths, q, k, v, table, base, count, before=()):
    rows, keys, _ = k.shape
    queries = keys // stride
    blk = lambda *shape: pl.BlockSpec((1,) + shape, lambda r, *_: (r + base,) + (0,) * len(shape))
    full = lambda *shape: pl.BlockSpec(shape, lambda r, *_: (0,) * len(shape))
    sds = jax.ShapeDtypeStruct
    return pl.pallas_call(
        partial(attend_kernel, base),
        grid_spec=pltpu.PrefetchScalarGridSpec(
            num_scalar_prefetch=2,
            grid=(count,),
            in_specs=[blk(queries, D), blk(keys, D), blk(keys, D), full(H, keys, queries)]
            + [ANY] * len(before),
            out_specs=[blk(queries, D), blk(H, keys, queries)],
            scratch_shapes=[pltpu.VMEM((D, queries), F32)],
        ),
        out_shape=[sds((rows, queries, D), BF16), sds((rows, H, keys, queries), BF16)],
        input_output_aliases={6 + i: i for i in range(len(before))},
        compiler_params=pltpu.CompilerParams(vmem_limit_bytes=VMEM_LIMIT),
        cost_estimate=pl.CostEstimate(
            flops=count * keys * queries * D * 8,
            bytes_accessed=20_000_000,
            transcendentals=count * H * keys * queries,
        ),
        name="attend",
    )(lengths, index, q, k, v, table, *before)


def expand_kernel(counts, me_ref, ctx_ref, resid_ref, vec_ref, bias_ref, *refs):
    c1, c2, c3 = counts
    leave_src, widen_src, narrow_src = refs[:c1], refs[c1 : c1 + c2], refs[c1 + c2 : c1 + c2 + c3]
    u_ref, act_ref, slope_ref, before_ref, out_ref, leave, widen, narrow, sem = refs[c1 + c2 + c3 :]
    first = pl.program_id(0) == 0

    @pl.when(first)
    def _():
        start_load(me_ref[0], leave_src, leave, sem.at[0], place_leave)
        start_load(me_ref[0], widen_src, widen, sem.at[1], place_widen)
        start_load(me_ref[0], narrow_src, narrow, sem.at[2], place_narrow)
        wait_load(leave, sem.at[0])

    u = wide(resid_ref[...]) + mm(ctx_ref[...], leave[...]) + vec_ref[2:3, :]
    u_ref[...] = u
    unit, _ = statistics(u)
    mixed = unit * vec_ref[3:4, :] + vec_ref[4:5, :]
    mixed_low = low(mixed)

    @pl.when(first)
    def _():
        wait_load(widen, sem.at[1])
        wait_load(narrow, sem.at[2])

    total = mixed + vec_ref[5:6, :]
    for j in range(4):
        cols = slice(D * j, D * j + D)
        h = mm(mixed_low, widen[j]) + bias_ref[0:1, cols]
        square = h * h
        gate = 0.5 + 0.5 * jnp.tanh(h * (GELU_A + GELU_A * GELU_B * square))
        act = h * gate
        slope = gate + act * (1.0 - gate) * (2.0 * GELU_A + 6.0 * GELU_A * GELU_B * square)
        slope_ref[:, cols] = low(slope)
        act = low(act)
        act_ref[:, cols] = act
        total = total + mm(act, narrow[16 * j : 16 * j + 16].reshape(D, D))
    before_ref[...] = total
    unit, _ = statistics(total)
    out_ref[...] = low(unit * vec_ref[6:7, :] + vec_ref[7:8, :])


def expand(index, ctx, resid, vectors, wide_bias, leave, widen, narrow):
    tokens = ctx.shape[0]
    tile = TILE_A
    blk = lambda width: pl.BlockSpec((tile, width), lambda r, *_: (r, 0))
    full = lambda *shape: pl.BlockSpec(shape, lambda r, *_: (0,) * len(shape))
    sds = jax.ShapeDtypeStruct
    sources = tuple(leave) + tuple(widen) + tuple(narrow)
    return pl.pallas_call(
        partial(expand_kernel, (len(leave), len(widen), len(narrow))),
        grid_spec=pltpu.PrefetchScalarGridSpec(
            num_scalar_prefetch=1,
            grid=(tokens // tile,),
            in_specs=[blk(D), blk(D), full(8, D), full(1, FF)] + [ANY] * len(sources),
            out_specs=[blk(D), blk(FF), blk(FF), blk(D), blk(D)],
            scratch_shapes=[
                pltpu.VMEM((D, D), BF16),
                pltpu.VMEM((4, D, D), BF16),
                pltpu.VMEM((64, 48, D), BF16),
                pltpu.SemaphoreType.DMA((3,)),
            ],
        ),
        out_shape=[
            sds((tokens, D), F32),
            sds((tokens, FF), BF16),
            sds((tokens, FF), BF16),
            sds((tokens, D), F32),
            sds((tokens, D), BF16),
        ],
        compiler_params=pltpu.CompilerParams(vmem_limit_bytes=VMEM_LIMIT),
        cost_estimate=pl.CostEstimate(
            flops=2 * tokens * D * (D + 2 * FF), bytes_accessed=30_000_000, transcendentals=tokens * FF
        ),
        name="expand",
    )(index, ctx, resid, vectors, wide_bias, *sources)


def contract_kernel(counts, me_ref, dz_ref, before_ref, slope_ref, u_ref, vec_ref, *refs):
    c1, c2, c3 = counts
    leave_src, widen_src, narrow_src = refs[:c1], refs[c1 : c1 + c2], refs[c1 + c2 : c1 + c2 + c3]
    refs = refs[c1 + c2 + c3 :]
    dback_ref, mixed_ref, dhid_ref, dattn_ref, du_ref, dctx_ref, dvec_ref, dbias_ref = refs[:8]
    leave, widen, narrow, sem = refs[8:]
    first = pl.program_id(0) == 0

    @pl.when(first)
    def _():
        start_load(me_ref[0], narrow_src, narrow, sem.at[2], place_narrow)
        start_load(me_ref[0], widen_src, widen, sem.at[1], place_widen)
        start_load(me_ref[0], leave_src, leave, sem.at[0], place_leave)
        dvec_ref[...] = jnp.zeros_like(dvec_ref)
        dbias_ref[...] = jnp.zeros_like(dbias_ref)

    dz = wide(dz_ref[...])
    unit, rstd = statistics(before_ref[...])
    dvec_ref[6:7, :] += column_sum(dz * unit)
    dvec_ref[7:8, :] += column_sum(dz)
    dpre = norm_pull(dz * vec_ref[6:7, :], unit, rstd)
    dback = low(dpre)
    dback_ref[...] = dback
    dvec_ref[5:6, :] += column_sum(wide(dback))
    unit, rstd = statistics(u_ref[...])
    mixed_ref[...] = low(unit * vec_ref[3:4, :] + vec_ref[4:5, :])

    @pl.when(first)
    def _():
        wait_load(narrow, sem.at[2])
        wait_load(widen, sem.at[1])
        wait_load(leave, sem.at[0])

    dmixed = dpre
    for j in range(4):
        cols = slice(D * j, D * j + D)
        dact = mm(dback, narrow[16 * j : 16 * j + 16].reshape(D, D), NT)
        dhid = low(dact * wide(slope_ref[:, cols]))
        dhid_ref[:, cols] = dhid
        dbias_ref[:, cols] += column_sum(wide(dhid))
        dmixed = dmixed + mm(dhid, widen[j], NT)
    dvec_ref[3:4, :] += column_sum(dmixed * unit)
    dvec_ref[4:5, :] += column_sum(dmixed)
    du = norm_pull(dmixed * vec_ref[3:4, :], unit, rstd)
    du_ref[...] = du
    dattn = low(du)
    dattn_ref[...] = dattn
    dvec_ref[2:3, :] += column_sum(wide(dattn))
    dctx_ref[...] = low(mm(dattn, leave[...], NT))


def contract(index, dz, before, hidden_units, u, vectors, leave, widen, narrow):
    tokens = dz.shape[0]
    tile = TILE_B
    blk = lambda width: pl.BlockSpec((tile, width), lambda r, *_: (r, 0))
    full = lambda *shape: pl.BlockSpec(shape, lambda r, *_: (0,) * len(shape))
    sds = jax.ShapeDtypeStruct
    sources = tuple(leave) + tuple(widen) + tuple(narrow)
    return pl.pallas_call(
        partial(contract_kernel, (len(leave), len(widen), len(narrow))),
        grid_spec=pltpu.PrefetchScalarGridSpec(
            num_scalar_prefetch=1,
            grid=(tokens // tile,),
            in_specs=[blk(D), blk(D), blk(FF), blk(D), full(8, D)] + [ANY] * len(sources),
            out_specs=[blk(D), blk(D), blk(FF), blk(D), blk(D), blk(D), full(8, D), full(1, FF)],
            scratch_shapes=[
                pltpu.VMEM((D, D), BF16),
                pltpu.VMEM((4, D, D), BF16),
                pltpu.VMEM((64, 48, D), BF16),
                pltpu.SemaphoreType.DMA((3,)),
            ],
        ),
        out_shape=[
            sds((tokens, D), BF16),
            sds((tokens, D), BF16),
            sds((tokens, FF), BF16),
            sds((tokens, D), BF16),
            sds((tokens, D), F32),
            sds((tokens, D), BF16),
            sds((8, D), F32),
            sds((1, FF), F32),
        ],
        compiler_params=pltpu.CompilerParams(vmem_limit_bytes=VMEM_LIMIT),
        cost_estimate=pl.CostEstimate(
            flops=2 * tokens * D * (D + 2 * FF), bytes_accessed=50_000_000, transcendentals=tokens * FF
        ),
        name="contract",
    )(index, dz, before, hidden_units, u, vectors, *sources)


def halves(core, value, width):
    left, right = value[:, :width], value[:, width:]
    first = core == 0
    return jnp.where(first, right, left), jnp.where(first, left, right)


def flush(pairs, start, rows, sem):
    copies = [
        pltpu.make_async_copy(scratch, out_ref.at[:, start : start + rows, :], sem.at[i])
        for i, (scratch, out_ref) in enumerate(pairs)
    ]
    for copy in copies:
        copy.start()
    for copy in copies:
        copy.wait()


def sum_call(kernel, name, total_rows, start, rows, grid, prefetch, inputs, in_specs, scratch, before, flops):
    out = jax.ShapeDtypeStruct((UNITS, total_rows, HALF), BF16)
    return pl.pallas_call(
        partial(kernel, start, rows),
        grid_spec=pltpu.PrefetchScalarGridSpec(
            num_scalar_prefetch=len(prefetch),
            grid=grid,
            in_specs=in_specs + [ANY] * len(before),
            out_specs=[ANY, ANY],
            scratch_shapes=[
                pltpu.VMEM((UNITS, rows, HALF), BF16),
                pltpu.VMEM((UNITS, rows, HALF), BF16),
                pltpu.SemaphoreType.DMA((2,)),
            ]
            + scratch,
        ),
        out_shape=[out, out],
        input_output_aliases={len(prefetch) + len(inputs) + i: i for i in range(len(before))},
        compiler_params=pltpu.CompilerParams(vmem_limit_bytes=VMEM_LIMIT),
        cost_estimate=pl.CostEstimate(flops=flops, bytes_accessed=16_000_000, transcendentals=0),
        name=name,
    )(*prefetch, *inputs, *before)


def narrow_grad_kernel(start, rows, me_ref, act_ref, dback_ref, ctx_ref, dattn_ref, *refs):
    send_out, keep_out, send_ref, keep_ref, sem = refs[-5:]
    step = pl.program_id(0)
    core = jnp.bitwise_and(me_ref[0], 1)
    chip = lax.shift_right_logical(me_ref[0], 1)

    @pl.when(step < 4)
    def _():
        send, keep = halves(core, mm(act_ref[...], dback_ref[...], TN), HALF)
        for i in range(4):
            at = position(chip, step * 4 + i)
            send_ref[at, 0:192, :] = low(send[192 * i : 192 * i + 192])
            keep_ref[at, 0:192, :] = low(keep[192 * i : 192 * i + 192])

    @pl.when(step == 4)
    def _():
        send, keep = halves(core, mm(ctx_ref[...], dattn_ref[...], TN), HALF)
        for i in range(UNITS):
            at = position(chip, i)
            send_ref[at, 192:240, :] = low(send[48 * i : 48 * i + 48])
            keep_ref[at, 192:240, :] = low(keep[48 * i : 48 * i + 48])
        flush(((send_ref, send_out), (keep_ref, keep_out)), start, rows, sem)


def halves(core, value, width):
    left, right = value[:, :width], value[:, width:]
    first = core == 0
    return jnp.where(first, right, left), jnp.where(first, left, right)


def narrow_grad(total_rows, index, act, dback, ctx, dattn):
    tokens = act.shape[0]
    specs = [pl.BlockSpec((tokens, D), lambda r, *_: (0, jnp.minimum(r, 3)))] + [whole(tokens, D)] * 3
    return sum_call(
        narrow_grad_kernel, "narrow_grad", total_rows, 0, 240, (5,), (index,),
        (act, dback, ctx, dattn), specs, [], (), 2 * tokens * D * (D + FF),
    )


def widen_grad_kernel(start, rows, me_ref, mixed_ref, dhid_ref, *refs):
    send_out, keep_out, send_ref, keep_ref, sem, turned = refs[-6:]
    step = pl.program_id(0)
    core = jnp.bitwise_and(me_ref[0], 1)
    chip = lax.shift_right_logical(me_ref[0], 1)

    @pl.when(step == 0)
    def _():
        turned[...] = mixed_ref[...].T

    grad = low(mm(turned[...], dhid_ref[...]))
    mine = lax.div(step, 2) == core
    for part in range(2):

        @pl.when(lax.rem(step, 2) == part)
        def _():
            for wanted, out_ref in ((True, keep_ref), (False, send_ref)):

                @pl.when(mine == wanted)
                def _():
                    for i in range(UNITS):
                        at = position(chip, i)
                        for q in range(2):
                            line = 96 * part + 48 * q
                            out_ref[at, line : line + 48, :] = grad[
                                48 * i : 48 * i + 48, HALF * q : HALF * q + HALF
                            ]

    @pl.when(step == 3)
    def _():
        flush(((send_ref, send_out), (keep_ref, keep_out)), start, rows, sem)


def widen_grad(total_rows, index, mixed_low, dhid, before):
    start = 240 if before else 0
    tokens = mixed_low.shape[0]
    specs = [whole(tokens, D), pl.BlockSpec((tokens, D), lambda r, *_: (0, r))]
    return sum_call(
        widen_grad_kernel, "widen_grad", total_rows, start, 192, (4,), (index,),
        (mixed_low, dhid), specs, [pltpu.VMEM((D, tokens), BF16)], before, 2 * tokens * D * FF,
    )


def entry_grad_kernel(start, rows, len_ref, me_ref, a_ref, b_ref, dq_ref, dk_ref, dv_ref, vec_ref, *refs):
    send_out, keep_out, send_ref, keep_ref, sem, total = refs[-6:]
    row = pl.program_id(0)
    core = jnp.bitwise_and(me_ref[0], 1)
    chip = lax.shift_right_logical(me_ref[0], 1)
    keys = b_ref.shape[1]

    @pl.when(row == 0)
    def _():
        total[...] = jnp.zeros_like(total)

    total[0] += mm(a_ref[0], dq_ref[0], TN)
    for block in range(keys // 256):

        @pl.when(block * 256 < len_ref[row])
        def _():
            lines = pl.ds(block * 256, 256)
            b = b_ref[0, lines, :].T
            total[1] += mm(b, dk_ref[0, lines, :])
            total[2] += mm(b, dv_ref[0, lines, :])

    @pl.when(row == pl.num_programs(0) - 1)
    def _():
        for m in range(3):
            send, keep = halves(core, total[m], HALF)
            for i in range(UNITS):
                at = position(chip, i)
                send_ref[at, 48 * m : 48 * m + 48, :] = low(send[48 * i : 48 * i + 48])
                keep_ref[at, 48 * m : 48 * m + 48, :] = low(keep[48 * i : 48 * i + 48])
        for i in range(UNITS):
            at = position(chip, i)
            send_ref[at, 144:160, :] = vec_ref[i, 1 - core]
            keep_ref[at, 144:160, :] = vec_ref[i, core]
        flush(((send_ref, send_out), (keep_ref, keep_out)), start, rows, sem)


def entry_grad(total_rows, start, index, lengths, a, b, dq, dk, dv, vec, before):
    rows, keys, _ = b.shape
    queries = a.shape[1]
    blk = lambda *shape: pl.BlockSpec((1,) + shape, lambda r, *_: (r,) + (0,) * len(shape))
    specs = [blk(queries, D), blk(keys, D), blk(queries, D), blk(keys, D), blk(keys, D)]
    specs.append(whole(UNITS, 2, 16, HALF))
    return sum_call(
        entry_grad_kernel, "entry_grad", total_rows, start, 160, (rows,), (lengths, index),
        (a, b, dq, dk, dv, vec), specs, [pltpu.VMEM((3, D, D), F32)], before,
        2 * rows * (queries + keys) * D * D,
    )


def retrace_kernel(stride, base, len_ref, me_ref, q_ref, k_ref, v_ref, dctx_ref, probs_ref, *refs):
    dq_ref, dk_ref, dv_ref, dvec_ref, diag_ref, ends_ref, bias_sum, turned = refs[-8:]
    row = pl.program_id(0)
    keys = k_ref.shape[1]
    queries = q_ref.shape[1]
    length = len_ref[row + base]

    @pl.when(row == 0)
    def _():
        bias_sum[...] = jnp.zeros_like(bias_sum)
        dvec_ref[...] = jnp.zeros_like(dvec_ref)

    def group_step(size, pairs, step, carry):
        loaded = []
        for p in range(pairs):
            lanes = pl.ds(pl.multiple_of((step * pairs + p) * 128, 128), 128)
            dctx = lane_masks(dctx_ref[0, :, lanes])
            value = v_ref[0, :size, lanes]
            loaded.append((lanes, dctx, [mm(value, dctx[i], NT) for i in range(2)]))
        made = []
        for p, (lanes, dctx, dprobs) in enumerate(loaded):
            grads, probs = [], []
            for i in range(2):
                h = 2 * (step * pairs + p) + i
                kept = probs_ref[0, h, :size, :]
                prob = wide(kept)
                inner = jnp.sum(prob * dprobs[i], axis=0, keepdims=True)
                inner = inner / jnp.sum(prob, axis=0, keepdims=True)
                grad = low(prob * (dprobs[i] - inner))
                for lane in range(queries // 128):
                    bias_sum[lane, h, :size, :] += wide(grad[:, 128 * lane : 128 * lane + 128])
                grads.append(grad)
                probs.append(kept)
            made.append((lanes, dctx, grads, probs))
        for p, (lanes, dctx, grads, probs) in enumerate(made):
            query = lane_masks(q_ref[0, :, lanes])
            key = k_ref[0, :size, lanes].T
            for i in range(2):
                h = 2 * (step * pairs + p) + i
                turned[pl.ds(pl.multiple_of(HD * h, HD), HD), :] = (
                    mm(key[HD * i : HD * i + HD], grads[i]) * HD**-0.5
                )
            dv_ref[0, :size, lanes] = low(
                mm(jnp.concatenate(probs, axis=1), jnp.concatenate(dctx, axis=0))
            )
            dk_ref[0, :size, lanes] = low(
                mm(jnp.concatenate(grads, axis=1), jnp.concatenate(query, axis=0))
            )
        return carry

    blocks = lax.div(length + 127, 128)
    for w in range(1, keys // 128 + 1):

        @pl.when(blocks == w)
        def _():
            size, pairs = 128 * w, GROUPS[w - 1]
            lax.fori_loop(0, H // 2 // pairs, partial(group_step, size, pairs), 0)
            if size < keys:
                dk_ref[0, size:, :] = jnp.zeros((keys - size, D), BF16)
                dv_ref[0, size:, :] = jnp.zeros((keys - size, D), BF16)
            dvec_ref[1:2, :] += column_sum(wide(dv_ref[0, :size, :]))

    dquery = low(turned[...].T)
    dq_ref[0] = dquery
    dvec_ref[0:1, :] += column_sum(wide(dquery))

    @pl.when(row == pl.num_programs(0) - 1)
    def _():
        ends_ref[...] = jnp.zeros_like(ends_ref)

        def collect(h, carry):
            below = above = jnp.zeros((1, queries), F32)
            for part in range(stride):
                block = jnp.concatenate(
                    [
                        bias_sum[lane, h, pl.ds(part, queries, stride=stride), :]
                        for lane in range(queries // 128)
                    ],
                    axis=1,
                )
                col = lax.broadcasted_iota(jnp.int32, block.shape, 1)
                line = lax.broadcasted_iota(jnp.int32, block.shape, 0)
                place = stride * (line - col) + part
                zero = jnp.zeros_like(block)
                below = below + column_sum(jnp.where(place <= -(NB // 2), block, zero))
                above = above + column_sum(jnp.where(place >= NB // 2 - 1, block, zero))
                inside = jnp.where((place > -(NB // 2)) & (place < NB // 2 - 1), block, zero)
                partial_sum = inside[:8]
                for a in range(1, queries // 8):
                    partial_sum = partial_sum + pltpu.roll(inside[8 * a : 8 * a + 8], queries - 8 * a, 1)
                sub = lax.broadcasted_iota(jnp.int32, partial_sum.shape, 0)
                lined = jnp.where(sub == 0, partial_sum, 0.0)
                for b in range(1, 8):
                    lined = lined + jnp.where(sub == b, pltpu.roll(partial_sum, queries - b, 1), 0.0)
                diag_ref[h, part] = jnp.broadcast_to(column_sum(lined), (8, queries))
            ends_ref[h, 0] = jnp.broadcast_to(below, (8, queries))
            ends_ref[h, 1] = jnp.broadcast_to(above, (8, queries))
            return carry

        lax.fori_loop(0, H, collect, 0)


def retrace(stride, index, lengths, q, k, v, dctx, probs, base, count, before=()):
    rows, keys, _ = k.shape
    queries = q.shape[1]
    blk = lambda *shape: pl.BlockSpec((1,) + shape, lambda r, *_: (r + base,) + (0,) * len(shape))
    full = lambda *shape: pl.BlockSpec(shape, lambda r, *_: (0,) * len(shape))
    sds = jax.ShapeDtypeStruct
    return pl.pallas_call(
        partial(retrace_kernel, stride, base),
        grid_spec=pltpu.PrefetchScalarGridSpec(
            num_scalar_prefetch=2,
            grid=(count,),
            in_specs=[
                blk(queries, D),
                blk(keys, D),
                blk(keys, D),
                blk(queries, D),
                blk(H, keys, queries),
            ]
            + [ANY] * len(before),
            out_specs=[
                blk(queries, D),
                blk(keys, D),
                blk(keys, D),
                full(8, D),
                full(H, stride, 8, queries),
                full(H, 2, 8, queries),
            ],
            scratch_shapes=[
                pltpu.VMEM((queries // 128, H, keys, 128), F32),
                pltpu.VMEM((D, queries), F32),
            ],
        ),
        out_shape=[
            sds((rows, queries, D), BF16),
            sds((rows, keys, D), BF16),
            sds((rows, keys, D), BF16),
            sds((8, D), F32),
            sds((H, stride, 8, queries), F32),
            sds((H, 2, 8, queries), F32),
        ],
        input_output_aliases={7 + i: i for i in range(len(before))},
        compiler_params=pltpu.CompilerParams(vmem_limit_bytes=VMEM_LIMIT),
        cost_estimate=pl.CostEstimate(
            flops=count * keys * queries * D * 10, bytes_accessed=20_000_000, transcendentals=count * H * keys * queries
        ),
        name="retrace",
    )(lengths, index, q, k, v, dctx, probs, *before)


def table_grad(stride, diag, ends):
    queries = diag.shape[-1]
    columns = []
    for bucket in range(NB):
        place = bucket - NB // 2
        if bucket == 0:
            columns.append(jnp.sum(ends[:, 0, 0], axis=-1))
        elif bucket == NB - 1:
            columns.append(jnp.sum(ends[:, 1, 0], axis=-1))
        else:
            part = place % stride
            columns.append(diag[:, part, 0, ((part - place) // stride) % queries])
    return jnp.stack(columns, axis=1).reshape(-1)


def inputs_kernel(stride, base, count, len_ref, me_ref, dq_ref, dk_ref, dv_ref, du_ref, *refs):
    sources = refs[:count]
    out_ref, entry, sem = refs[-3:]
    row = pl.program_id(0)
    keys = dk_ref.shape[1]
    queries = dq_ref.shape[1]

    @pl.when(row == 0)
    def _():
        start_load(me_ref[0], sources, entry, sem.at[0], place_entry)
        wait_load(entry, sem.at[0])

    total = mm(dq_ref[0], entry[0], NT) + du_ref[0]
    if stride == 1:
        out_ref[0] = total + mm(dk_ref[0], entry[1], NT) + mm(dv_ref[0], entry[2], NT)
        return
    total = 0.5 * total
    upper = low(total)
    lower = low(total - wide(upper))
    for block in range(keys // 256):
        rows = pl.ds(block * 256, 256)
        place = lax.broadcasted_iota(jnp.int32, (256, queries), 0) + 256 * block
        mine = lax.broadcasted_iota(jnp.int32, (256, queries), 1)
        pair = jnp.where(lax.shift_right_logical(place, 1) == mine, 1.0, 0.0).astype(BF16)
        spread = mm(pair, upper) + mm(pair, lower)

        @pl.when(block * 256 < len_ref[row + base])
        def _():
            out_ref[0, rows, :] = (
                spread + mm(dk_ref[0, rows, :], entry[1], NT) + mm(dv_ref[0, rows, :], entry[2], NT)
            )

        @pl.when(block * 256 >= len_ref[row + base])
        def _():
            out_ref[0, rows, :] = spread


def input_grads(stride, index, lengths, dq, dk, dv, du, sources, base, count, before=()):
    rows, keys, _ = dk.shape
    queries = dq.shape[1]
    blk = lambda *shape: pl.BlockSpec((1,) + shape, lambda r, *_: (r + base,) + (0,) * len(shape))
    return pl.pallas_call(
        partial(inputs_kernel, stride, base, len(sources)),
        grid_spec=pltpu.PrefetchScalarGridSpec(
            num_scalar_prefetch=2,
            grid=(count,),
            in_specs=[blk(queries, D), blk(keys, D), blk(keys, D), blk(queries, D)] + [ANY] * (len(sources) + len(before)),
            out_specs=blk(keys, D),
            scratch_shapes=[pltpu.VMEM((3, D, D), BF16), pltpu.SemaphoreType.DMA((1,))],
        ),
        out_shape=jax.ShapeDtypeStruct((rows, keys, D), F32),
        input_output_aliases={6 + len(sources) + i: i for i in range(len(before))},
        compiler_params=pltpu.CompilerParams(vmem_limit_bytes=VMEM_LIMIT),
        cost_estimate=pl.CostEstimate(
            flops=2 * count * (queries + keys) * D * D, bytes_accessed=20_000_000, transcendentals=0
        ),
        name="input_grads",
    )(lengths, index, dq, dk, dv, du, *sources, *before)


def vectors_by_unit(dvec, dbias, dtable):
    flat = vector_units(dvec, dbias, dtable, 32)
    return jnp.pad(low(flat), ((0, 0), (0, 16 * HALF - flat.shape[1]))).reshape(UNITS, 2, 16, HALF)


NARROW_CUTS = ((192, 96), (48, 24))
WIDEN_CUTS = ((48, 24),) * 4
FEED_CUTS = NARROW_CUTS + WIDEN_CUTS
ENTRY_CUTS = ((48, 24),) * 3


def join(left, right):
    return jnp.concatenate([left, right], axis=-1)


def feed_shards(left, right):
    widen = jnp.concatenate([left[120:216].reshape(4, 24, HALF), right[120:216].reshape(4, 24, HALF)])
    return (
        join(left[96:120], right[96:120]),
        widen.transpose(1, 0, 2).reshape(24, FF),
        join(left[:96], right[:96]),
    )


def entry_shards(left, right):
    return join(left, right).reshape(3, 24, D)


def absolute_units(pair):
    send, keep = pair
    merged = jnp.stack([keep, send], axis=2)
    rest = merged.shape[1:]
    merged = merged.reshape((4, 4) + rest).transpose(1, 0, 2, 3, 4)
    return wide(merged.reshape((UNITS,) + rest))


def plain_shards(feed, entry):
    feed, entry = absolute_units(feed), absolute_units(entry)
    narrow = feed[:, :192].reshape(FF, D)
    leave = feed[:, 192:240].reshape(D, D)
    widen = feed[:, 240:432].reshape(UNITS, 4, 48, 2, HALF).transpose(0, 2, 3, 1, 4).reshape(D, FF)
    vectors = entry[:, 144:].transpose(0, 2, 1, 3).reshape(32, -1)
    entry = entry[:, :144].reshape(UNITS, 3, 48, D).transpose(1, 0, 2, 3).reshape(3, D, D)
    scatter = lambda value, dim: lax.psum_scatter(value, AX, scatter_dimension=dim, tiled=True)
    rows = vectors.shape[0]
    cut, mid = 8 * D // rows, 8 * D // rows + FF // rows
    last = mid + H * NB // rows
    vec = vectors[:, :cut].reshape(rows, 8, -1).transpose(1, 0, 2).reshape(8, D)
    return (
        scatter(entry, 1),
        scatter(leave, 0),
        scatter(widen, 0),
        scatter(narrow, 0),
        scatter(vec, 1),
        scatter(vectors[:, cut:mid].reshape(-1), 0),
        scatter(vectors[:, mid:last].reshape(-1), 0),
    )


def plain_gather(entry, leave, widen, narrow):
    gather = lambda value, dim: lax.all_gather(value, AX, axis=dim, tiled=True)
    widen = gather(widen, 0).reshape(D, 4, D).transpose(1, 0, 2)
    return (
        (gather(entry, 1),),
        (gather(leave, 0),),
        (widen,),
        (gather(narrow, 0).reshape(64, 48, D),),
    )


def plain_vectors(*small):
    gather = lambda value, dim: lax.all_gather(value, AX, axis=dim, tiled=True)
    parts = []
    for value in small:
        full = gather(value, value.ndim - 1)
        if value.ndim == 2:
            parts.append(full.reshape(8, 32, 24).transpose(1, 0, 2))
        else:
            parts.append(full.reshape(32, -1))
    slabs = vector_slab(*parts).reshape(4, 4, 2, 16, 128).transpose(2, 1, 0, 3, 4)
    return slabs[0].reshape(UNITS, 16, 128), slabs[1].reshape(UNITS, 16, 128)


def on_device(
    devices,
    hidden,
    lengths,
    cotangent,
    inflow,
    outflow,
    widener,
    narrower,
    shifts,
    offsets,
    distance,
    intake,
    outtake,
    expander,
    squeezer,
    adjusts,
    leanings,
    spacing,
):
    rows, seq, width = hidden.shape
    half = seq // 2
    fast = devices == 32
    index = lax.axis_index(AX)
    core = index % 2
    halved = (lengths + 1) // 2
    layer_one = (inflow, outflow, widener, narrower)
    layer_two = (intake, outtake, expander, squeezer)

    small = (shifts, offsets, distance, adjusts, leanings, spacing)
    if fast:
        ticks = Ticks(index.astype(jnp.int32).reshape(1))
        tick = ticks.run
        vec = Job(vector_stages, vector_slab(*small))
        eo1, w1 = gather_jobs(core, True, *layer_one)
        eo2, w2 = gather_jobs(core, False, *layer_two)
        tick([eo1, vec, w1])
        tick([eo1, vec, w1])
        tick([eo1, vec, w1])
        prepared = tick([eo1], lambda me: prepare(me, *vec.result, seq, half))
        tick([eo1, eo2, w2])
    else:
        ticks = Ticks(jnp.zeros((1,), jnp.int32))
        eo1 = w1 = eo2 = w2 = None
        plain_one, plain_two = plain_gather(*layer_one), plain_gather(*layer_two)
        prepared = prepare(ticks.me, *plain_vectors(*small), seq, half)

        def tick(jobs, kernel=None):
            return ticks.run([], kernel)

    def weights(layer, names):
        if fast:
            jobs = {"e": (eo1, eo2), "o": (eo1, eo2), "w": (w1, w2), "n": (w1, w2)}
            return [jobs[name][layer].result for name in names]
        return [(plain_one, plain_two)[layer]["eown".index(name)] for name in names]

    vec1, bias1, tab1, vec2, bias2, tab2 = prepared
    flatten = lambda value: value.reshape(-1, D)
    part = rows // 2

    def begin(stride, me, lens, x, vec_in, layer, tab):
        made = project(stride, me, lens, x, vec_in, *weights(layer, "e"))
        q, k, v = made[-3:]
        return made, attend(stride, me, lens, q, k, v, tab, 0, part)

    def finish(stride, me, lens, made, tab, head):
        return attend(stride, me, lens, *made[-3:], tab, part, rows - part, head)

    made1, head = tick([w1, eo2, w2], lambda me: begin(2, me, lengths, hidden, vec1, 0, tab1))
    ctx1, probs1 = tick([w1, eo2], lambda me: finish(2, me, lengths, made1, tab1, head))
    pooled, pooled_low, q1, k1, v1 = made1
    tick([w1])
    u1, act1, slope1, before1, first_out = tick(
        [eo2, w2],
        lambda me: expand(me, flatten(ctx1), flatten(pooled), vec1, bias1, *weights(0, "own")),
    )
    pooled_layer = first_out.reshape(rows, half, width)

    tick([eo2])
    tick([eo2])
    made2, head = tick([w2], lambda me: begin(1, me, halved, pooled_layer, vec2, 1, tab2))
    ctx2, probs2 = tick([w2], lambda me: finish(1, me, halved, made2, tab2, head))
    q2, k2, v2 = made2
    tick([w2])
    u2, act2, slope2, before2, second_out = tick(
        [], lambda me: expand(me, flatten(ctx2), first_out, vec2, bias2, *weights(1, "own"))
    )

    def reducing(pair, cuts):
        return Job(reduce_stages, core, cuts, *pair) if fast else pair

    dback, mixed_low, dhid, dattn, du, dctx, dvec, dbias = tick(
        [],
        lambda me: contract(me, cotangent.reshape(-1, D), before2, slope2, u2, vec2, *weights(1, "own")),
    )

    narrow2 = tick([], lambda me: narrow_grad(240, me, act2, dback, flatten(ctx2), dattn))
    sumn2 = reducing(narrow2, NARROW_CUTS)
    widen2 = tick([sumn2], lambda me: widen_grad(192, me, mixed_low, dhid, ()))
    sumw2 = reducing(widen2, WIDEN_CUTS)
    back = tick(
        [sumn2, sumw2],
        lambda me: retrace(1, me, halved, q2, k2, v2, dctx.reshape(q2.shape), probs2, 0, rows),
    )
    dq, dk, dv, dvec_top, diag, ends = back
    packed = vectors_by_unit(dvec + dvec_top, dbias, table_grad(1, diag, ends))

    def entry_end(me):
        made = entry_grad(160, 0, me, halved, pooled_layer, pooled_layer, dq, dk, dv, packed, ())
        parts = (dq, dk, dv, du.reshape(q2.shape), *weights(1, "e"))
        return made, input_grads(1, me, halved, *parts, 0, rows)

    entry2, dlayer = tick([sumn2, sumw2], entry_end)
    sume2 = reducing(entry2, ENTRY_CUTS)

    dback, mixed_low, dhid, dattn, du, dctx, dvec, dbias = tick(
        [sumw2, sumn2, sume2],
        lambda me: contract(me, flatten(dlayer), before1, slope1, u1, vec1, *weights(0, "own")),
    )
    narrow1 = tick(
        [sumw2, sumn2, sume2], lambda me: narrow_grad(240, me, act1, dback, flatten(ctx1), dattn)
    )
    sumn1 = reducing(narrow1, NARROW_CUTS)
    widen1 = tick([sumn1, sumw2, sume2], lambda me: widen_grad(192, me, mixed_low, dhid, ()))
    sumw1 = reducing(widen1, WIDEN_CUTS)
    parts = (q1, k1, v1, dctx.reshape(q1.shape), probs1)
    head = tick([sumn1, sumw1, sume2, sumn2], lambda me: retrace(2, me, lengths, *parts, 0, part))
    back = tick(
        [sumn1, sumw1, sume2], lambda me: retrace(2, me, lengths, *parts, part, rows - part, head[:3])
    )
    dq, dk, dv = back[:3]
    dvec_top, diag, ends = [one + two for one, two in zip(head[3:], back[3:])]
    packed = vectors_by_unit(dvec + dvec_top, dbias, table_grad(2, diag, ends))
    entry1 = tick(
        [sumw1, sumn1, sumw2],
        lambda me: entry_grad(160, 0, me, lengths, pooled_low, hidden, dq, dk, dv, packed, ()),
    )
    sume1 = reducing(entry1, ENTRY_CUTS)
    parts = (dq, dk, dv, du.reshape(q1.shape), *weights(0, "e"))
    head = tick(
        [sume1, sumw1, sumn1, sume2], lambda me: input_grads(2, me, lengths, *parts, 0, part)
    )
    hidden_grad = tick(
        [sume1, sumw1, sumn1],
        lambda me: input_grads(2, me, lengths, *parts, part, rows - part, (head,)),
    )
    if fast:
        for job in (sume1, sumw1, sumn1, sumn2, sumw2, sume2):
            while job.result is None:
                tick([job, sumw1] if job is sume1 else [job])
        left, right, rest = sume2.result
        feed = [jnp.concatenate(sides) for sides in zip(sumn2.result[:2], sumw2.result[:2])]
        shards_two = (entry_shards(left, right),) + feed_shards(*feed)
        shards_two = shards_two + split_vectors(rest.reshape(-1), 32)
        left, right, rest = sume1.result
        feed = [jnp.concatenate(sides) for sides in zip(sumn1.result[:2], sumw1.result[:2])]
        shards_one = (entry_shards(left, right),) + feed_shards(*feed)
        shards_one = shards_one + split_vectors(rest.reshape(-1), 32)
    else:
        feed2 = [jnp.concatenate(sides, axis=1) for sides in zip(narrow2, widen2)]
        feed1 = [jnp.concatenate(sides, axis=1) for sides in zip(narrow1, widen1)]
        shards_one, shards_two = plain_shards(feed1, entry1), plain_shards(feed2, entry2)
    return (
        pooled_layer,
        second_out.reshape(rows, half, width),
        hidden_grad,
        *shards_one,
        *shards_two[:4],
        shards_two[4][1:],
        shards_two[5],
        shards_two[6],
        shards_two[4][0],
    )


def solution(mesh):
    both = ("wide", "narrow")
    rows = P(both, None, None)
    weights = (
        P(None, both, None),
        P(both, None),
        P(both, None),
        P(both, None),
        P(None, both),
        P(both),
        P(both),
    )
    return jax.shard_map(
        partial(on_device, mesh.size),
        mesh=mesh,
        in_specs=(rows, P(both), rows) + weights + weights,
        out_specs=(rows, rows, rows) + weights + weights + (P(both),),
        check_vma=False,
    )
```

```python
from functools import partial

import jax
import jax.numpy as jnp
from jax import lax
from jax.experimental import pallas as pl
from jax.experimental.pallas import tpu as pltpu
from jax.sharding import PartitionSpec as P

H = 12
HD = 64
NB = 32
D = 768
FF = 3072
HALF = 384
EPS = 1e-06
AX = ("wide", "narrow")
CORE, XBIT, YBIT, Z0, Z1 = 1, 2, 4, 8, 16
UNITS = 16
F32 = jnp.float32
BF16 = jnp.bfloat16
GELU_A = 0.7978845608028654
GELU_B = 0.044715
NN = (((1,), (0,)), ((), ()))
NT = (((1,), (1,)), ((), ()))
TN = (((0,), (0,)), ((), ()))
GROUPS = (6, 3, 2, 2)
TILE_A = 256
TILE_B = 256
VMEM_LIMIT = 60 * 1024 * 1024
ANY = pl.BlockSpec(memory_space=pl.ANY)


def mm(left, right, dims=NN):
    return lax.dot_general(left, right, dims, preferred_element_type=F32)


def wide(value):
    return value.astype(F32)


def low(value):
    return value.astype(BF16)


SENT = []


def swap(value, mask):
    SENT.append(value)
    return lax.ppermute(value, AX, [(i, i ^ mask) for i in range(32)])


def pick(core, first, second):
    return jnp.where(core == 0, first, second)


class Job:
    def __init__(self, stages, *operands):
        self.stages = stages(*operands)
        self.operands = next(self.stages)
        self.result = None

    def step(self, operands):
        try:
            self.operands = self.stages.send(operands)
        except StopIteration as stop:
            self.result = stop.value
            self.operands = ()


class Ticks:
    def __init__(self, me):
        self.me = me
        self.last = ()
        self.flying = []

    def run(self, jobs, kernel=None):
        jobs = [job for job in jobs if job.result is None]
        tied = jobs + [job for job in self.flying if job not in jobs]
        operands = [job.operands if job.result is None else job.result for job in tied]
        self.me, operands, self.last = lax.optimization_barrier((self.me, operands, self.last))
        SENT.clear()
        for job, value in zip(tied, operands):
            if job in jobs:
                job.step(value)
            elif job.result is None:
                job.operands = value
            else:
                job.result = value
        self.flying = jobs
        if kernel is None:
            return None
        self.me = lax.optimization_barrier((self.me, list(SENT)))[0]
        out = kernel(self.me)
        self.last = jax.tree.leaves(out)[-1]
        return out


def gather_stages(pair, direct, keep, send):
    keep, send = yield keep, send
    core = lax.axis_index(AX) % 2
    recv = swap(send, CORE)
    slab = pair(pick(core, keep, recv), pick(core, recv, keep))
    slab = yield slab
    if direct:
        own = jnp.stack([slab, swap(slab, Z0), swap(slab, Z1), swap(slab, Z0 | Z1)])
    else:
        two = jnp.stack([slab, swap(slab, Z0)])
        two = yield two
        own = jnp.concatenate([two, swap(two, Z1)])
    own = yield own
    across_y = swap(own, YBIT)
    across_x = swap(own, XBIT)
    far = (swap(own, CORE),)
    own, across_y, across_x, far = yield own, across_y, across_x, far
    diag = (swap(across_y[:2], XBIT), swap(across_x[2:], YBIT))
    far = far + (swap(across_x, CORE), swap(across_y, CORE))
    mine, far = yield (own, across_x, across_y) + diag, far
    return mine + far + tuple(swap(piece, CORE) for piece in mine[3:])


def vector_stages(slab):
    slab = yield slab
    own = jnp.stack([slab, swap(slab, Z0), swap(slab, Z1), swap(slab, Z0 | Z1)])
    own = yield own
    across = [own, swap(own, XBIT), swap(own, YBIT), swap(own, XBIT | YBIT)]
    across = yield across
    near = jnp.concatenate(across)
    return near, swap(near, CORE)


def pair_entry(first, second):
    return jnp.concatenate([first.reshape(4, 24, HALF), second.reshape(4, 24, HALF)], axis=1)


def pair_wide(first, second):
    widen = jnp.concatenate([first[:96].reshape(4, 24, HALF), second[:96].reshape(4, 24, HALF)], axis=1)
    widen = widen.reshape(2, 2, 48, HALF).transpose(0, 2, 1, 3).reshape(2, 48, D)
    narrow = jnp.concatenate([first[96:].reshape(2, 48, HALF), second[96:].reshape(2, 48, HALF)], axis=2)
    return jnp.concatenate([widen, narrow], axis=0)


def gather_jobs(core, direct, entry, leave, widen, narrow):
    def halved(value):
        return pick(core, value[0], value[1]), pick(core, value[1], value[0])

    eo = jnp.concatenate([entry, leave[None]]).reshape(96, 2, HALF).transpose(1, 0, 2)
    widen = widen.reshape(24, 2, 4, HALF).transpose(1, 2, 0, 3).reshape(2, 96, HALF)
    narrow = narrow.reshape(96, 2, HALF).transpose(1, 0, 2)
    both = jnp.concatenate([widen, narrow], axis=1)
    return (
        Job(gather_stages, pair_entry, direct, *halved(eo)),
        Job(gather_stages, pair_wide, False, *halved(both)),
    )


def reduce_stages(core, cuts, direct, send, keep):
    shape = (4, 4) + keep.shape[1:]
    send, keep = yield send, keep
    keep = keep.reshape(shape)
    recv = swap(send, CORE).reshape(shape)
    keep, recv = yield keep, recv
    diag_low = swap(low(wide(keep[3, :2]) + wide(recv[3, :2])), XBIT)
    diag_high = swap(low(wide(keep[3, 2:]) + wide(recv[3, 2:])), YBIT)
    keep, recv, diag_low, diag_high = yield keep, recv, diag_low, diag_high
    to_y = wide(keep[2]) + wide(recv[2])
    to_x = wide(keep[1]) + wide(recv[1])
    rest = [(0, 0)] * 2
    to_y = low(to_y + jnp.pad(wide(diag_low), [(0, 2)] + rest))
    to_x = low(to_x + jnp.pad(wide(diag_high), [(2, 0)] + rest))
    from_y, from_x = swap(to_y, YBIT), swap(to_x, XBIT)
    keep, recv, from_y, from_x = yield keep, recv, from_y, from_x

    def part(k):
        return (wide(keep[0, k]) + wide(recv[0, k])) + (wide(from_y[k]) + wide(from_x[k]))

    if direct:
        far = tuple(swap(low(part(k)), mask) for k, mask in ((1, Z0), (2, Z1), (3, Z0 | Z1)))
        keep, recv, from_y, from_x, far = yield keep, recv, from_y, from_x, far
        total = part(0) + wide(far[0]) + wide(far[1]) + wide(far[2])
    else:
        far = swap(jnp.stack([low(part(2)), low(part(3))]), Z1)
        keep, recv, from_y, from_x, far = yield keep, recv, from_y, from_x, far
        near = swap(low(part(1) + wide(far[1])), Z0)
        keep, recv, from_y, from_x, far, near = yield keep, recv, from_y, from_x, far, near
        total = part(0) + wide(far[0]) + wide(near)
    keeps, sends = [], []
    start = 0
    for rows, group in cuts:
        slab = total[start : start + rows].reshape(-1, 2, group, HALF)
        start += rows
        keeps.append(pick(core, slab[:, 0], slab[:, 1]).reshape(-1, HALF))
        sends.append(pick(core, slab[:, 1], slab[:, 0]).reshape(-1, HALF))
    rest = total[start:]
    keep, send = jnp.concatenate(keeps), jnp.concatenate(sends)
    recv = swap(send, CORE)
    return pick(core, keep, recv), pick(core, recv, keep), rest


def vector_units(vectors, wide_bias, table, parts):
    flat = jnp.concatenate(
        [
            vectors.reshape(8, parts, -1).transpose(1, 0, 2).reshape(parts, -1),
            wide_bias.reshape(parts, -1),
            table.reshape(parts, -1),
        ],
        axis=1,
    )
    return flat


def split_vectors(flat, parts):
    cut = 8 * D // parts
    mid = cut + FF // parts
    return flat[:cut].reshape(8, -1), flat[cut:mid], flat[mid : mid + H * NB // parts]


def position(chip, unit):
    rel = jnp.bitwise_xor(chip, unit)
    return jnp.bitwise_and(rel, 3) * 4 + lax.shift_right_logical(rel, 2)


def start_load(me, refs, dst, sem, place):
    if len(refs) == 1:
        pltpu.make_async_copy(refs[0], dst, sem).start()
        return
    chip = lax.shift_right_logical(me, 1)
    for side in range(2):
        half = jnp.bitwise_xor(jnp.bitwise_and(me, 1), side)
        own, across_x, across_y, diag_low, diag_high = refs[5 * side : 5 * side + 5]
        for k in range(4):
            for step, ref, at in (
                (0, own, k),
                (1, across_x, k),
                (2, across_y, k),
                (3, diag_low if k < 2 else diag_high, k % 2),
            ):
                unit = jnp.bitwise_xor(chip, 4 * k + step)
                for source, target in place(ref.at[at], dst, unit, half):
                    pltpu.make_async_copy(source, target, sem).start()


def wait_load(dst, sem):
    pltpu.make_async_copy(dst, dst, sem).wait()


def place_entry(src, dst, unit, half):
    rows, cols = pl.multiple_of(unit * 48, 16), pl.multiple_of(half * HALF, 128)
    return [(src.at[0:3], dst.at[:, pl.ds(rows, 48), pl.ds(cols, HALF)])]


def place_leave(src, dst, unit, half):
    rows, cols = pl.multiple_of(unit * 48, 16), pl.multiple_of(half * HALF, 128)
    return [(src.at[3], dst.at[pl.ds(rows, 48), pl.ds(cols, HALF)])]


def place_widen(src, dst, unit, half):
    rows = pl.multiple_of(unit * 48, 16)
    return [(src.at[0:2], dst.at[pl.ds(half * 2, 2), pl.ds(rows, 48), :])]


def place_narrow(src, dst, unit, half):
    cols = pl.multiple_of(half * HALF, 128)
    return [
        (
            src.at[2:4, :, HALF * g : HALF * g + HALF],
            dst.at[pl.ds(unit * 4 + 2 * g, 2), :, pl.ds(cols, HALF)],
        )
        for g in range(2)
    ]


def build_bias(table, bias, stride):
    keys = bias.shape[1]
    for part in range(bias.shape[2] // 128):
        row = lax.broadcasted_iota(jnp.int32, (keys, 128), 0)
        col = lax.broadcasted_iota(jnp.int32, (keys, 128), 1) + 128 * part
        bucket = jnp.clip(row - stride * col, -(NB // 2), NB // 2 - 1) + NB // 2
        for h in range(H):
            values = jnp.broadcast_to(table[h : h + 1, :], (keys, 128))
            bias[h, :, 128 * part : 128 * part + 128] = low(
                jnp.take_along_axis(values, bucket, axis=1, mode="promise_in_bounds")
            )


def prepare_kernel(me_ref, near_ref, far_ref, *refs):
    outs, tables = refs[:6], refs[6:]
    core = jnp.bitwise_and(me_ref[0], 1)
    chip = lax.shift_right_logical(me_ref[0], 1)
    for table in tables:
        table[...] = jnp.zeros_like(table)
    for d in range(32):
        at = position(chip, d // 2)
        slab = jnp.where(core == d % 2, wide(near_ref[at]), wide(far_ref[at]))
        for layer in range(2):
            vec_ref, wide_ref = outs[3 * layer], outs[3 * layer + 1]
            rows = slab[8 * layer : 8 * layer + 8]
            vec_ref[:, 24 * d : 24 * d + 24] = rows[:, :24]
            wide_ref[:, 96 * d : 96 * d + 96] = rows[0:1, 32:128]
            h, start = 12 * d // NB, 12 * d % NB
            count = min(12, NB - start)
            tables[layer][h : h + 1, start : start + count] = rows[1:2, 32 : 32 + count]
            if count < 12:
                tables[layer][h + 1 : h + 2, 0 : 12 - count] = rows[1:2, 32 + count : 44]
    build_bias(tables[0], outs[2], 2)
    build_bias(tables[1], outs[5], 1)


def prepare(index, near, far, keys, queries):
    sds = jax.ShapeDtypeStruct
    shapes = []
    for length in (keys, queries):
        shapes += [sds((8, D), F32), sds((1, FF), F32), sds((H, length, queries), BF16)]
    return pl.pallas_call(
        prepare_kernel,
        grid_spec=pltpu.PrefetchScalarGridSpec(
            num_scalar_prefetch=1,
            grid=(1,),
            in_specs=[whole(UNITS, 16, 128)] * 2,
            out_specs=[whole(*shape.shape) for shape in shapes],
            scratch_shapes=[pltpu.VMEM((16, 128), F32)] * 2,
        ),
        out_shape=shapes,
        compiler_params=pltpu.CompilerParams(vmem_limit_bytes=VMEM_LIMIT),
        cost_estimate=pl.CostEstimate(flops=10_000_000, bytes_accessed=10_000_000, transcendentals=0),
        name="prepare",
    )(index, near, far)


def vector_slab(vectors_one, wide_one, table_one, vectors_two, wide_two, table_two):
    lead = wide_one.shape[:-1]
    left = jnp.concatenate([vectors_one, vectors_two], axis=-2)
    left = jnp.pad(left, [(0, 0)] * (left.ndim - 1) + [(0, 8)])
    rows = []
    for wide_bias, table in ((wide_one, table_one), (wide_two, table_two)):
        table = jnp.pad(table, [(0, 0)] * len(lead) + [(0, 84)])
        pair = jnp.stack([wide_bias, table], axis=-2)
        rows.append(jnp.pad(pair, [(0, 0)] * len(lead) + [(0, 6), (0, 0)]))
    return jnp.concatenate([left, jnp.concatenate(rows, axis=-2)], axis=-1)


def whole(*shape):
    return pl.BlockSpec(shape, lambda r, *_: (0,) * len(shape))


def lane_masks(value):
    lane = lax.broadcasted_iota(jnp.int32, value.shape, 1)
    zero = jnp.zeros_like(value)
    return jnp.where(lane < HD, value, zero), jnp.where(lane < HD, zero, value)


def masked_scores(keys, query, bias, count):
    scores = mm(keys, query, NT) + wide(bias)
    size = scores.shape[0]
    head, tail = scores[: size - 128], scores[size - 128 :]
    row = lax.broadcasted_iota(jnp.int32, tail.shape, 0) + (size - 128)
    tail = jnp.where(row < count, tail, -1e30)
    return tail if size == 128 else jnp.concatenate([head, tail], axis=0)


def statistics(value):
    mean = jnp.mean(value, axis=-1, keepdims=True)
    centred = value - mean
    spread = jnp.mean(centred * centred, axis=-1, keepdims=True)
    rstd = lax.rsqrt(spread + EPS)
    return centred * rstd, rstd


def norm_pull(grad, unit, rstd):
    return rstd * (
        grad
        - jnp.mean(grad, axis=-1, keepdims=True)
        - unit * jnp.mean(grad * unit, axis=-1, keepdims=True)
    )


def column_sum(value):
    return jnp.sum(value, axis=0, keepdims=True)


def project_kernel(stride, count, len_ref, me_ref, x_ref, vec_ref, *refs):
    sources = refs[:count]
    refs = refs[count:]
    if stride == 2:
        pooled_ref, pooled_low_ref, *refs = refs
    q_ref, k_ref, v_ref, entry, sem = refs
    row = pl.program_id(0)
    keys = x_ref.shape[1]
    queries = q_ref.shape[1]

    @pl.when(row == 0)
    def _():
        start_load(me_ref[0], sources, entry, sem.at[0], place_entry)
        wait_load(entry, sem.at[0])

    length = len_ref[row]
    if stride == 2:
        place = lax.broadcasted_iota(jnp.int32, (queries, keys), 1)
        mine = lax.broadcasted_iota(jnp.int32, (queries, keys), 0)
        pair = jnp.where(lax.shift_right_logical(place, 1) == mine, 0.5, 0.0).astype(BF16)
        pooled = mm(pair, x_ref[0])
        pooled_ref[0] = pooled
        query_in = low(pooled)
        pooled_low_ref[0] = query_in
    else:
        query_in = x_ref[0]
    q_ref[0] = low(wide(low(mm(query_in, entry[0]) + vec_ref[0:1, :])) * HD**-0.5)
    for block in range(keys // 256):

        @pl.when(block * 256 < length)
        def _():
            rows = pl.ds(block * 256, 256)
            x = x_ref[0, rows, :]
            k_ref[0, rows, :] = low(mm(x, entry[1]))
            v_ref[0, rows, :] = low(mm(x, entry[2]) + vec_ref[1:2, :])


def project(stride, index, lengths, x, vectors, sources):
    rows, keys, _ = x.shape
    queries = keys // stride
    blk = lambda *shape: pl.BlockSpec((1,) + shape, lambda r, *_: (r,) + (0,) * len(shape))
    full = lambda *shape: pl.BlockSpec(shape, lambda r, *_: (0,) * len(shape))
    sds = jax.ShapeDtypeStruct
    outs = [
        (sds((rows, queries, D), BF16), blk(queries, D)),
        (sds((rows, keys, D), BF16), blk(keys, D)),
        (sds((rows, keys, D), BF16), blk(keys, D)),
    ]
    if stride == 2:
        outs = [
            (sds((rows, queries, D), F32), blk(queries, D)),
            (sds((rows, queries, D), BF16), blk(queries, D)),
        ] + outs
    return pl.pallas_call(
        partial(project_kernel, stride, len(sources)),
        grid_spec=pltpu.PrefetchScalarGridSpec(
            num_scalar_prefetch=2,
            grid=(rows,),
            in_specs=[blk(keys, D), full(8, D)] + [ANY] * len(sources),
            out_specs=[o[1] for o in outs],
            scratch_shapes=[pltpu.VMEM((3, D, D), BF16), pltpu.SemaphoreType.DMA((1,))],
        ),
        out_shape=[o[0] for o in outs],
        compiler_params=pltpu.CompilerParams(vmem_limit_bytes=VMEM_LIMIT),
        cost_estimate=pl.CostEstimate(
            flops=rows * keys * D * D * 4, bytes_accessed=20_000_000, transcendentals=0
        ),
        name="project",
    )(lengths, index, x, vectors, *sources)


def attend_kernel(base, len_ref, me_ref, q_ref, k_ref, v_ref, bias, *refs):
    ctx_ref, probs_ref, turned = refs[-3:]
    row = pl.program_id(0)
    keys = k_ref.shape[1]
    length = len_ref[row + base]

    def group_step(size, pairs, step, carry):
        made = []
        for p in range(pairs):
            lanes = pl.ds(pl.multiple_of((step * pairs + p) * 128, 128), 128)
            queries_low = lane_masks(q_ref[0, :, lanes])
            key = k_ref[0, :size, lanes]
            value = v_ref[0, :size, lanes].T
            for i in range(2):
                h = 2 * (step * pairs + p) + i
                scores = masked_scores(key, queries_low[i], bias[h, :size, :], length)
                made.append((h, scores, value[HD * i : HD * i + HD]))
        kept = []
        for h, scores, value in made:
            top = jnp.max(scores, axis=0, keepdims=True)
            probs = jnp.exp(scores - top)
            probs = low(probs * (1.0 / jnp.sum(probs, axis=0, keepdims=True)))
            probs_ref[0, h, :size, :] = probs
            kept.append((h, probs, value))
        for h, probs, value in kept:
            turned[pl.ds(pl.multiple_of(HD * h, HD), HD), :] = mm(value, probs)
        return carry

    blocks = lax.div(length + 127, 128)
    for w in range(1, keys // 128 + 1):

        @pl.when(blocks == w)
        def _():
            pairs = GROUPS[w - 1]
            lax.fori_loop(0, H // 2 // pairs, partial(group_step, 128 * w, pairs), 0)

    ctx_ref[0] = low(turned[...].T)


def attend(stride, index, lengths, q, k, v, table, base, count, before=()):
    rows, keys, _ = k.shape
    queries = keys // stride
    blk = lambda *shape: pl.BlockSpec((1,) + shape, lambda r, *_: (r + base,) + (0,) * len(shape))
    full = lambda *shape: pl.BlockSpec(shape, lambda r, *_: (0,) * len(shape))
    sds = jax.ShapeDtypeStruct
    return pl.pallas_call(
        partial(attend_kernel, base),
        grid_spec=pltpu.PrefetchScalarGridSpec(
            num_scalar_prefetch=2,
            grid=(count,),
            in_specs=[blk(queries, D), blk(keys, D), blk(keys, D), full(H, keys, queries)]
            + [ANY] * len(before),
            out_specs=[blk(queries, D), blk(H, keys, queries)],
            scratch_shapes=[pltpu.VMEM((D, queries), F32)],
        ),
        out_shape=[sds((rows, queries, D), BF16), sds((rows, H, keys, queries), BF16)],
        input_output_aliases={6 + i: i for i in range(len(before))},
        compiler_params=pltpu.CompilerParams(vmem_limit_bytes=VMEM_LIMIT),
        cost_estimate=pl.CostEstimate(
            flops=count * keys * queries * D * 8,
            bytes_accessed=20_000_000,
            transcendentals=count * H * keys * queries,
        ),
        name="attend",
    )(lengths, index, q, k, v, table, *before)


def expand_kernel(counts, me_ref, ctx_ref, resid_ref, vec_ref, bias_ref, *refs):
    c1, c2, c3 = counts
    leave_src, widen_src, narrow_src = refs[:c1], refs[c1 : c1 + c2], refs[c1 + c2 : c1 + c2 + c3]
    u_ref, act_ref, slope_ref, before_ref, out_ref, leave, widen, narrow, sem = refs[c1 + c2 + c3 :]
    first = pl.program_id(0) == 0

    @pl.when(first)
    def _():
        start_load(me_ref[0], leave_src, leave, sem.at[0], place_leave)
        start_load(me_ref[0], widen_src, widen, sem.at[1], place_widen)
        start_load(me_ref[0], narrow_src, narrow, sem.at[2], place_narrow)
        wait_load(leave, sem.at[0])

    u = wide(resid_ref[...]) + mm(ctx_ref[...], leave[...]) + vec_ref[2:3, :]
    u_ref[...] = u
    unit, _ = statistics(u)
    mixed = unit * vec_ref[3:4, :] + vec_ref[4:5, :]
    mixed_low = low(mixed)

    @pl.when(first)
    def _():
        wait_load(widen, sem.at[1])
        wait_load(narrow, sem.at[2])

    total = mixed + vec_ref[5:6, :]
    for j in range(4):
        cols = slice(D * j, D * j + D)
        h = mm(mixed_low, widen[j]) + bias_ref[0:1, cols]
        square = h * h
        gate = 0.5 + 0.5 * jnp.tanh(h * (GELU_A + GELU_A * GELU_B * square))
        act = h * gate
        slope = gate + act * (1.0 - gate) * (2.0 * GELU_A + 6.0 * GELU_A * GELU_B * square)
        slope_ref[:, cols] = low(slope)
        act = low(act)
        act_ref[:, cols] = act
        total = total + mm(act, narrow[16 * j : 16 * j + 16].reshape(D, D))
    before_ref[...] = total
    unit, _ = statistics(total)
    out_ref[...] = low(unit * vec_ref[6:7, :] + vec_ref[7:8, :])


def expand(index, ctx, resid, vectors, wide_bias, leave, widen, narrow):
    tokens = ctx.shape[0]
    tile = TILE_A
    blk = lambda width: pl.BlockSpec((tile, width), lambda r, *_: (r, 0))
    full = lambda *shape: pl.BlockSpec(shape, lambda r, *_: (0,) * len(shape))
    sds = jax.ShapeDtypeStruct
    sources = tuple(leave) + tuple(widen) + tuple(narrow)
    return pl.pallas_call(
        partial(expand_kernel, (len(leave), len(widen), len(narrow))),
        grid_spec=pltpu.PrefetchScalarGridSpec(
            num_scalar_prefetch=1,
            grid=(tokens // tile,),
            in_specs=[blk(D), blk(D), full(8, D), full(1, FF)] + [ANY] * len(sources),
            out_specs=[blk(D), blk(FF), blk(FF), blk(D), blk(D)],
            scratch_shapes=[
                pltpu.VMEM((D, D), BF16),
                pltpu.VMEM((4, D, D), BF16),
                pltpu.VMEM((64, 48, D), BF16),
                pltpu.SemaphoreType.DMA((3,)),
            ],
        ),
        out_shape=[
            sds((tokens, D), F32),
            sds((tokens, FF), BF16),
            sds((tokens, FF), BF16),
            sds((tokens, D), F32),
            sds((tokens, D), BF16),
        ],
        compiler_params=pltpu.CompilerParams(vmem_limit_bytes=VMEM_LIMIT),
        cost_estimate=pl.CostEstimate(
            flops=2 * tokens * D * (D + 2 * FF), bytes_accessed=30_000_000, transcendentals=tokens * FF
        ),
        name="expand",
    )(index, ctx, resid, vectors, wide_bias, *sources)


def contract_kernel(counts, me_ref, dz_ref, before_ref, slope_ref, u_ref, vec_ref, *refs):
    c1, c2, c3 = counts
    leave_src, widen_src, narrow_src = refs[:c1], refs[c1 : c1 + c2], refs[c1 + c2 : c1 + c2 + c3]
    refs = refs[c1 + c2 + c3 :]
    dback_ref, mixed_ref, dhid_ref, dattn_ref, du_ref, dctx_ref, dvec_ref, dbias_ref = refs[:8]
    leave, widen, narrow, sem = refs[8:]
    first = pl.program_id(0) == 0

    @pl.when(first)
    def _():
        start_load(me_ref[0], narrow_src, narrow, sem.at[2], place_narrow)
        start_load(me_ref[0], widen_src, widen, sem.at[1], place_widen)
        start_load(me_ref[0], leave_src, leave, sem.at[0], place_leave)
        dvec_ref[...] = jnp.zeros_like(dvec_ref)
        dbias_ref[...] = jnp.zeros_like(dbias_ref)

    dz = wide(dz_ref[...])
    unit, rstd = statistics(before_ref[...])
    dvec_ref[6:7, :] += column_sum(dz * unit)
    dvec_ref[7:8, :] += column_sum(dz)
    dpre = norm_pull(dz * vec_ref[6:7, :], unit, rstd)
    dback = low(dpre)
    dback_ref[...] = dback
    dvec_ref[5:6, :] += column_sum(wide(dback))
    unit, rstd = statistics(u_ref[...])
    mixed_ref[...] = low(unit * vec_ref[3:4, :] + vec_ref[4:5, :])

    @pl.when(first)
    def _():
        wait_load(narrow, sem.at[2])
        wait_load(widen, sem.at[1])
        wait_load(leave, sem.at[0])

    dmixed = dpre
    for j in range(4):
        cols = slice(D * j, D * j + D)
        dact = mm(dback, narrow[16 * j : 16 * j + 16].reshape(D, D), NT)
        dhid = low(dact * wide(slope_ref[:, cols]))
        dhid_ref[:, cols] = dhid
        dbias_ref[:, cols] += column_sum(wide(dhid))
        dmixed = dmixed + mm(dhid, widen[j], NT)
    dvec_ref[3:4, :] += column_sum(dmixed * unit)
    dvec_ref[4:5, :] += column_sum(dmixed)
    du = norm_pull(dmixed * vec_ref[3:4, :], unit, rstd)
    du_ref[...] = du
    dattn = low(du)
    dattn_ref[...] = dattn
    dvec_ref[2:3, :] += column_sum(wide(dattn))
    dctx_ref[...] = low(mm(dattn, leave[...], NT))


def contract(index, dz, before, hidden_units, u, vectors, leave, widen, narrow):
    tokens = dz.shape[0]
    tile = TILE_B
    blk = lambda width: pl.BlockSpec((tile, width), lambda r, *_: (r, 0))
    full = lambda *shape: pl.BlockSpec(shape, lambda r, *_: (0,) * len(shape))
    sds = jax.ShapeDtypeStruct
    sources = tuple(leave) + tuple(widen) + tuple(narrow)
    return pl.pallas_call(
        partial(contract_kernel, (len(leave), len(widen), len(narrow))),
        grid_spec=pltpu.PrefetchScalarGridSpec(
            num_scalar_prefetch=1,
            grid=(tokens // tile,),
            in_specs=[blk(D), blk(D), blk(FF), blk(D), full(8, D)] + [ANY] * len(sources),
            out_specs=[blk(D), blk(D), blk(FF), blk(D), blk(D), blk(D), full(8, D), full(1, FF)],
            scratch_shapes=[
                pltpu.VMEM((D, D), BF16),
                pltpu.VMEM((4, D, D), BF16),
                pltpu.VMEM((64, 48, D), BF16),
                pltpu.SemaphoreType.DMA((3,)),
            ],
        ),
        out_shape=[
            sds((tokens, D), BF16),
            sds((tokens, D), BF16),
            sds((tokens, FF), BF16),
            sds((tokens, D), BF16),
            sds((tokens, D), F32),
            sds((tokens, D), BF16),
            sds((8, D), F32),
            sds((1, FF), F32),
        ],
        compiler_params=pltpu.CompilerParams(vmem_limit_bytes=VMEM_LIMIT),
        cost_estimate=pl.CostEstimate(
            flops=2 * tokens * D * (D + 2 * FF), bytes_accessed=50_000_000, transcendentals=tokens * FF
        ),
        name="contract",
    )(index, dz, before, hidden_units, u, vectors, *sources)


def halves(core, value, width):
    left, right = value[:, :width], value[:, width:]
    first = core == 0
    return jnp.where(first, right, left), jnp.where(first, left, right)


def flush(pairs, start, rows, sem):
    copies = [
        pltpu.make_async_copy(scratch, out_ref.at[:, start : start + rows, :], sem.at[i])
        for i, (scratch, out_ref) in enumerate(pairs)
    ]
    for copy in copies:
        copy.start()
    for copy in copies:
        copy.wait()


def sum_call(kernel, name, total_rows, start, rows, grid, prefetch, inputs, in_specs, scratch, before, flops):
    out = jax.ShapeDtypeStruct((UNITS, total_rows, HALF), BF16)
    return pl.pallas_call(
        partial(kernel, start, rows),
        grid_spec=pltpu.PrefetchScalarGridSpec(
            num_scalar_prefetch=len(prefetch),
            grid=grid,
            in_specs=in_specs + [ANY] * len(before),
            out_specs=[ANY, ANY],
            scratch_shapes=[
                pltpu.VMEM((UNITS, rows, HALF), BF16),
                pltpu.VMEM((UNITS, rows, HALF), BF16),
                pltpu.SemaphoreType.DMA((2,)),
            ]
            + scratch,
        ),
        out_shape=[out, out],
        input_output_aliases={len(prefetch) + len(inputs) + i: i for i in range(len(before))},
        compiler_params=pltpu.CompilerParams(vmem_limit_bytes=VMEM_LIMIT),
        cost_estimate=pl.CostEstimate(flops=flops, bytes_accessed=16_000_000, transcendentals=0),
        name=name,
    )(*prefetch, *inputs, *before)


def narrow_grad_kernel(start, rows, me_ref, act_ref, dback_ref, ctx_ref, dattn_ref, *refs):
    send_out, keep_out, send_ref, keep_ref, sem = refs[-5:]
    step = pl.program_id(0)
    core = jnp.bitwise_and(me_ref[0], 1)
    chip = lax.shift_right_logical(me_ref[0], 1)

    @pl.when(step < 4)
    def _():
        send, keep = halves(core, mm(act_ref[...], dback_ref[...], TN), HALF)
        for i in range(4):
            at = position(chip, step * 4 + i)
            send_ref[at, 0:192, :] = low(send[192 * i : 192 * i + 192])
            keep_ref[at, 0:192, :] = low(keep[192 * i : 192 * i + 192])

    @pl.when(step == 4)
    def _():
        send, keep = halves(core, mm(ctx_ref[...], dattn_ref[...], TN), HALF)
        for i in range(UNITS):
            at = position(chip, i)
            send_ref[at, 192:240, :] = low(send[48 * i : 48 * i + 48])
            keep_ref[at, 192:240, :] = low(keep[48 * i : 48 * i + 48])
        flush(((send_ref, send_out), (keep_ref, keep_out)), start, rows, sem)


def halves(core, value, width):
    left, right = value[:, :width], value[:, width:]
    first = core == 0
    return jnp.where(first, right, left), jnp.where(first, left, right)


def narrow_grad(total_rows, index, act, dback, ctx, dattn):
    tokens = act.shape[0]
    specs = [pl.BlockSpec((tokens, D), lambda r, *_: (0, jnp.minimum(r, 3)))] + [whole(tokens, D)] * 3
    return sum_call(
        narrow_grad_kernel, "narrow_grad", total_rows, 0, 240, (5,), (index,),
        (act, dback, ctx, dattn), specs, [], (), 2 * tokens * D * (D + FF),
    )


def widen_grad_kernel(start, rows, me_ref, mixed_ref, dhid_ref, *refs):
    send_out, keep_out, send_ref, keep_ref, sem, turned = refs[-6:]
    step = pl.program_id(0)
    core = jnp.bitwise_and(me_ref[0], 1)
    chip = lax.shift_right_logical(me_ref[0], 1)

    @pl.when(step == 0)
    def _():
        turned[...] = mixed_ref[...].T

    grad = low(mm(turned[...], dhid_ref[...]))
    mine = lax.div(step, 2) == core
    for part in range(2):

        @pl.when(lax.rem(step, 2) == part)
        def _():
            for wanted, out_ref in ((True, keep_ref), (False, send_ref)):

                @pl.when(mine == wanted)
                def _():
                    for i in range(UNITS):
                        at = position(chip, i)
                        for q in range(2):
                            line = 96 * part + 48 * q
                            out_ref[at, line : line + 48, :] = grad[
                                48 * i : 48 * i + 48, HALF * q : HALF * q + HALF
                            ]

    @pl.when(step == 3)
    def _():
        flush(((send_ref, send_out), (keep_ref, keep_out)), start, rows, sem)


def widen_grad(total_rows, index, mixed_low, dhid, before):
    start = 240 if before else 0
    tokens = mixed_low.shape[0]
    specs = [whole(tokens, D), pl.BlockSpec((tokens, D), lambda r, *_: (0, r))]
    return sum_call(
        widen_grad_kernel, "widen_grad", total_rows, start, 192, (4,), (index,),
        (mixed_low, dhid), specs, [pltpu.VMEM((D, tokens), BF16)], before, 2 * tokens * D * FF,
    )


def entry_grad_kernel(start, rows, len_ref, me_ref, a_ref, b_ref, dq_ref, dk_ref, dv_ref, vec_ref, *refs):
    send_out, keep_out, send_ref, keep_ref, sem, total = refs[-6:]
    row = pl.program_id(0)
    core = jnp.bitwise_and(me_ref[0], 1)
    chip = lax.shift_right_logical(me_ref[0], 1)
    keys = b_ref.shape[1]

    @pl.when(row == 0)
    def _():
        total[...] = jnp.zeros_like(total)

    total[0] += mm(a_ref[0], dq_ref[0], TN)
    for block in range(keys // 256):

        @pl.when(block * 256 < len_ref[row])
        def _():
            lines = pl.ds(block * 256, 256)
            b = b_ref[0, lines, :].T
            total[1] += mm(b, dk_ref[0, lines, :])
            total[2] += mm(b, dv_ref[0, lines, :])

    @pl.when(row == pl.num_programs(0) - 1)
    def _():
        for m in range(3):
            send, keep = halves(core, total[m], HALF)
            for i in range(UNITS):
                at = position(chip, i)
                send_ref[at, 48 * m : 48 * m + 48, :] = low(send[48 * i : 48 * i + 48])
                keep_ref[at, 48 * m : 48 * m + 48, :] = low(keep[48 * i : 48 * i + 48])
        for i in range(UNITS):
            at = position(chip, i)
            send_ref[at, 144:160, :] = vec_ref[i, 1 - core]
            keep_ref[at, 144:160, :] = vec_ref[i, core]
        flush(((send_ref, send_out), (keep_ref, keep_out)), start, rows, sem)


def entry_grad(total_rows, start, index, lengths, a, b, dq, dk, dv, vec, before):
    rows, keys, _ = b.shape
    queries = a.shape[1]
    blk = lambda *shape: pl.BlockSpec((1,) + shape, lambda r, *_: (r,) + (0,) * len(shape))
    specs = [blk(queries, D), blk(keys, D), blk(queries, D), blk(keys, D), blk(keys, D)]
    specs.append(whole(UNITS, 2, 16, HALF))
    return sum_call(
        entry_grad_kernel, "entry_grad", total_rows, start, 160, (rows,), (lengths, index),
        (a, b, dq, dk, dv, vec), specs, [pltpu.VMEM((3, D, D), F32)], before,
        2 * rows * (queries + keys) * D * D,
    )


def retrace_kernel(stride, base, len_ref, me_ref, q_ref, k_ref, v_ref, dctx_ref, probs_ref, *refs):
    dq_ref, dk_ref, dv_ref, dvec_ref, diag_ref, ends_ref, bias_sum, turned = refs[-8:]
    row = pl.program_id(0)
    keys = k_ref.shape[1]
    queries = q_ref.shape[1]
    length = len_ref[row + base]

    @pl.when(row == 0)
    def _():
        bias_sum[...] = jnp.zeros_like(bias_sum)
        dvec_ref[...] = jnp.zeros_like(dvec_ref)

    def group_step(size, pairs, step, carry):
        loaded = []
        for p in range(pairs):
            lanes = pl.ds(pl.multiple_of((step * pairs + p) * 128, 128), 128)
            dctx = lane_masks(dctx_ref[0, :, lanes])
            value = v_ref[0, :size, lanes]
            loaded.append((lanes, dctx, [mm(value, dctx[i], NT) for i in range(2)]))
        made = []
        for p, (lanes, dctx, dprobs) in enumerate(loaded):
            grads, probs = [], []
            for i in range(2):
                h = 2 * (step * pairs + p) + i
                kept = probs_ref[0, h, :size, :]
                prob = wide(kept)
                inner = jnp.sum(prob * dprobs[i], axis=0, keepdims=True)
                inner = inner / jnp.sum(prob, axis=0, keepdims=True)
                grad = low(prob * (dprobs[i] - inner))
                for lane in range(queries // 128):
                    bias_sum[lane, h, :size, :] += wide(grad[:, 128 * lane : 128 * lane + 128])
                grads.append(grad)
                probs.append(kept)
            made.append((lanes, dctx, grads, probs))
        for p, (lanes, dctx, grads, probs) in enumerate(made):
            query = lane_masks(q_ref[0, :, lanes])
            key = k_ref[0, :size, lanes].T
            for i in range(2):
                h = 2 * (step * pairs + p) + i
                turned[pl.ds(pl.multiple_of(HD * h, HD), HD), :] = (
                    mm(key[HD * i : HD * i + HD], grads[i]) * HD**-0.5
                )
            dv_ref[0, :size, lanes] = low(
                mm(jnp.concatenate(probs, axis=1), jnp.concatenate(dctx, axis=0))
            )
            dk_ref[0, :size, lanes] = low(
                mm(jnp.concatenate(grads, axis=1), jnp.concatenate(query, axis=0))
            )
        return carry

    blocks = lax.div(length + 127, 128)
    for w in range(1, keys // 128 + 1):

        @pl.when(blocks == w)
        def _():
            size, pairs = 128 * w, GROUPS[w - 1]
            lax.fori_loop(0, H // 2 // pairs, partial(group_step, size, pairs), 0)
            if size < keys:
                dk_ref[0, size:, :] = jnp.zeros((keys - size, D), BF16)
                dv_ref[0, size:, :] = jnp.zeros((keys - size, D), BF16)
            dvec_ref[1:2, :] += column_sum(wide(dv_ref[0, :size, :]))

    dquery = low(turned[...].T)
    dq_ref[0] = dquery
    dvec_ref[0:1, :] += column_sum(wide(dquery))

    @pl.when(row == pl.num_programs(0) - 1)
    def _():
        ends_ref[...] = jnp.zeros_like(ends_ref)

        def collect(h, carry):
            below = above = jnp.zeros((1, queries), F32)
            for part in range(stride):
                block = jnp.concatenate(
                    [
                        bias_sum[lane, h, pl.ds(part, queries, stride=stride), :]
                        for lane in range(queries // 128)
                    ],
                    axis=1,
                )
                col = lax.broadcasted_iota(jnp.int32, block.shape, 1)
                line = lax.broadcasted_iota(jnp.int32, block.shape, 0)
                place = stride * (line - col) + part
                zero = jnp.zeros_like(block)
                below = below + column_sum(jnp.where(place <= -(NB // 2), block, zero))
                above = above + column_sum(jnp.where(place >= NB // 2 - 1, block, zero))
                inside = jnp.where((place > -(NB // 2)) & (place < NB // 2 - 1), block, zero)
                partial_sum = inside[:8]
                for a in range(1, queries // 8):
                    partial_sum = partial_sum + pltpu.roll(inside[8 * a : 8 * a + 8], queries - 8 * a, 1)
                sub = lax.broadcasted_iota(jnp.int32, partial_sum.shape, 0)
                lined = jnp.where(sub == 0, partial_sum, 0.0)
                for b in range(1, 8):
                    lined = lined + jnp.where(sub == b, pltpu.roll(partial_sum, queries - b, 1), 0.0)
                diag_ref[h, part] = jnp.broadcast_to(column_sum(lined), (8, queries))
            ends_ref[h, 0] = jnp.broadcast_to(below, (8, queries))
            ends_ref[h, 1] = jnp.broadcast_to(above, (8, queries))
            return carry

        lax.fori_loop(0, H, collect, 0)


def retrace(stride, index, lengths, q, k, v, dctx, probs, base, count, before=()):
    rows, keys, _ = k.shape
    queries = q.shape[1]
    blk = lambda *shape: pl.BlockSpec((1,) + shape, lambda r, *_: (r + base,) + (0,) * len(shape))
    full = lambda *shape: pl.BlockSpec(shape, lambda r, *_: (0,) * len(shape))
    sds = jax.ShapeDtypeStruct
    return pl.pallas_call(
        partial(retrace_kernel, stride, base),
        grid_spec=pltpu.PrefetchScalarGridSpec(
            num_scalar_prefetch=2,
            grid=(count,),
            in_specs=[
                blk(queries, D),
                blk(keys, D),
                blk(keys, D),
                blk(queries, D),
                blk(H, keys, queries),
            ]
            + [ANY] * len(before),
            out_specs=[
                blk(queries, D),
                blk(keys, D),
                blk(keys, D),
                full(8, D),
                full(H, stride, 8, queries),
                full(H, 2, 8, queries),
            ],
            scratch_shapes=[
                pltpu.VMEM((queries // 128, H, keys, 128), F32),
                pltpu.VMEM((D, queries), F32),
            ],
        ),
        out_shape=[
            sds((rows, queries, D), BF16),
            sds((rows, keys, D), BF16),
            sds((rows, keys, D), BF16),
            sds((8, D), F32),
            sds((H, stride, 8, queries), F32),
            sds((H, 2, 8, queries), F32),
        ],
        input_output_aliases={7 + i: i for i in range(len(before))},
        compiler_params=pltpu.CompilerParams(vmem_limit_bytes=VMEM_LIMIT),
        cost_estimate=pl.CostEstimate(
            flops=count * keys * queries * D * 10, bytes_accessed=20_000_000, transcendentals=count * H * keys * queries
        ),
        name="retrace",
    )(lengths, index, q, k, v, dctx, probs, *before)


def table_grad(stride, diag, ends):
    queries = diag.shape[-1]
    columns = []
    for bucket in range(NB):
        place = bucket - NB // 2
        if bucket == 0:
            columns.append(jnp.sum(ends[:, 0, 0], axis=-1))
        elif bucket == NB - 1:
            columns.append(jnp.sum(ends[:, 1, 0], axis=-1))
        else:
            part = place % stride
            columns.append(diag[:, part, 0, ((part - place) // stride) % queries])
    return jnp.stack(columns, axis=1).reshape(-1)


def inputs_kernel(stride, base, count, len_ref, me_ref, dq_ref, dk_ref, dv_ref, du_ref, *refs):
    sources = refs[:count]
    out_ref, entry, sem = refs[-3:]
    row = pl.program_id(0)
    keys = dk_ref.shape[1]
    queries = dq_ref.shape[1]

    @pl.when(row == 0)
    def _():
        start_load(me_ref[0], sources, entry, sem.at[0], place_entry)
        wait_load(entry, sem.at[0])

    total = mm(dq_ref[0], entry[0], NT) + du_ref[0]
    if stride == 1:
        out_ref[0] = total + mm(dk_ref[0], entry[1], NT) + mm(dv_ref[0], entry[2], NT)
        return
    total = 0.5 * total
    upper = low(total)
    lower = low(total - wide(upper))
    for block in range(keys // 256):
        rows = pl.ds(block * 256, 256)
        place = lax.broadcasted_iota(jnp.int32, (256, queries), 0) + 256 * block
        mine = lax.broadcasted_iota(jnp.int32, (256, queries), 1)
        pair = jnp.where(lax.shift_right_logical(place, 1) == mine, 1.0, 0.0).astype(BF16)
        spread = mm(pair, upper) + mm(pair, lower)

        @pl.when(block * 256 < len_ref[row + base])
        def _():
            out_ref[0, rows, :] = (
                spread + mm(dk_ref[0, rows, :], entry[1], NT) + mm(dv_ref[0, rows, :], entry[2], NT)
            )

        @pl.when(block * 256 >= len_ref[row + base])
        def _():
            out_ref[0, rows, :] = spread


def input_grads(stride, index, lengths, dq, dk, dv, du, sources, base, count, before=()):
    rows, keys, _ = dk.shape
    queries = dq.shape[1]
    blk = lambda *shape: pl.BlockSpec((1,) + shape, lambda r, *_: (r + base,) + (0,) * len(shape))
    return pl.pallas_call(
        partial(inputs_kernel, stride, base, len(sources)),
        grid_spec=pltpu.PrefetchScalarGridSpec(
            num_scalar_prefetch=2,
            grid=(count,),
            in_specs=[blk(queries, D), blk(keys, D), blk(keys, D), blk(queries, D)] + [ANY] * (len(sources) + len(before)),
            out_specs=blk(keys, D),
            scratch_shapes=[pltpu.VMEM((3, D, D), BF16), pltpu.SemaphoreType.DMA((1,))],
        ),
        out_shape=jax.ShapeDtypeStruct((rows, keys, D), F32),
        input_output_aliases={6 + len(sources) + i: i for i in range(len(before))},
        compiler_params=pltpu.CompilerParams(vmem_limit_bytes=VMEM_LIMIT),
        cost_estimate=pl.CostEstimate(
            flops=2 * count * (queries + keys) * D * D, bytes_accessed=20_000_000, transcendentals=0
        ),
        name="input_grads",
    )(lengths, index, dq, dk, dv, du, *sources, *before)


def vectors_by_unit(dvec, dbias, dtable):
    flat = vector_units(dvec, dbias, dtable, 32)
    return jnp.pad(low(flat), ((0, 0), (0, 16 * HALF - flat.shape[1]))).reshape(UNITS, 2, 16, HALF)


NARROW_CUTS = ((192, 96), (48, 24))
WIDEN_CUTS = ((48, 24),) * 4
FEED_CUTS = NARROW_CUTS + WIDEN_CUTS
ENTRY_CUTS = ((48, 24),) * 3


def join(left, right):
    return jnp.concatenate([left, right], axis=-1)


def feed_shards(left, right):
    widen = jnp.concatenate([left[120:216].reshape(4, 24, HALF), right[120:216].reshape(4, 24, HALF)])
    return (
        join(left[96:120], right[96:120]),
        widen.transpose(1, 0, 2).reshape(24, FF),
        join(left[:96], right[:96]),
    )


def entry_shards(left, right):
    return join(left, right).reshape(3, 24, D)


def absolute_units(pair):
    send, keep = pair
    merged = jnp.stack([keep, send], axis=2)
    rest = merged.shape[1:]
    merged = merged.reshape((4, 4) + rest).transpose(1, 0, 2, 3, 4)
    return wide(merged.reshape((UNITS,) + rest))


def plain_shards(feed, entry):
    feed, entry = absolute_units(feed), absolute_units(entry)
    narrow = feed[:, :192].reshape(FF, D)
    leave = feed[:, 192:240].reshape(D, D)
    widen = feed[:, 240:432].reshape(UNITS, 4, 48, 2, HALF).transpose(0, 2, 3, 1, 4).reshape(D, FF)
    vectors = entry[:, 144:].transpose(0, 2, 1, 3).reshape(32, -1)
    entry = entry[:, :144].reshape(UNITS, 3, 48, D).transpose(1, 0, 2, 3).reshape(3, D, D)
    scatter = lambda value, dim: lax.psum_scatter(value, AX, scatter_dimension=dim, tiled=True)
    rows = vectors.shape[0]
    cut, mid = 8 * D // rows, 8 * D // rows + FF // rows
    last = mid + H * NB // rows
    vec = vectors[:, :cut].reshape(rows, 8, -1).transpose(1, 0, 2).reshape(8, D)
    return (
        scatter(entry, 1),
        scatter(leave, 0),
        scatter(widen, 0),
        scatter(narrow, 0),
        scatter(vec, 1),
        scatter(vectors[:, cut:mid].reshape(-1), 0),
        scatter(vectors[:, mid:last].reshape(-1), 0),
    )


def plain_gather(entry, leave, widen, narrow):
    gather = lambda value, dim: lax.all_gather(value, AX, axis=dim, tiled=True)
    widen = gather(widen, 0).reshape(D, 4, D).transpose(1, 0, 2)
    return (
        (gather(entry, 1),),
        (gather(leave, 0),),
        (widen,),
        (gather(narrow, 0).reshape(64, 48, D),),
    )


def plain_vectors(*small):
    gather = lambda value, dim: lax.all_gather(value, AX, axis=dim, tiled=True)
    parts = []
    for value in small:
        full = gather(value, value.ndim - 1)
        if value.ndim == 2:
            parts.append(full.reshape(8, 32, 24).transpose(1, 0, 2))
        else:
            parts.append(full.reshape(32, -1))
    slabs = vector_slab(*parts).reshape(4, 4, 2, 16, 128).transpose(2, 1, 0, 3, 4)
    return slabs[0].reshape(UNITS, 16, 128), slabs[1].reshape(UNITS, 16, 128)


def on_device(
    devices,
    hidden,
    lengths,
    cotangent,
    inflow,
    outflow,
    widener,
    narrower,
    shifts,
    offsets,
    distance,
    intake,
    outtake,
    expander,
    squeezer,
    adjusts,
    leanings,
    spacing,
):
    rows, seq, width = hidden.shape
    half = seq // 2
    fast = devices == 32
    index = lax.axis_index(AX)
    core = index % 2
    halved = (lengths + 1) // 2
    layer_one = (inflow, outflow, widener, narrower)
    layer_two = (intake, outtake, expander, squeezer)

    small = (shifts, offsets, distance, adjusts, leanings, spacing)
    if fast:
        ticks = Ticks(index.astype(jnp.int32).reshape(1))
        tick = ticks.run
        vec = Job(vector_stages, vector_slab(*small))
        eo1, w1 = gather_jobs(core, True, *layer_one)
        eo2, w2 = gather_jobs(core, False, *layer_two)
        tick([eo1, vec, w1])
        tick([eo1, vec, w1])
        tick([eo1, vec, w1])
        prepared = tick([eo1], lambda me: prepare(me, *vec.result, seq, half))
        tick([eo1, eo2, w2])
    else:
        ticks = Ticks(jnp.zeros((1,), jnp.int32))
        eo1 = w1 = eo2 = w2 = None
        plain_one, plain_two = plain_gather(*layer_one), plain_gather(*layer_two)
        prepared = prepare(ticks.me, *plain_vectors(*small), seq, half)

        def tick(jobs, kernel=None):
            return ticks.run([], kernel)

    def weights(layer, names):
        if fast:
            jobs = {"e": (eo1, eo2), "o": (eo1, eo2), "w": (w1, w2), "n": (w1, w2)}
            return [jobs[name][layer].result for name in names]
        return [(plain_one, plain_two)[layer]["eown".index(name)] for name in names]

    vec1, bias1, tab1, vec2, bias2, tab2 = prepared
    flatten = lambda value: value.reshape(-1, D)
    part = rows // 2

    def begin(stride, me, lens, x, vec_in, layer, tab):
        made = project(stride, me, lens, x, vec_in, *weights(layer, "e"))
        q, k, v = made[-3:]
        return made, attend(stride, me, lens, q, k, v, tab, 0, part)

    def finish(stride, me, lens, made, tab, head):
        return attend(stride, me, lens, *made[-3:], tab, part, rows - part, head)

    made1, head = tick([w1, eo2, w2], lambda me: begin(2, me, lengths, hidden, vec1, 0, tab1))
    ctx1, probs1 = tick([w1, eo2], lambda me: finish(2, me, lengths, made1, tab1, head))
    pooled, pooled_low, q1, k1, v1 = made1
    tick([w1])
    u1, act1, slope1, before1, first_out = tick(
        [eo2, w2],
        lambda me: expand(me, flatten(ctx1), flatten(pooled), vec1, bias1, *weights(0, "own")),
    )
    pooled_layer = first_out.reshape(rows, half, width)

    tick([eo2])
    tick([eo2])
    made2, head = tick([w2], lambda me: begin(1, me, halved, pooled_layer, vec2, 1, tab2))
    ctx2, probs2 = tick([w2], lambda me: finish(1, me, halved, made2, tab2, head))
    q2, k2, v2 = made2
    tick([w2])
    u2, act2, slope2, before2, second_out = tick(
        [], lambda me: expand(me, flatten(ctx2), first_out, vec2, bias2, *weights(1, "own"))
    )

    def reducing(pair, cuts, direct=False):
        return Job(reduce_stages, core, cuts, direct, *pair) if fast else pair

    dback, mixed_low, dhid, dattn, du, dctx, dvec, dbias = tick(
        [],
        lambda me: contract(me, cotangent.reshape(-1, D), before2, slope2, u2, vec2, *weights(1, "own")),
    )

    narrow2 = tick([], lambda me: narrow_grad(240, me, act2, dback, flatten(ctx2), dattn))
    sumn2 = reducing(narrow2, NARROW_CUTS)
    widen2 = tick([sumn2], lambda me: widen_grad(192, me, mixed_low, dhid, ()))
    sumw2 = reducing(widen2, WIDEN_CUTS)
    back = tick(
        [sumn2, sumw2],
        lambda me: retrace(1, me, halved, q2, k2, v2, dctx.reshape(q2.shape), probs2, 0, rows),
    )
    dq, dk, dv, dvec_top, diag, ends = back
    packed = vectors_by_unit(dvec + dvec_top, dbias, table_grad(1, diag, ends))

    def entry_end(me):
        made = entry_grad(160, 0, me, halved, pooled_layer, pooled_layer, dq, dk, dv, packed, ())
        parts = (dq, dk, dv, du.reshape(q2.shape), *weights(1, "e"))
        return made, input_grads(1, me, halved, *parts, 0, rows)

    entry2, dlayer = tick([sumn2, sumw2], entry_end)
    sume2 = reducing(entry2, ENTRY_CUTS)

    dback, mixed_low, dhid, dattn, du, dctx, dvec, dbias = tick(
        [sumw2, sumn2, sume2],
        lambda me: contract(me, flatten(dlayer), before1, slope1, u1, vec1, *weights(0, "own")),
    )
    narrow1 = tick(
        [sumw2, sumn2, sume2], lambda me: narrow_grad(240, me, act1, dback, flatten(ctx1), dattn)
    )
    sumn1 = reducing(narrow1, NARROW_CUTS)
    widen1 = tick([sumn1, sumw2, sume2], lambda me: widen_grad(192, me, mixed_low, dhid, ()))
    sumw1 = reducing(widen1, WIDEN_CUTS)
    parts = (q1, k1, v1, dctx.reshape(q1.shape), probs1)
    head = tick([sumn1, sumw1, sume2, sumn2], lambda me: retrace(2, me, lengths, *parts, 0, part))
    back = tick(
        [sumn1, sumw1, sume2], lambda me: retrace(2, me, lengths, *parts, part, rows - part, head[:3])
    )
    dq, dk, dv = back[:3]
    dvec_top, diag, ends = [one + two for one, two in zip(head[3:], back[3:])]
    packed = vectors_by_unit(dvec + dvec_top, dbias, table_grad(2, diag, ends))
    entry1 = tick(
        [sumw1, sumn1, sumw2],
        lambda me: entry_grad(160, 0, me, lengths, pooled_low, hidden, dq, dk, dv, packed, ()),
    )
    sume1 = reducing(entry1, ENTRY_CUTS, True)
    parts = (dq, dk, dv, du.reshape(q1.shape), *weights(0, "e"))
    ends = (0, 1, 2, rows) if rows > 2 else (0, rows)
    beside = ([sume1, sumn1, sume2], [sume1, sumn1], [sume1, sumw1])
    done = ()
    for first, last, jobs in zip(ends, ends[1:], beside):
        done = (
            tick(
                jobs,
                lambda me: input_grads(2, me, lengths, *parts, first, last - first, done),
            ),
        )
    (hidden_grad,) = done
    if fast:
        for job in (sume1, sumw1, sumn1, sumn2, sumw2, sume2):
            while job.result is None:
                tick([job, sumw1] if job is sume1 else [job])
        left, right, rest = sume2.result
        feed = [jnp.concatenate(sides) for sides in zip(sumn2.result[:2], sumw2.result[:2])]
        shards_two = (entry_shards(left, right),) + feed_shards(*feed)
        shards_two = shards_two + split_vectors(rest.reshape(-1), 32)
        left, right, rest = sume1.result
        feed = [jnp.concatenate(sides) for sides in zip(sumn1.result[:2], sumw1.result[:2])]
        shards_one = (entry_shards(left, right),) + feed_shards(*feed)
        shards_one = shards_one + split_vectors(rest.reshape(-1), 32)
    else:
        feed2 = [jnp.concatenate(sides, axis=1) for sides in zip(narrow2, widen2)]
        feed1 = [jnp.concatenate(sides, axis=1) for sides in zip(narrow1, widen1)]
        shards_one, shards_two = plain_shards(feed1, entry1), plain_shards(feed2, entry2)
    return (
        pooled_layer,
        second_out.reshape(rows, half, width),
        hidden_grad,
        *shards_one,
        *shards_two[:4],
        shards_two[4][1:],
        shards_two[5],
        shards_two[6],
        shards_two[4][0],
    )


def solution(mesh):
    both = ("wide", "narrow")
    rows = P(both, None, None)
    weights = (
        P(None, both, None),
        P(both, None),
        P(both, None),
        P(both, None),
        P(None, both),
        P(both),
        P(both),
    )
    return jax.shard_map(
        partial(on_device, mesh.size),
        mesh=mesh,
        in_specs=(rows, P(both), rows) + weights + weights,
        out_specs=(rows, rows, rows) + weights + weights + (P(both),),
        check_vma=False,
    )
```

```python
from functools import partial

import jax
import jax.numpy as jnp
from jax import lax
from jax.experimental import pallas as pl
from jax.experimental.pallas import tpu as pltpu
from jax.sharding import PartitionSpec as P

H = 12
HD = 64
NB = 32
D = 768
FF = 3072
HALF = 384
EPS = 1e-06
AX = ("wide", "narrow")
CORE, XBIT, YBIT, Z0, Z1 = 1, 2, 4, 8, 16
UNITS = 16
F32 = jnp.float32
BF16 = jnp.bfloat16
GELU_A = 0.7978845608028654
GELU_B = 0.044715
NN = (((1,), (0,)), ((), ()))
NT = (((1,), (1,)), ((), ()))
TN = (((0,), (0,)), ((), ()))
GROUPS = (6, 6, 3, 3)
TILE_A = 256
TILE_B = 256
VMEM_LIMIT = 60 * 1024 * 1024
ANY = pl.BlockSpec(memory_space=pl.ANY)


def mm(left, right, dims=NN):
    return lax.dot_general(left, right, dims, preferred_element_type=F32)


def wide(value):
    return value.astype(F32)


def low(value):
    return value.astype(BF16)


SENT = []


def swap(value, mask):
    SENT.append(value)
    return lax.ppermute(value, AX, [(i, i ^ mask) for i in range(32)])


def pick(core, first, second):
    return jnp.where(core == 0, first, second)


class Job:
    def __init__(self, stages, *operands):
        self.stages = stages(*operands)
        self.operands = next(self.stages)
        self.result = None

    def step(self, operands):
        try:
            self.operands = self.stages.send(operands)
        except StopIteration as stop:
            self.result = stop.value
            self.operands = ()


class Ticks:
    def __init__(self, me):
        self.me = me
        self.last = ()
        self.flying = []

    def run(self, jobs, kernel=None):
        jobs = [job for job in jobs if job.result is None]
        tied = jobs + [job for job in self.flying if job not in jobs]
        operands = [job.operands if job.result is None else job.result for job in tied]
        self.me, operands, self.last = lax.optimization_barrier((self.me, operands, self.last))
        SENT.clear()
        for job, value in zip(tied, operands):
            if job in jobs:
                job.step(value)
            elif job.result is None:
                job.operands = value
            else:
                job.result = value
        self.flying = jobs
        if kernel is None:
            return None
        self.me = lax.optimization_barrier((self.me, list(SENT)))[0]
        out = kernel(self.me)
        self.last = jax.tree.leaves(out)[-1]
        return out


def gather_stages(pair, direct, keep, send):
    keep, send = yield keep, send
    core = lax.axis_index(AX) % 2
    recv = [swap(value, CORE) for value in send]
    first = [pick(core, mine, other) for mine, other in zip(keep, recv)]
    second = [pick(core, other, mine) for mine, other in zip(keep, recv)]
    slab = pair(first, second)
    slab = yield slab
    if direct:
        own = jnp.stack([slab, swap(slab, Z0), swap(slab, Z1), swap(slab, Z0 | Z1)])
    else:
        two = jnp.stack([slab, swap(slab, Z0)])
        two = yield two
        if direct is None:
            far = swap(two[:, :2], Z1)
            two, far = yield two, far
            far = jnp.concatenate([far, swap(two[:, 2:], Z1)], axis=1)
        else:
            far = swap(two, Z1)
        own = jnp.concatenate([two, far])
    own = yield own
    across_y = swap(own, YBIT)
    across_x = swap(own, XBIT)
    far = (swap(own, CORE),)
    own, across_y, across_x, far = yield own, across_y, across_x, far
    diag = (swap(across_y[:2], XBIT), swap(across_x[2:], YBIT))
    far = far + (swap(across_x, CORE), swap(across_y, CORE))
    mine, far = yield (own, across_x, across_y) + diag, far
    return mine + far + tuple(swap(piece, CORE) for piece in mine[3:])


def vector_stages(slab):
    slab = yield slab
    own = jnp.stack([slab, swap(slab, Z0), swap(slab, Z1), swap(slab, Z0 | Z1)])
    own = yield own
    across = [own, swap(own, XBIT), swap(own, YBIT), swap(own, XBIT | YBIT)]
    across = yield across
    near = jnp.concatenate(across)
    return near, swap(near, CORE)


def pair_entry(first, second):
    return jnp.concatenate([first[0], second[0]], axis=1)


def pair_wide(first, second):
    widen = jnp.concatenate([first[0], second[0]], axis=0).reshape(48, 2, D).transpose(1, 0, 2)
    narrow = jnp.concatenate([first[1].reshape(2, 48, HALF), second[1].reshape(2, 48, HALF)], axis=2)
    return jnp.concatenate([widen, narrow], axis=0)


def gather_jobs(core, ways, entry, leave, widen, narrow):
    def halved(*values):
        sides = []
        for side in (core, 1 - core):
            half = lambda value: value.shape[-1] // 2
            sides.append(
                [lax.dynamic_slice_in_dim(v, side * half(v), half(v), axis=-1) for v in values]
            )
        return sides

    eo = jnp.concatenate([entry, leave[None]])
    return (
        Job(gather_stages, pair_entry, ways[0], *halved(eo)),
        Job(gather_stages, pair_wide, ways[1], *halved(widen, narrow)),
    )


def reduce_stages(core, cuts, direct, send, keep):
    shape = (4, 4) + keep.shape[1:]
    send, keep = yield send, keep
    keep = keep.reshape(shape)
    recv = swap(send, CORE).reshape(shape)
    keep, recv = yield keep, recv
    diag_low = swap(low(wide(keep[3, :2]) + wide(recv[3, :2])), XBIT)
    diag_high = swap(low(wide(keep[3, 2:]) + wide(recv[3, 2:])), YBIT)
    keep, recv, diag_low, diag_high = yield keep, recv, diag_low, diag_high
    to_y = wide(keep[2]) + wide(recv[2])
    to_x = wide(keep[1]) + wide(recv[1])
    rest = [(0, 0)] * 2
    to_y = low(to_y + jnp.pad(wide(diag_low), [(0, 2)] + rest))
    to_x = low(to_x + jnp.pad(wide(diag_high), [(2, 0)] + rest))
    from_y, from_x = swap(to_y, YBIT), swap(to_x, XBIT)
    keep, recv, from_y, from_x = yield keep, recv, from_y, from_x

    def part(k):
        return (wide(keep[0, k]) + wide(recv[0, k])) + (wide(from_y[k]) + wide(from_x[k]))

    if direct:
        far = tuple(swap(low(part(k)), mask) for k, mask in ((1, Z0), (2, Z1), (3, Z0 | Z1)))
        keep, recv, from_y, from_x, far = yield keep, recv, from_y, from_x, far
        total = part(0) + wide(far[0]) + wide(far[1]) + wide(far[2])
    else:
        far = swap(jnp.stack([low(part(2)), low(part(3))]), Z1)
        keep, recv, from_y, from_x, far = yield keep, recv, from_y, from_x, far
        near = swap(low(part(1) + wide(far[1])), Z0)
        keep, recv, from_y, from_x, far, near = yield keep, recv, from_y, from_x, far, near
        total = part(0) + wide(far[0]) + wide(near)
    keeps, sends = [], []
    start = 0
    for rows, group in cuts:
        slab = total[start : start + rows].reshape(-1, 2, group, HALF)
        start += rows
        keeps.append(pick(core, slab[:, 0], slab[:, 1]).reshape(-1, HALF))
        sends.append(pick(core, slab[:, 1], slab[:, 0]).reshape(-1, HALF))
    rest = total[start:]
    keep, send = jnp.concatenate(keeps), jnp.concatenate(sends)
    recv = swap(send, CORE)
    return pick(core, keep, recv), pick(core, recv, keep), rest


def vector_units(vectors, wide_bias, table, parts):
    flat = jnp.concatenate(
        [
            vectors.reshape(8, parts, -1).transpose(1, 0, 2).reshape(parts, -1),
            wide_bias.reshape(parts, -1),
            table.reshape(parts, -1),
        ],
        axis=1,
    )
    return flat


def split_vectors(flat, parts):
    cut = 8 * D // parts
    mid = cut + FF // parts
    return flat[:cut].reshape(8, -1), flat[cut:mid], flat[mid : mid + H * NB // parts]


def position(chip, unit):
    rel = jnp.bitwise_xor(chip, unit)
    return jnp.bitwise_and(rel, 3) * 4 + lax.shift_right_logical(rel, 2)


def start_load(me, refs, dst, sem, place):
    if len(refs) == 1:
        pltpu.make_async_copy(refs[0], dst, sem).start()
        return
    chip = lax.shift_right_logical(me, 1)
    for side in range(2):
        half = jnp.bitwise_xor(jnp.bitwise_and(me, 1), side)
        own, across_x, across_y, diag_low, diag_high = refs[5 * side : 5 * side + 5]
        for k in range(4):
            for step, ref, at in (
                (0, own, k),
                (1, across_x, k),
                (2, across_y, k),
                (3, diag_low if k < 2 else diag_high, k % 2),
            ):
                unit = jnp.bitwise_xor(chip, 4 * k + step)
                for source, target in place(ref.at[at], dst, unit, half):
                    pltpu.make_async_copy(source, target, sem).start()


def wait_load(dst, sem):
    pltpu.make_async_copy(dst, dst, sem).wait()


def place_entry(src, dst, unit, half):
    rows, cols = pl.multiple_of(unit * 48, 16), pl.multiple_of(half * HALF, 128)
    return [(src.at[0:3], dst.at[:, pl.ds(rows, 48), pl.ds(cols, HALF)])]


def place_leave(src, dst, unit, half):
    rows, cols = pl.multiple_of(unit * 48, 16), pl.multiple_of(half * HALF, 128)
    return [(src.at[3], dst.at[pl.ds(rows, 48), pl.ds(cols, HALF)])]


def place_widen(src, dst, unit, half):
    rows = pl.multiple_of(unit * 48, 16)
    return [(src.at[0:2], dst.at[pl.ds(half * 2, 2), pl.ds(rows, 48), :])]


def place_narrow(src, dst, unit, half):
    cols = pl.multiple_of(half * HALF, 128)
    return [
        (
            src.at[2:4, :, HALF * g : HALF * g + HALF],
            dst.at[pl.ds(unit * 4 + 2 * g, 2), :, pl.ds(cols, HALF)],
        )
        for g in range(2)
    ]


def build_bias(table, bias, stride):
    keys = bias.shape[1]
    for part in range(bias.shape[2] // 128):
        row = lax.broadcasted_iota(jnp.int32, (keys, 128), 0)
        col = lax.broadcasted_iota(jnp.int32, (keys, 128), 1) + 128 * part
        bucket = jnp.clip(row - stride * col, -(NB // 2), NB // 2 - 1) + NB // 2
        for h in range(H):
            values = jnp.broadcast_to(table[h : h + 1, :], (keys, 128))
            bias[h, :, 128 * part : 128 * part + 128] = low(
                jnp.take_along_axis(values, bucket, axis=1, mode="promise_in_bounds")
            )


def prepare_kernel(me_ref, near_ref, far_ref, *refs):
    outs, tables = refs[:6], refs[6:]
    core = jnp.bitwise_and(me_ref[0], 1)
    chip = lax.shift_right_logical(me_ref[0], 1)
    for table in tables:
        table[...] = jnp.zeros_like(table)
    for d in range(32):
        at = position(chip, d // 2)
        slab = jnp.where(core == d % 2, wide(near_ref[at]), wide(far_ref[at]))
        for layer in range(2):
            vec_ref, wide_ref = outs[3 * layer], outs[3 * layer + 1]
            rows = slab[8 * layer : 8 * layer + 8]
            vec_ref[:, 24 * d : 24 * d + 24] = rows[:, :24]
            wide_ref[:, 96 * d : 96 * d + 96] = rows[0:1, 32:128]
            h, start = 12 * d // NB, 12 * d % NB
            count = min(12, NB - start)
            tables[layer][h : h + 1, start : start + count] = rows[1:2, 32 : 32 + count]
            if count < 12:
                tables[layer][h + 1 : h + 2, 0 : 12 - count] = rows[1:2, 32 + count : 44]
    build_bias(tables[0], outs[2], 2)
    build_bias(tables[1], outs[5], 1)


def prepare(index, near, far, keys, queries):
    sds = jax.ShapeDtypeStruct
    shapes = []
    for length in (keys, queries):
        shapes += [sds((8, D), F32), sds((1, FF), F32), sds((H, length, queries), BF16)]
    return pl.pallas_call(
        prepare_kernel,
        grid_spec=pltpu.PrefetchScalarGridSpec(
            num_scalar_prefetch=1,
            grid=(1,),
            in_specs=[whole(UNITS, 16, 128)] * 2,
            out_specs=[whole(*shape.shape) for shape in shapes],
            scratch_shapes=[pltpu.VMEM((16, 128), F32)] * 2,
        ),
        out_shape=shapes,
        compiler_params=pltpu.CompilerParams(vmem_limit_bytes=VMEM_LIMIT),
        cost_estimate=pl.CostEstimate(flops=10_000_000, bytes_accessed=10_000_000, transcendentals=0),
        name="prepare",
    )(index, near, far)


def vector_slab(vectors_one, wide_one, table_one, vectors_two, wide_two, table_two):
    lead = wide_one.shape[:-1]
    left = jnp.concatenate([vectors_one, vectors_two], axis=-2)
    left = jnp.pad(left, [(0, 0)] * (left.ndim - 1) + [(0, 8)])
    rows = []
    for wide_bias, table in ((wide_one, table_one), (wide_two, table_two)):
        table = jnp.pad(table, [(0, 0)] * len(lead) + [(0, 84)])
        pair = jnp.stack([wide_bias, table], axis=-2)
        rows.append(jnp.pad(pair, [(0, 0)] * len(lead) + [(0, 6), (0, 0)]))
    return jnp.concatenate([left, jnp.concatenate(rows, axis=-2)], axis=-1)


def whole(*shape):
    return pl.BlockSpec(shape, lambda r, *_: (0,) * len(shape))


def lane_masks(value):
    lane = lax.broadcasted_iota(jnp.int32, value.shape, 1)
    zero = jnp.zeros_like(value)
    return jnp.where(lane < HD, value, zero), jnp.where(lane < HD, zero, value)


def masked_scores(keys, query, bias, count):
    scores = mm(keys, query, NT) + wide(bias)
    size = scores.shape[0]
    head, tail = scores[: size - 128], scores[size - 128 :]
    row = lax.broadcasted_iota(jnp.int32, tail.shape, 0) + (size - 128)
    tail = jnp.where(row < count, tail, -1e30)
    return tail if size == 128 else jnp.concatenate([head, tail], axis=0)


def statistics(value):
    mean = jnp.mean(value, axis=-1, keepdims=True)
    centred = value - mean
    spread = jnp.mean(centred * centred, axis=-1, keepdims=True)
    rstd = lax.rsqrt(spread + EPS)
    return centred * rstd, rstd


def norm_pull(grad, unit, rstd):
    return rstd * (
        grad
        - jnp.mean(grad, axis=-1, keepdims=True)
        - unit * jnp.mean(grad * unit, axis=-1, keepdims=True)
    )


def column_sum(value):
    return jnp.sum(value, axis=0, keepdims=True)


def project_kernel(stride, count, len_ref, me_ref, x_ref, vec_ref, *refs):
    sources = refs[:count]
    refs = refs[count:]
    if stride == 2:
        pooled_ref, pooled_low_ref, *refs = refs
    q_ref, k_ref, v_ref, entry, sem = refs
    row = pl.program_id(0)
    keys = x_ref.shape[1]
    queries = q_ref.shape[1]

    @pl.when(row == 0)
    def _():
        start_load(me_ref[0], sources, entry, sem.at[0], place_entry)
        wait_load(entry, sem.at[0])

    length = len_ref[row]
    if stride == 2:
        place = lax.broadcasted_iota(jnp.int32, (queries, keys), 1)
        mine = lax.broadcasted_iota(jnp.int32, (queries, keys), 0)
        pair = jnp.where(lax.shift_right_logical(place, 1) == mine, 0.5, 0.0).astype(BF16)
        pooled = mm(pair, x_ref[0])
        pooled_ref[0] = pooled
        query_in = low(pooled)
        pooled_low_ref[0] = query_in
    else:
        query_in = x_ref[0]
    q_ref[0] = low(wide(low(mm(query_in, entry[0]) + vec_ref[0:1, :])) * HD**-0.5)
    for block in range(keys // 256):

        @pl.when(block * 256 < length)
        def _():
            rows = pl.ds(block * 256, 256)
            x = x_ref[0, rows, :]
            k_ref[0, rows, :] = low(mm(x, entry[1]))
            v_ref[0, rows, :] = low(mm(x, entry[2]) + vec_ref[1:2, :])


def project(stride, index, lengths, x, vectors, sources):
    rows, keys, _ = x.shape
    queries = keys // stride
    blk = lambda *shape: pl.BlockSpec((1,) + shape, lambda r, *_: (r,) + (0,) * len(shape))
    full = lambda *shape: pl.BlockSpec(shape, lambda r, *_: (0,) * len(shape))
    sds = jax.ShapeDtypeStruct
    outs = [
        (sds((rows, queries, D), BF16), blk(queries, D)),
        (sds((rows, keys, D), BF16), blk(keys, D)),
        (sds((rows, keys, D), BF16), blk(keys, D)),
    ]
    if stride == 2:
        outs = [
            (sds((rows, queries, D), F32), blk(queries, D)),
            (sds((rows, queries, D), BF16), blk(queries, D)),
        ] + outs
    return pl.pallas_call(
        partial(project_kernel, stride, len(sources)),
        grid_spec=pltpu.PrefetchScalarGridSpec(
            num_scalar_prefetch=2,
            grid=(rows,),
            in_specs=[blk(keys, D), full(8, D)] + [ANY] * len(sources),
            out_specs=[o[1] for o in outs],
            scratch_shapes=[pltpu.VMEM((3, D, D), BF16), pltpu.SemaphoreType.DMA((1,))],
        ),
        out_shape=[o[0] for o in outs],
        compiler_params=pltpu.CompilerParams(vmem_limit_bytes=VMEM_LIMIT),
        cost_estimate=pl.CostEstimate(
            flops=rows * keys * D * D * 4, bytes_accessed=20_000_000, transcendentals=0
        ),
        name="project",
    )(lengths, index, x, vectors, *sources)


def attend_kernel(base, len_ref, me_ref, q_ref, k_ref, v_ref, bias, *refs):
    ctx_ref, probs_ref, turned = refs[-3:]
    row = pl.program_id(0)
    keys = k_ref.shape[1]
    length = len_ref[row + base]

    def group_step(size, pairs, step, carry):
        made = []
        for p in range(pairs):
            lanes = pl.ds(pl.multiple_of((step * pairs + p) * 128, 128), 128)
            queries_low = lane_masks(q_ref[0, :, lanes])
            key = k_ref[0, :size, lanes]
            value = v_ref[0, :size, lanes].T
            for i in range(2):
                h = 2 * (step * pairs + p) + i
                scores = masked_scores(key, queries_low[i], bias[h, :size, :], length)
                made.append((h, scores, value[HD * i : HD * i + HD]))
        kept = []
        for h, scores, value in made:
            top = jnp.max(scores, axis=0, keepdims=True)
            probs = jnp.exp(scores - top)
            probs = low(probs * (1.0 / jnp.sum(probs, axis=0, keepdims=True)))
            probs_ref[0, h, :size, :] = probs
            kept.append((h, probs, value))
        for h, probs, value in kept:
            turned[pl.ds(pl.multiple_of(HD * h, HD), HD), :] = mm(value, probs)
        return carry

    blocks = lax.div(length + 127, 128)
    for w in range(1, keys // 128 + 1):

        @pl.when(blocks == w)
        def _():
            pairs = GROUPS[w - 1]
            lax.fori_loop(0, H // 2 // pairs, partial(group_step, 128 * w, pairs), 0)

    ctx_ref[0] = low(turned[...].T)


def attend(stride, index, lengths, q, k, v, table, base, count, before=()):
    rows, keys, _ = k.shape
    queries = keys // stride
    blk = lambda *shape: pl.BlockSpec((1,) + shape, lambda r, *_: (r + base,) + (0,) * len(shape))
    full = lambda *shape: pl.BlockSpec(shape, lambda r, *_: (0,) * len(shape))
    sds = jax.ShapeDtypeStruct
    return pl.pallas_call(
        partial(attend_kernel, base),
        grid_spec=pltpu.PrefetchScalarGridSpec(
            num_scalar_prefetch=2,
            grid=(count,),
            in_specs=[blk(queries, D), blk(keys, D), blk(keys, D), full(H, keys, queries)]
            + [ANY] * len(before),
            out_specs=[blk(queries, D), blk(H, keys, queries)],
            scratch_shapes=[pltpu.VMEM((D, queries), F32)],
        ),
        out_shape=[sds((rows, queries, D), BF16), sds((rows, H, keys, queries), BF16)],
        input_output_aliases={6 + i: i for i in range(len(before))},
        compiler_params=pltpu.CompilerParams(vmem_limit_bytes=VMEM_LIMIT),
        cost_estimate=pl.CostEstimate(
            flops=count * keys * queries * D * 8,
            bytes_accessed=20_000_000,
            transcendentals=count * H * keys * queries,
        ),
        name="attend",
    )(lengths, index, q, k, v, table, *before)


def expand_kernel(counts, me_ref, ctx_ref, resid_ref, vec_ref, bias_ref, *refs):
    c1, c2, c3 = counts
    leave_src, widen_src, narrow_src = refs[:c1], refs[c1 : c1 + c2], refs[c1 + c2 : c1 + c2 + c3]
    u_ref, act_ref, slope_ref, before_ref, out_ref, leave, widen, narrow, sem = refs[c1 + c2 + c3 :]
    first = pl.program_id(0) == 0

    @pl.when(first)
    def _():
        start_load(me_ref[0], leave_src, leave, sem.at[0], place_leave)
        start_load(me_ref[0], widen_src, widen, sem.at[1], place_widen)
        start_load(me_ref[0], narrow_src, narrow, sem.at[2], place_narrow)
        wait_load(leave, sem.at[0])

    u = wide(resid_ref[...]) + mm(ctx_ref[...], leave[...]) + vec_ref[2:3, :]
    u_ref[...] = u
    unit, _ = statistics(u)
    mixed = unit * vec_ref[3:4, :] + vec_ref[4:5, :]
    mixed_low = low(mixed)

    @pl.when(first)
    def _():
        wait_load(widen, sem.at[1])
        wait_load(narrow, sem.at[2])

    total = mixed + vec_ref[5:6, :]
    for j in range(4):
        cols = slice(D * j, D * j + D)
        h = mm(mixed_low, widen[j]) + bias_ref[0:1, cols]
        square = h * h
        gate = 0.5 + 0.5 * jnp.tanh(h * (GELU_A + GELU_A * GELU_B * square))
        act = h * gate
        slope = gate + act * (1.0 - gate) * (2.0 * GELU_A + 6.0 * GELU_A * GELU_B * square)
        slope_ref[:, cols] = low(slope)
        act = low(act)
        act_ref[:, cols] = act
        total = total + mm(act, narrow[16 * j : 16 * j + 16].reshape(D, D))
    before_ref[...] = total
    unit, _ = statistics(total)
    out_ref[...] = low(unit * vec_ref[6:7, :] + vec_ref[7:8, :])


def expand(index, ctx, resid, vectors, wide_bias, leave, widen, narrow):
    tokens = ctx.shape[0]
    tile = TILE_A
    blk = lambda width: pl.BlockSpec((tile, width), lambda r, *_: (r, 0))
    full = lambda *shape: pl.BlockSpec(shape, lambda r, *_: (0,) * len(shape))
    sds = jax.ShapeDtypeStruct
    sources = tuple(leave) + tuple(widen) + tuple(narrow)
    return pl.pallas_call(
        partial(expand_kernel, (len(leave), len(widen), len(narrow))),
        grid_spec=pltpu.PrefetchScalarGridSpec(
            num_scalar_prefetch=1,
            grid=(tokens // tile,),
            in_specs=[blk(D), blk(D), full(8, D), full(1, FF)] + [ANY] * len(sources),
            out_specs=[blk(D), blk(FF), blk(FF), blk(D), blk(D)],
            scratch_shapes=[
                pltpu.VMEM((D, D), BF16),
                pltpu.VMEM((4, D, D), BF16),
                pltpu.VMEM((64, 48, D), BF16),
                pltpu.SemaphoreType.DMA((3,)),
            ],
        ),
        out_shape=[
            sds((tokens, D), F32),
            sds((tokens, FF), BF16),
            sds((tokens, FF), BF16),
            sds((tokens, D), F32),
            sds((tokens, D), BF16),
        ],
        compiler_params=pltpu.CompilerParams(vmem_limit_bytes=VMEM_LIMIT),
        cost_estimate=pl.CostEstimate(
            flops=2 * tokens * D * (D + 2 * FF), bytes_accessed=30_000_000, transcendentals=tokens * FF
        ),
        name="expand",
    )(index, ctx, resid, vectors, wide_bias, *sources)


def contract_kernel(counts, me_ref, dz_ref, before_ref, slope_ref, u_ref, vec_ref, *refs):
    c1, c2, c3 = counts
    leave_src, widen_src, narrow_src = refs[:c1], refs[c1 : c1 + c2], refs[c1 + c2 : c1 + c2 + c3]
    refs = refs[c1 + c2 + c3 :]
    dback_ref, mixed_ref, dhid_ref, dattn_ref, du_ref, dctx_ref, dvec_ref, dbias_ref = refs[:8]
    leave, widen, narrow, sem = refs[8:]
    first = pl.program_id(0) == 0

    @pl.when(first)
    def _():
        start_load(me_ref[0], narrow_src, narrow, sem.at[2], place_narrow)
        start_load(me_ref[0], widen_src, widen, sem.at[1], place_widen)
        start_load(me_ref[0], leave_src, leave, sem.at[0], place_leave)
        dvec_ref[...] = jnp.zeros_like(dvec_ref)
        dbias_ref[...] = jnp.zeros_like(dbias_ref)

    dz = wide(dz_ref[...])
    unit, rstd = statistics(before_ref[...])
    dvec_ref[6:7, :] += column_sum(dz * unit)
    dvec_ref[7:8, :] += column_sum(dz)
    dpre = norm_pull(dz * vec_ref[6:7, :], unit, rstd)
    dback = low(dpre)
    dback_ref[...] = dback
    dvec_ref[5:6, :] += column_sum(wide(dback))
    unit, rstd = statistics(u_ref[...])
    mixed_ref[...] = low(unit * vec_ref[3:4, :] + vec_ref[4:5, :])

    @pl.when(first)
    def _():
        wait_load(narrow, sem.at[2])
        wait_load(widen, sem.at[1])
        wait_load(leave, sem.at[0])

    dmixed = dpre
    for j in range(4):
        cols = slice(D * j, D * j + D)
        dact = mm(dback, narrow[16 * j : 16 * j + 16].reshape(D, D), NT)
        dhid = low(dact * wide(slope_ref[:, cols]))
        dhid_ref[:, cols] = dhid
        dbias_ref[:, cols] += column_sum(wide(dhid))
        dmixed = dmixed + mm(dhid, widen[j], NT)
    dvec_ref[3:4, :] += column_sum(dmixed * unit)
    dvec_ref[4:5, :] += column_sum(dmixed)
    du = norm_pull(dmixed * vec_ref[3:4, :], unit, rstd)
    du_ref[...] = du
    dattn = low(du)
    dattn_ref[...] = dattn
    dvec_ref[2:3, :] += column_sum(wide(dattn))
    dctx_ref[...] = low(mm(dattn, leave[...], NT))


def contract(index, dz, before, hidden_units, u, vectors, leave, widen, narrow):
    tokens = dz.shape[0]
    tile = TILE_B
    blk = lambda width: pl.BlockSpec((tile, width), lambda r, *_: (r, 0))
    full = lambda *shape: pl.BlockSpec(shape, lambda r, *_: (0,) * len(shape))
    sds = jax.ShapeDtypeStruct
    sources = tuple(leave) + tuple(widen) + tuple(narrow)
    return pl.pallas_call(
        partial(contract_kernel, (len(leave), len(widen), len(narrow))),
        grid_spec=pltpu.PrefetchScalarGridSpec(
            num_scalar_prefetch=1,
            grid=(tokens // tile,),
            in_specs=[blk(D), blk(D), blk(FF), blk(D), full(8, D)] + [ANY] * len(sources),
            out_specs=[blk(D), blk(D), blk(FF), blk(D), blk(D), blk(D), full(8, D), full(1, FF)],
            scratch_shapes=[
                pltpu.VMEM((D, D), BF16),
                pltpu.VMEM((4, D, D), BF16),
                pltpu.VMEM((64, 48, D), BF16),
                pltpu.SemaphoreType.DMA((3,)),
            ],
        ),
        out_shape=[
            sds((tokens, D), BF16),
            sds((tokens, D), BF16),
            sds((tokens, FF), BF16),
            sds((tokens, D), BF16),
            sds((tokens, D), F32),
            sds((tokens, D), BF16),
            sds((8, D), F32),
            sds((1, FF), F32),
        ],
        compiler_params=pltpu.CompilerParams(vmem_limit_bytes=VMEM_LIMIT),
        cost_estimate=pl.CostEstimate(
            flops=2 * tokens * D * (D + 2 * FF), bytes_accessed=50_000_000, transcendentals=tokens * FF
        ),
        name="contract",
    )(index, dz, before, hidden_units, u, vectors, *sources)


def halves(core, value, width):
    left, right = value[:, :width], value[:, width:]
    first = core == 0
    return jnp.where(first, right, left), jnp.where(first, left, right)


def flush(pairs, start, rows, sem):
    copies = [
        pltpu.make_async_copy(scratch, out_ref.at[:, start : start + rows, :], sem.at[i])
        for i, (scratch, out_ref) in enumerate(pairs)
    ]
    for copy in copies:
        copy.start()
    for copy in copies:
        copy.wait()


def sum_call(kernel, name, total_rows, start, rows, grid, prefetch, inputs, in_specs, scratch, before, flops):
    out = jax.ShapeDtypeStruct((UNITS, total_rows, HALF), BF16)
    return pl.pallas_call(
        partial(kernel, start, rows),
        grid_spec=pltpu.PrefetchScalarGridSpec(
            num_scalar_prefetch=len(prefetch),
            grid=grid,
            in_specs=in_specs + [ANY] * len(before),
            out_specs=[ANY, ANY],
            scratch_shapes=[
                pltpu.VMEM((UNITS, rows, HALF), BF16),
                pltpu.VMEM((UNITS, rows, HALF), BF16),
                pltpu.SemaphoreType.DMA((2,)),
            ]
            + scratch,
        ),
        out_shape=[out, out],
        input_output_aliases={len(prefetch) + len(inputs) + i: i for i in range(len(before))},
        compiler_params=pltpu.CompilerParams(vmem_limit_bytes=VMEM_LIMIT),
        cost_estimate=pl.CostEstimate(flops=flops, bytes_accessed=16_000_000, transcendentals=0),
        name=name,
    )(*prefetch, *inputs, *before)


def narrow_grad_kernel(start, rows, me_ref, act_ref, dback_ref, ctx_ref, dattn_ref, *refs):
    send_out, keep_out, send_ref, keep_ref, sem = refs[-5:]
    step = pl.program_id(0)
    core = jnp.bitwise_and(me_ref[0], 1)
    chip = lax.shift_right_logical(me_ref[0], 1)

    @pl.when(step < 4)
    def _():
        send, keep = halves(core, mm(act_ref[...], dback_ref[...], TN), HALF)
        for i in range(4):
            at = position(chip, step * 4 + i)
            send_ref[at, 0:192, :] = low(send[192 * i : 192 * i + 192])
            keep_ref[at, 0:192, :] = low(keep[192 * i : 192 * i + 192])

    @pl.when(step == 4)
    def _():
        send, keep = halves(core, mm(ctx_ref[...], dattn_ref[...], TN), HALF)
        for i in range(UNITS):
            at = position(chip, i)
            send_ref[at, 192:240, :] = low(send[48 * i : 48 * i + 48])
            keep_ref[at, 192:240, :] = low(keep[48 * i : 48 * i + 48])
        flush(((send_ref, send_out), (keep_ref, keep_out)), start, rows, sem)


def halves(core, value, width):
    left, right = value[:, :width], value[:, width:]
    first = core == 0
    return jnp.where(first, right, left), jnp.where(first, left, right)


def narrow_grad(total_rows, index, act, dback, ctx, dattn):
    tokens = act.shape[0]
    specs = [pl.BlockSpec((tokens, D), lambda r, *_: (0, jnp.minimum(r, 3)))] + [whole(tokens, D)] * 3
    return sum_call(
        narrow_grad_kernel, "narrow_grad", total_rows, 0, 240, (5,), (index,),
        (act, dback, ctx, dattn), specs, [], (), 2 * tokens * D * (D + FF),
    )


def widen_grad_kernel(start, rows, me_ref, mixed_ref, dhid_ref, *refs):
    send_out, keep_out, send_ref, keep_ref, sem, turned = refs[-6:]
    step = pl.program_id(0)
    core = jnp.bitwise_and(me_ref[0], 1)
    chip = lax.shift_right_logical(me_ref[0], 1)

    @pl.when(step == 0)
    def _():
        turned[...] = mixed_ref[...].T

    grad = low(mm(turned[...], dhid_ref[...]))
    mine = lax.div(step, 2) == core
    for part in range(2):

        @pl.when(lax.rem(step, 2) == part)
        def _():
            for wanted, out_ref in ((True, keep_ref), (False, send_ref)):

                @pl.when(mine == wanted)
                def _():
                    for i in range(UNITS):
                        at = position(chip, i)
                        for q in range(2):
                            line = 96 * part + 48 * q
                            out_ref[at, line : line + 48, :] = grad[
                                48 * i : 48 * i + 48, HALF * q : HALF * q + HALF
                            ]

    @pl.when(step == 3)
    def _():
        flush(((send_ref, send_out), (keep_ref, keep_out)), start, rows, sem)


def widen_grad(total_rows, index, mixed_low, dhid, before):
    start = 240 if before else 0
    tokens = mixed_low.shape[0]
    specs = [whole(tokens, D), pl.BlockSpec((tokens, D), lambda r, *_: (0, r))]
    return sum_call(
        widen_grad_kernel, "widen_grad", total_rows, start, 192, (4,), (index,),
        (mixed_low, dhid), specs, [pltpu.VMEM((D, tokens), BF16)], before, 2 * tokens * D * FF,
    )


def entry_grad_kernel(start, rows, len_ref, me_ref, a_ref, b_ref, dq_ref, dk_ref, dv_ref, vec_ref, *refs):
    send_out, keep_out, send_ref, keep_ref, sem, total = refs[-6:]
    row = pl.program_id(0)
    core = jnp.bitwise_and(me_ref[0], 1)
    chip = lax.shift_right_logical(me_ref[0], 1)
    keys = b_ref.shape[1]

    @pl.when(row == 0)
    def _():
        total[...] = jnp.zeros_like(total)

    total[0] += mm(a_ref[0], dq_ref[0], TN)
    for block in range(keys // 256):

        @pl.when(block * 256 < len_ref[row])
        def _():
            lines = pl.ds(block * 256, 256)
            b = b_ref[0, lines, :].T
            total[1] += mm(b, dk_ref[0, lines, :])
            total[2] += mm(b, dv_ref[0, lines, :])

    @pl.when(row == pl.num_programs(0) - 1)
    def _():
        for m in range(3):
            send, keep = halves(core, total[m], HALF)
            for i in range(UNITS):
                at = position(chip, i)
                send_ref[at, 48 * m : 48 * m + 48, :] = low(send[48 * i : 48 * i + 48])
                keep_ref[at, 48 * m : 48 * m + 48, :] = low(keep[48 * i : 48 * i + 48])
        for i in range(UNITS):
            at = position(chip, i)
            send_ref[at, 144:160, :] = vec_ref[i, 1 - core]
            keep_ref[at, 144:160, :] = vec_ref[i, core]
        flush(((send_ref, send_out), (keep_ref, keep_out)), start, rows, sem)


def entry_grad(total_rows, start, index, lengths, a, b, dq, dk, dv, vec, before):
    rows, keys, _ = b.shape
    queries = a.shape[1]
    blk = lambda *shape: pl.BlockSpec((1,) + shape, lambda r, *_: (r,) + (0,) * len(shape))
    specs = [blk(queries, D), blk(keys, D), blk(queries, D), blk(keys, D), blk(keys, D)]
    specs.append(whole(UNITS, 2, 16, HALF))
    return sum_call(
        entry_grad_kernel, "entry_grad", total_rows, start, 160, (rows,), (lengths, index),
        (a, b, dq, dk, dv, vec), specs, [pltpu.VMEM((3, D, D), F32)], before,
        2 * rows * (queries + keys) * D * D,
    )


def retrace_kernel(stride, base, len_ref, me_ref, q_ref, k_ref, v_ref, dctx_ref, probs_ref, *refs):
    dq_ref, dk_ref, dv_ref, dvec_ref, diag_ref, ends_ref, bias_sum, turned = refs[-8:]
    row = pl.program_id(0)
    keys = k_ref.shape[1]
    queries = q_ref.shape[1]
    length = len_ref[row + base]

    @pl.when(row == 0)
    def _():
        bias_sum[...] = jnp.zeros_like(bias_sum)
        dvec_ref[...] = jnp.zeros_like(dvec_ref)

    def group_step(size, pairs, step, carry):
        loaded = []
        for p in range(pairs):
            lanes = pl.ds(pl.multiple_of((step * pairs + p) * 128, 128), 128)
            dctx = lane_masks(dctx_ref[0, :, lanes])
            value = v_ref[0, :size, lanes]
            loaded.append((lanes, dctx, [mm(value, dctx[i], NT) for i in range(2)]))
        made = []
        for p, (lanes, dctx, dprobs) in enumerate(loaded):
            grads, probs = [], []
            for i in range(2):
                h = 2 * (step * pairs + p) + i
                kept = probs_ref[0, h, :size, :]
                prob = wide(kept)
                inner = jnp.sum(prob * dprobs[i], axis=0, keepdims=True)
                inner = inner / jnp.sum(prob, axis=0, keepdims=True)
                grad = low(prob * (dprobs[i] - inner))
                for lane in range(queries // 128):
                    bias_sum[lane, h, :size, :] += wide(grad[:, 128 * lane : 128 * lane + 128])
                grads.append(grad)
                probs.append(kept)
            made.append((lanes, dctx, grads, probs))
        for p, (lanes, dctx, grads, probs) in enumerate(made):
            query = lane_masks(q_ref[0, :, lanes])
            key = k_ref[0, :size, lanes].T
            for i in range(2):
                h = 2 * (step * pairs + p) + i
                turned[pl.ds(pl.multiple_of(HD * h, HD), HD), :] = (
                    mm(key[HD * i : HD * i + HD], grads[i]) * HD**-0.5
                )
            dv_ref[0, :size, lanes] = low(
                mm(jnp.concatenate(probs, axis=1), jnp.concatenate(dctx, axis=0))
            )
            dk_ref[0, :size, lanes] = low(
                mm(jnp.concatenate(grads, axis=1), jnp.concatenate(query, axis=0))
            )
        return carry

    blocks = lax.div(length + 127, 128)
    for w in range(1, keys // 128 + 1):

        @pl.when(blocks == w)
        def _():
            size, pairs = 128 * w, GROUPS[w - 1]
            lax.fori_loop(0, H // 2 // pairs, partial(group_step, size, pairs), 0)
            if size < keys:
                dk_ref[0, size:, :] = jnp.zeros((keys - size, D), BF16)
                dv_ref[0, size:, :] = jnp.zeros((keys - size, D), BF16)
            dvec_ref[1:2, :] += column_sum(wide(dv_ref[0, :size, :]))

    dquery = low(turned[...].T)
    dq_ref[0] = dquery
    dvec_ref[0:1, :] += column_sum(wide(dquery))

    @pl.when(row == pl.num_programs(0) - 1)
    def _():
        ends_ref[...] = jnp.zeros_like(ends_ref)

        def collect(h, carry):
            below = above = jnp.zeros((1, queries), F32)
            for part in range(stride):
                block = jnp.concatenate(
                    [
                        bias_sum[lane, h, pl.ds(part, queries, stride=stride), :]
                        for lane in range(queries // 128)
                    ],
                    axis=1,
                )
                col = lax.broadcasted_iota(jnp.int32, block.shape, 1)
                line = lax.broadcasted_iota(jnp.int32, block.shape, 0)
                place = stride * (line - col) + part
                zero = jnp.zeros_like(block)
                below = below + column_sum(jnp.where(place <= -(NB // 2), block, zero))
                above = above + column_sum(jnp.where(place >= NB // 2 - 1, block, zero))
                inside = jnp.where((place > -(NB // 2)) & (place < NB // 2 - 1), block, zero)
                partial_sum = inside[:8]
                for a in range(1, queries // 8):
                    partial_sum = partial_sum + pltpu.roll(inside[8 * a : 8 * a + 8], queries - 8 * a, 1)
                sub = lax.broadcasted_iota(jnp.int32, partial_sum.shape, 0)
                lined = jnp.where(sub == 0, partial_sum, 0.0)
                for b in range(1, 8):
                    lined = lined + jnp.where(sub == b, pltpu.roll(partial_sum, queries - b, 1), 0.0)
                diag_ref[h, part] = jnp.broadcast_to(column_sum(lined), (8, queries))
            ends_ref[h, 0] = jnp.broadcast_to(below, (8, queries))
            ends_ref[h, 1] = jnp.broadcast_to(above, (8, queries))
            return carry

        lax.fori_loop(0, H, collect, 0)


def retrace(stride, index, lengths, q, k, v, dctx, probs, base, count, before=()):
    rows, keys, _ = k.shape
    queries = q.shape[1]
    blk = lambda *shape: pl.BlockSpec((1,) + shape, lambda r, *_: (r + base,) + (0,) * len(shape))
    full = lambda *shape: pl.BlockSpec(shape, lambda r, *_: (0,) * len(shape))
    sds = jax.ShapeDtypeStruct
    return pl.pallas_call(
        partial(retrace_kernel, stride, base),
        grid_spec=pltpu.PrefetchScalarGridSpec(
            num_scalar_prefetch=2,
            grid=(count,),
            in_specs=[
                blk(queries, D),
                blk(keys, D),
                blk(keys, D),
                blk(queries, D),
                blk(H, keys, queries),
            ]
            + [ANY] * len(before),
            out_specs=[
                blk(queries, D),
                blk(keys, D),
                blk(keys, D),
                full(8, D),
                full(H, stride, 8, queries),
                full(H, 2, 8, queries),
            ],
            scratch_shapes=[
                pltpu.VMEM((queries // 128, H, keys, 128), F32),
                pltpu.VMEM((D, queries), F32),
            ],
        ),
        out_shape=[
            sds((rows, queries, D), BF16),
            sds((rows, keys, D), BF16),
            sds((rows, keys, D), BF16),
            sds((8, D), F32),
            sds((H, stride, 8, queries), F32),
            sds((H, 2, 8, queries), F32),
        ],
        input_output_aliases={7 + i: i for i in range(len(before))},
        compiler_params=pltpu.CompilerParams(vmem_limit_bytes=VMEM_LIMIT),
        cost_estimate=pl.CostEstimate(
            flops=count * keys * queries * D * 10, bytes_accessed=20_000_000, transcendentals=count * H * keys * queries
        ),
        name="retrace",
    )(lengths, index, q, k, v, dctx, probs, *before)


def table_grad(stride, diag, ends):
    queries = diag.shape[-1]
    columns = []
    for bucket in range(NB):
        place = bucket - NB // 2
        if bucket == 0:
            columns.append(jnp.sum(ends[:, 0, 0], axis=-1))
        elif bucket == NB - 1:
            columns.append(jnp.sum(ends[:, 1, 0], axis=-1))
        else:
            part = place % stride
            columns.append(diag[:, part, 0, ((part - place) // stride) % queries])
    return jnp.stack(columns, axis=1).reshape(-1)


def inputs_kernel(stride, base, count, len_ref, me_ref, dq_ref, dk_ref, dv_ref, du_ref, *refs):
    sources = refs[:count]
    out_ref, entry, sem = refs[-3:]
    row = pl.program_id(0)
    keys = dk_ref.shape[1]
    queries = dq_ref.shape[1]

    @pl.when(row == 0)
    def _():
        start_load(me_ref[0], sources, entry, sem.at[0], place_entry)
        wait_load(entry, sem.at[0])

    total = mm(dq_ref[0], entry[0], NT) + du_ref[0]
    if stride == 1:
        out_ref[0] = total + mm(dk_ref[0], entry[1], NT) + mm(dv_ref[0], entry[2], NT)
        return
    total = 0.5 * total
    upper = low(total)
    lower = low(total - wide(upper))
    for block in range(keys // 256):
        rows = pl.ds(block * 256, 256)
        place = lax.broadcasted_iota(jnp.int32, (256, queries), 0) + 256 * block
        mine = lax.broadcasted_iota(jnp.int32, (256, queries), 1)
        pair = jnp.where(lax.shift_right_logical(place, 1) == mine, 1.0, 0.0).astype(BF16)
        spread = mm(pair, upper) + mm(pair, lower)

        @pl.when(block * 256 < len_ref[row + base])
        def _():
            out_ref[0, rows, :] = (
                spread + mm(dk_ref[0, rows, :], entry[1], NT) + mm(dv_ref[0, rows, :], entry[2], NT)
            )

        @pl.when(block * 256 >= len_ref[row + base])
        def _():
            out_ref[0, rows, :] = spread


def input_grads(stride, index, lengths, dq, dk, dv, du, sources, base, count, before=()):
    rows, keys, _ = dk.shape
    queries = dq.shape[1]
    blk = lambda *shape: pl.BlockSpec((1,) + shape, lambda r, *_: (r + base,) + (0,) * len(shape))
    return pl.pallas_call(
        partial(inputs_kernel, stride, base, len(sources)),
        grid_spec=pltpu.PrefetchScalarGridSpec(
            num_scalar_prefetch=2,
            grid=(count,),
            in_specs=[blk(queries, D), blk(keys, D), blk(keys, D), blk(queries, D)] + [ANY] * (len(sources) + len(before)),
            out_specs=blk(keys, D),
            scratch_shapes=[pltpu.VMEM((3, D, D), BF16), pltpu.SemaphoreType.DMA((1,))],
        ),
        out_shape=jax.ShapeDtypeStruct((rows, keys, D), F32),
        input_output_aliases={6 + len(sources) + i: i for i in range(len(before))},
        compiler_params=pltpu.CompilerParams(vmem_limit_bytes=VMEM_LIMIT),
        cost_estimate=pl.CostEstimate(
            flops=2 * count * (queries + keys) * D * D, bytes_accessed=20_000_000, transcendentals=0
        ),
        name="input_grads",
    )(lengths, index, dq, dk, dv, du, *sources, *before)


def vectors_by_unit(dvec, dbias, dtable):
    flat = vector_units(dvec, dbias, dtable, 32)
    return jnp.pad(low(flat), ((0, 0), (0, 16 * HALF - flat.shape[1]))).reshape(UNITS, 2, 16, HALF)


NARROW_CUTS = ((192, 96), (48, 24))
WIDEN_CUTS = ((48, 24),) * 4
FEED_CUTS = NARROW_CUTS + WIDEN_CUTS
ENTRY_CUTS = ((48, 24),) * 3


def join(left, right):
    return jnp.concatenate([left, right], axis=-1)


def feed_shards(left, right):
    widen = jnp.concatenate([left[120:216].reshape(4, 24, HALF), right[120:216].reshape(4, 24, HALF)])
    return (
        join(left[96:120], right[96:120]),
        widen.transpose(1, 0, 2).reshape(24, FF),
        join(left[:96], right[:96]),
    )


def entry_shards(left, right):
    return join(left, right).reshape(3, 24, D)


def absolute_units(pair):
    send, keep = pair
    merged = jnp.stack([keep, send], axis=2)
    rest = merged.shape[1:]
    merged = merged.reshape((4, 4) + rest).transpose(1, 0, 2, 3, 4)
    return wide(merged.reshape((UNITS,) + rest))


def plain_shards(feed, entry):
    feed, entry = absolute_units(feed), absolute_units(entry)
    narrow = feed[:, :192].reshape(FF, D)
    leave = feed[:, 192:240].reshape(D, D)
    widen = feed[:, 240:432].reshape(UNITS, 4, 48, 2, HALF).transpose(0, 2, 3, 1, 4).reshape(D, FF)
    vectors = entry[:, 144:].transpose(0, 2, 1, 3).reshape(32, -1)
    entry = entry[:, :144].reshape(UNITS, 3, 48, D).transpose(1, 0, 2, 3).reshape(3, D, D)
    scatter = lambda value, dim: lax.psum_scatter(value, AX, scatter_dimension=dim, tiled=True)
    rows = vectors.shape[0]
    cut, mid = 8 * D // rows, 8 * D // rows + FF // rows
    last = mid + H * NB // rows
    vec = vectors[:, :cut].reshape(rows, 8, -1).transpose(1, 0, 2).reshape(8, D)
    return (
        scatter(entry, 1),
        scatter(leave, 0),
        scatter(widen, 0),
        scatter(narrow, 0),
        scatter(vec, 1),
        scatter(vectors[:, cut:mid].reshape(-1), 0),
        scatter(vectors[:, mid:last].reshape(-1), 0),
    )


def plain_gather(entry, leave, widen, narrow):
    gather = lambda value, dim: lax.all_gather(value, AX, axis=dim, tiled=True)
    widen = gather(widen, 0).reshape(D, 4, D).transpose(1, 0, 2)
    return (
        (gather(entry, 1),),
        (gather(leave, 0),),
        (widen,),
        (gather(narrow, 0).reshape(64, 48, D),),
    )


def plain_vectors(*small):
    gather = lambda value, dim: lax.all_gather(value, AX, axis=dim, tiled=True)
    parts = []
    for value in small:
        full = gather(value, value.ndim - 1)
        if value.ndim == 2:
            parts.append(full.reshape(8, 32, 24).transpose(1, 0, 2))
        else:
            parts.append(full.reshape(32, -1))
    slabs = vector_slab(*parts).reshape(4, 4, 2, 16, 128).transpose(2, 1, 0, 3, 4)
    return slabs[0].reshape(UNITS, 16, 128), slabs[1].reshape(UNITS, 16, 128)


def on_device(
    devices,
    hidden,
    lengths,
    cotangent,
    inflow,
    outflow,
    widener,
    narrower,
    shifts,
    offsets,
    distance,
    intake,
    outtake,
    expander,
    squeezer,
    adjusts,
    leanings,
    spacing,
):
    rows, seq, width = hidden.shape
    half = seq // 2
    fast = devices == 32
    index = lax.axis_index(AX)
    core = index % 2
    halved = (lengths + 1) // 2
    layer_one = (inflow, outflow, widener, narrower)
    layer_two = (intake, outtake, expander, squeezer)

    small = (shifts, offsets, distance, adjusts, leanings, spacing)
    if fast:
        ticks = Ticks(index.astype(jnp.int32).reshape(1))
        tick = ticks.run
        vec = Job(vector_stages, vector_slab(*small))
        eo1, w1 = gather_jobs(core, (True, None), *layer_one)
        eo2, w2 = gather_jobs(core, (False, False), *layer_two)
        tick([eo1, vec, w1])
        tick([eo1, vec, w1])
        tick([eo1, vec, w1])
        prepared = tick([eo1, w1], lambda me: prepare(me, *vec.result, seq, half))
        tick([eo1, eo2, w2])
    else:
        ticks = Ticks(jnp.zeros((1,), jnp.int32))
        eo1 = w1 = eo2 = w2 = None
        plain_one, plain_two = plain_gather(*layer_one), plain_gather(*layer_two)
        prepared = prepare(ticks.me, *plain_vectors(*small), seq, half)

        def tick(jobs, kernel=None):
            return ticks.run([], kernel)

    def weights(layer, names):
        if fast:
            jobs = {"e": (eo1, eo2), "o": (eo1, eo2), "w": (w1, w2), "n": (w1, w2)}
            return [jobs[name][layer].result for name in names]
        return [(plain_one, plain_two)[layer]["eown".index(name)] for name in names]

    vec1, bias1, tab1, vec2, bias2, tab2 = prepared
    flatten = lambda value: value.reshape(-1, D)
    part = rows // 2

    def begin(stride, me, lens, x, vec_in, layer, tab):
        made = project(stride, me, lens, x, vec_in, *weights(layer, "e"))
        q, k, v = made[-3:]
        return made, attend(stride, me, lens, q, k, v, tab, 0, part)

    def finish(stride, me, lens, made, tab, head):
        return attend(stride, me, lens, *made[-3:], tab, part, rows - part, head)

    made1, head = tick([w1, eo2, w2], lambda me: begin(2, me, lengths, hidden, vec1, 0, tab1))
    ctx1, probs1 = tick([w1, eo2], lambda me: finish(2, me, lengths, made1, tab1, head))
    pooled, pooled_low, q1, k1, v1 = made1
    tick([w1])
    u1, act1, slope1, before1, first_out = tick(
        [eo2, w2],
        lambda me: expand(me, flatten(ctx1), flatten(pooled), vec1, bias1, *weights(0, "own")),
    )
    pooled_layer = first_out.reshape(rows, half, width)

    tick([eo2])
    tick([eo2])
    made2, head = tick([w2], lambda me: begin(1, me, halved, pooled_layer, vec2, 1, tab2))
    ctx2, probs2 = tick([w2], lambda me: finish(1, me, halved, made2, tab2, head))
    q2, k2, v2 = made2
    tick([w2])
    u2, act2, slope2, before2, second_out = tick(
        [], lambda me: expand(me, flatten(ctx2), first_out, vec2, bias2, *weights(1, "own"))
    )

    def reducing(pair, cuts, direct=False):
        return Job(reduce_stages, core, cuts, direct, *pair) if fast else pair

    dback, mixed_low, dhid, dattn, du, dctx, dvec, dbias = tick(
        [],
        lambda me: contract(me, cotangent.reshape(-1, D), before2, slope2, u2, vec2, *weights(1, "own")),
    )

    narrow2 = tick([], lambda me: narrow_grad(240, me, act2, dback, flatten(ctx2), dattn))
    sumn2 = reducing(narrow2, NARROW_CUTS)
    widen2 = tick([sumn2], lambda me: widen_grad(192, me, mixed_low, dhid, ()))
    sumw2 = reducing(widen2, WIDEN_CUTS)
    back = tick(
        [sumn2, sumw2],
        lambda me: retrace(1, me, halved, q2, k2, v2, dctx.reshape(q2.shape), probs2, 0, rows),
    )
    dq, dk, dv, dvec_top, diag, ends = back
    packed = vectors_by_unit(dvec + dvec_top, dbias, table_grad(1, diag, ends))

    def entry_end(me):
        made = entry_grad(160, 0, me, halved, pooled_layer, pooled_layer, dq, dk, dv, packed, ())
        parts = (dq, dk, dv, du.reshape(q2.shape), *weights(1, "e"))
        return made, input_grads(1, me, halved, *parts, 0, rows)

    entry2, dlayer = tick([sumn2, sumw2], entry_end)
    sume2 = reducing(entry2, ENTRY_CUTS)

    dback, mixed_low, dhid, dattn, du, dctx, dvec, dbias = tick(
        [sumw2, sumn2, sume2],
        lambda me: contract(me, flatten(dlayer), before1, slope1, u1, vec1, *weights(0, "own")),
    )
    narrow1 = tick(
        [sumw2, sumn2, sume2], lambda me: narrow_grad(240, me, act1, dback, flatten(ctx1), dattn)
    )
    sumn1 = reducing(narrow1, NARROW_CUTS)
    widen1 = tick([sumn1, sumw2, sume2], lambda me: widen_grad(192, me, mixed_low, dhid, ()))
    sumw1 = reducing(widen1, WIDEN_CUTS)
    parts = (q1, k1, v1, dctx.reshape(q1.shape), probs1)
    head = tick([sumn1, sumw1, sume2, sumn2], lambda me: retrace(2, me, lengths, *parts, 0, part))
    back = tick(
        [sumn1, sumw1, sume2], lambda me: retrace(2, me, lengths, *parts, part, rows - part, head[:3])
    )
    dq, dk, dv = back[:3]
    dvec_top, diag, ends = [one + two for one, two in zip(head[3:], back[3:])]
    packed = vectors_by_unit(dvec + dvec_top, dbias, table_grad(2, diag, ends))
    entry1 = tick(
        [sumw1, sumn1, sumw2],
        lambda me: entry_grad(160, 0, me, lengths, pooled_low, hidden, dq, dk, dv, packed, ()),
    )
    sume1 = reducing(entry1, ENTRY_CUTS, True)
    parts = (dq, dk, dv, du.reshape(q1.shape), *weights(0, "e"))
    ends = (0, 1, 2, rows) if rows > 2 else (0, rows)
    beside = ([sume1, sumn1, sume2], [sume1, sumn1], [sume1, sumw1])
    done = ()
    for first, last, jobs in zip(ends, ends[1:], beside):
        done = (
            tick(
                jobs,
                lambda me: input_grads(2, me, lengths, *parts, first, last - first, done),
            ),
        )
    (hidden_grad,) = done
    if fast:
        for job in (sume1, sumw1, sumn1, sumn2, sumw2, sume2):
            while job.result is None:
                tick([job, sumw1] if job is sume1 else [job])
        left, right, rest = sume2.result
        feed = [jnp.concatenate(sides) for sides in zip(sumn2.result[:2], sumw2.result[:2])]
        shards_two = (entry_shards(left, right),) + feed_shards(*feed)
        shards_two = shards_two + split_vectors(rest.reshape(-1), 32)
        left, right, rest = sume1.result
        feed = [jnp.concatenate(sides) for sides in zip(sumn1.result[:2], sumw1.result[:2])]
        shards_one = (entry_shards(left, right),) + feed_shards(*feed)
        shards_one = shards_one + split_vectors(rest.reshape(-1), 32)
    else:
        feed2 = [jnp.concatenate(sides, axis=1) for sides in zip(narrow2, widen2)]
        feed1 = [jnp.concatenate(sides, axis=1) for sides in zip(narrow1, widen1)]
        shards_one, shards_two = plain_shards(feed1, entry1), plain_shards(feed2, entry2)
    return (
        pooled_layer,
        second_out.reshape(rows, half, width),
        hidden_grad,
        *shards_one,
        *shards_two[:4],
        shards_two[4][1:],
        shards_two[5],
        shards_two[6],
        shards_two[4][0],
    )


def solution(mesh):
    both = ("wide", "narrow")
    rows = P(both, None, None)
    weights = (
        P(None, both, None),
        P(both, None),
        P(both, None),
        P(both, None),
        P(None, both),
        P(both),
        P(both),
    )
    return jax.shard_map(
        partial(on_device, mesh.size),
        mesh=mesh,
        in_specs=(rows, P(both), rows) + weights + weights,
        out_specs=(rows, rows, rows) + weights + weights + (P(both),),
        check_vma=False,
    )
```

```python
from functools import partial

import jax
import jax.numpy as jnp
from jax import lax
from jax.experimental import pallas as pl
from jax.experimental.pallas import tpu as pltpu
from jax.sharding import PartitionSpec as P

H = 12
HD = 64
NB = 32
D = 768
FF = 3072
HALF = 384
EPS = 1e-06
AX = ("wide", "narrow")
CORE, XBIT, YBIT, Z0, Z1 = 1, 2, 4, 8, 16
UNITS = 16
F32 = jnp.float32
BF16 = jnp.bfloat16
GELU_A = 0.7978845608028654
GELU_B = 0.044715
NN = (((1,), (0,)), ((), ()))
NT = (((1,), (1,)), ((), ()))
TN = (((0,), (0,)), ((), ()))
GROUPS = (6, 6, 3, 3)
TILE_A = 256
TILE_B = 256
VMEM_LIMIT = 60 * 1024 * 1024
ANY = pl.BlockSpec(memory_space=pl.ANY)


def mm(left, right, dims=NN):
    return lax.dot_general(left, right, dims, preferred_element_type=F32)


def wide(value):
    return value.astype(F32)


def low(value):
    return value.astype(BF16)


SENT = []


def swap(value, mask):
    SENT.append(value)
    return lax.ppermute(value, AX, [(i, i ^ mask) for i in range(32)])


def pick(core, first, second):
    return jnp.where(core == 0, first, second)


class Job:
    def __init__(self, stages, *operands):
        self.stages = stages(*operands)
        self.operands = next(self.stages)
        self.result = None

    def step(self, operands):
        try:
            self.operands = self.stages.send(operands)
        except StopIteration as stop:
            self.result = stop.value
            self.operands = ()


class Ticks:
    def __init__(self, me):
        self.me = me
        self.last = ()
        self.flying = []

    def run(self, jobs, kernel=None):
        jobs = [job for job in jobs if job.result is None]
        tied = jobs + [job for job in self.flying if job not in jobs]
        operands = [job.operands if job.result is None else job.result for job in tied]
        self.me, operands, self.last = lax.optimization_barrier((self.me, operands, self.last))
        SENT.clear()
        for job, value in zip(tied, operands):
            if job in jobs:
                job.step(value)
            elif job.result is None:
                job.operands = value
            else:
                job.result = value
        self.flying = jobs
        if kernel is None:
            return None
        self.me = lax.optimization_barrier((self.me, list(SENT)))[0]
        out = kernel(self.me)
        self.last = jax.tree.leaves(out)[-1]
        return out


def gather_stages(pair, direct, keep, send):
    keep, send = yield keep, send
    core = lax.axis_index(AX) % 2
    recv = [swap(value, CORE) for value in send]
    first = [pick(core, mine, other) for mine, other in zip(keep, recv)]
    second = [pick(core, other, mine) for mine, other in zip(keep, recv)]
    slab = pair(first, second)
    slab = yield slab
    if direct:
        own = jnp.stack([slab, swap(slab, Z0), swap(slab, Z1), swap(slab, Z0 | Z1)])
    else:
        two = jnp.stack([slab, swap(slab, Z0)])
        two = yield two
        if direct is None:
            far = swap(two[:, :2], Z1)
            two, far = yield two, far
            far = jnp.concatenate([far, swap(two[:, 2:], Z1)], axis=1)
        else:
            far = swap(two, Z1)
        own = jnp.concatenate([two, far])
    own = yield own
    across_y = swap(own, YBIT)
    across_x = swap(own, XBIT)
    far = (swap(own, CORE),)
    own, across_y, across_x, far = yield own, across_y, across_x, far
    diag = (swap(across_y[:2], XBIT), swap(across_x[2:], YBIT))
    far = far + (swap(across_x, CORE), swap(across_y, CORE))
    mine, far = yield (own, across_x, across_y) + diag, far
    return mine + far + tuple(swap(piece, CORE) for piece in mine[3:])


def vector_stages(slab):
    slab = yield slab
    own = jnp.stack([slab, swap(slab, Z0), swap(slab, Z1), swap(slab, Z0 | Z1)])
    own = yield own
    across = [own, swap(own, XBIT), swap(own, YBIT), swap(own, XBIT | YBIT)]
    across = yield across
    near = jnp.concatenate(across)
    return near, swap(near, CORE)


def pair_entry(first, second):
    return jnp.concatenate([first[0], second[0]], axis=1)


def pair_wide(first, second):
    widen = jnp.concatenate([first[0], second[0]], axis=0).reshape(48, 2, D).transpose(1, 0, 2)
    narrow = jnp.concatenate([first[1].reshape(2, 48, HALF), second[1].reshape(2, 48, HALF)], axis=2)
    return jnp.concatenate([widen, narrow], axis=0)


def gather_jobs(core, ways, entry, leave, widen, narrow):
    def halved(*values):
        sides = []
        for side in (core, 1 - core):
            half = lambda value: value.shape[-1] // 2
            sides.append(
                [lax.dynamic_slice_in_dim(v, side * half(v), half(v), axis=-1) for v in values]
            )
        return sides

    eo = jnp.concatenate([entry, leave[None]])
    return (
        Job(gather_stages, pair_entry, ways[0], *halved(eo)),
        Job(gather_stages, pair_wide, ways[1], *halved(widen, narrow)),
    )


def reduce_stages(core, cuts, direct, send, keep):
    shape = (4, 4) + keep.shape[1:]
    send, keep = yield send, keep
    keep = keep.reshape(shape)
    recv = swap(send, CORE).reshape(shape)
    keep, recv = yield keep, recv
    diag_low = swap(low(wide(keep[3, :2]) + wide(recv[3, :2])), XBIT)
    diag_high = swap(low(wide(keep[3, 2:]) + wide(recv[3, 2:])), YBIT)
    keep, recv, diag_low, diag_high = yield keep, recv, diag_low, diag_high
    to_y = wide(keep[2]) + wide(recv[2])
    to_x = wide(keep[1]) + wide(recv[1])
    rest = [(0, 0)] * 2
    to_y = low(to_y + jnp.pad(wide(diag_low), [(0, 2)] + rest))
    to_x = low(to_x + jnp.pad(wide(diag_high), [(2, 0)] + rest))
    from_y, from_x = swap(to_y, YBIT), swap(to_x, XBIT)
    keep, recv, from_y, from_x = yield keep, recv, from_y, from_x

    def part(k):
        return (wide(keep[0, k]) + wide(recv[0, k])) + (wide(from_y[k]) + wide(from_x[k]))

    if direct:
        far = tuple(swap(low(part(k)), mask) for k, mask in ((1, Z0), (2, Z1), (3, Z0 | Z1)))
        keep, recv, from_y, from_x, far = yield keep, recv, from_y, from_x, far
        total = part(0) + wide(far[0]) + wide(far[1]) + wide(far[2])
    else:
        far = swap(jnp.stack([low(part(2)), low(part(3))]), Z1)
        keep, recv, from_y, from_x, far = yield keep, recv, from_y, from_x, far
        near = swap(low(part(1) + wide(far[1])), Z0)
        keep, recv, from_y, from_x, far, near = yield keep, recv, from_y, from_x, far, near
        total = part(0) + wide(far[0]) + wide(near)
    keeps, sends = [], []
    start = 0
    for rows, group in cuts:
        slab = total[start : start + rows].reshape(-1, 2, group, HALF)
        start += rows
        keeps.append(pick(core, slab[:, 0], slab[:, 1]).reshape(-1, HALF))
        sends.append(pick(core, slab[:, 1], slab[:, 0]).reshape(-1, HALF))
    rest = total[start:]
    keep, send = jnp.concatenate(keeps), jnp.concatenate(sends)
    recv = swap(send, CORE)
    return pick(core, keep, recv), pick(core, recv, keep), rest


def vector_units(vectors, wide_bias, table, parts):
    flat = jnp.concatenate(
        [
            vectors.reshape(8, parts, -1).transpose(1, 0, 2).reshape(parts, -1),
            wide_bias.reshape(parts, -1),
            table.reshape(parts, -1),
        ],
        axis=1,
    )
    return flat


def split_vectors(flat, parts):
    cut = 8 * D // parts
    mid = cut + FF // parts
    return flat[:cut].reshape(8, -1), flat[cut:mid], flat[mid : mid + H * NB // parts]


def position(chip, unit):
    rel = jnp.bitwise_xor(chip, unit)
    return jnp.bitwise_and(rel, 3) * 4 + lax.shift_right_logical(rel, 2)


def start_load(me, refs, dst, sem, place):
    if len(refs) == 1:
        pltpu.make_async_copy(refs[0], dst, sem).start()
        return
    chip = lax.shift_right_logical(me, 1)
    for side in range(2):
        half = jnp.bitwise_xor(jnp.bitwise_and(me, 1), side)
        own, across_x, across_y, diag_low, diag_high = refs[5 * side : 5 * side + 5]
        for k in range(4):
            for step, ref, at in (
                (0, own, k),
                (1, across_x, k),
                (2, across_y, k),
                (3, diag_low if k < 2 else diag_high, k % 2),
            ):
                unit = jnp.bitwise_xor(chip, 4 * k + step)
                for source, target in place(ref.at[at], dst, unit, half):
                    pltpu.make_async_copy(source, target, sem).start()


def wait_load(dst, sem):
    pltpu.make_async_copy(dst, dst, sem).wait()


def place_entry(src, dst, unit, half):
    rows, cols = pl.multiple_of(unit * 48, 16), pl.multiple_of(half * HALF, 128)
    return [(src.at[0:3], dst.at[:, pl.ds(rows, 48), pl.ds(cols, HALF)])]


def place_leave(src, dst, unit, half):
    rows, cols = pl.multiple_of(unit * 48, 16), pl.multiple_of(half * HALF, 128)
    return [(src.at[3], dst.at[pl.ds(rows, 48), pl.ds(cols, HALF)])]


def place_widen(src, dst, unit, half):
    rows = pl.multiple_of(unit * 48, 16)
    return [(src.at[0:2], dst.at[pl.ds(half * 2, 2), pl.ds(rows, 48), :])]


def place_narrow(src, dst, unit, half):
    cols = pl.multiple_of(half * HALF, 128)
    return [
        (
            src.at[2:4, :, HALF * g : HALF * g + HALF],
            dst.at[pl.ds(unit * 4 + 2 * g, 2), :, pl.ds(cols, HALF)],
        )
        for g in range(2)
    ]


def build_bias(table, bias, stride):
    keys = bias.shape[1]
    for part in range(bias.shape[2] // 128):
        row = lax.broadcasted_iota(jnp.int32, (keys, 128), 0)
        col = lax.broadcasted_iota(jnp.int32, (keys, 128), 1) + 128 * part
        bucket = jnp.clip(row - stride * col, -(NB // 2), NB // 2 - 1) + NB // 2
        for h in range(H):
            values = jnp.broadcast_to(table[h : h + 1, :], (keys, 128))
            bias[h, :, 128 * part : 128 * part + 128] = low(
                jnp.take_along_axis(values, bucket, axis=1, mode="promise_in_bounds")
            )


def prepare_kernel(me_ref, near_ref, far_ref, *refs):
    outs, tables = refs[:6], refs[6:]
    core = jnp.bitwise_and(me_ref[0], 1)
    chip = lax.shift_right_logical(me_ref[0], 1)
    for table in tables:
        table[...] = jnp.zeros_like(table)
    for d in range(32):
        at = position(chip, d // 2)
        slab = jnp.where(core == d % 2, wide(near_ref[at]), wide(far_ref[at]))
        for layer in range(2):
            vec_ref, wide_ref = outs[3 * layer], outs[3 * layer + 1]
            rows = slab[8 * layer : 8 * layer + 8]
            vec_ref[:, 24 * d : 24 * d + 24] = rows[:, :24]
            wide_ref[:, 96 * d : 96 * d + 96] = rows[0:1, 32:128]
            h, start = 12 * d // NB, 12 * d % NB
            count = min(12, NB - start)
            tables[layer][h : h + 1, start : start + count] = rows[1:2, 32 : 32 + count]
            if count < 12:
                tables[layer][h + 1 : h + 2, 0 : 12 - count] = rows[1:2, 32 + count : 44]
    build_bias(tables[0], outs[2], 2)
    build_bias(tables[1], outs[5], 1)


def prepare(index, near, far, keys, queries):
    sds = jax.ShapeDtypeStruct
    shapes = []
    for length in (keys, queries):
        shapes += [sds((8, D), F32), sds((1, FF), F32), sds((H, length, queries), BF16)]
    return pl.pallas_call(
        prepare_kernel,
        grid_spec=pltpu.PrefetchScalarGridSpec(
            num_scalar_prefetch=1,
            grid=(1,),
            in_specs=[whole(UNITS, 16, 128)] * 2,
            out_specs=[whole(*shape.shape) for shape in shapes],
            scratch_shapes=[pltpu.VMEM((16, 128), F32)] * 2,
        ),
        out_shape=shapes,
        compiler_params=pltpu.CompilerParams(vmem_limit_bytes=VMEM_LIMIT),
        cost_estimate=pl.CostEstimate(flops=10_000_000, bytes_accessed=10_000_000, transcendentals=0),
        name="prepare",
    )(index, near, far)


def vector_slab(vectors_one, wide_one, table_one, vectors_two, wide_two, table_two):
    lead = wide_one.shape[:-1]
    left = jnp.concatenate([vectors_one, vectors_two], axis=-2)
    left = jnp.pad(left, [(0, 0)] * (left.ndim - 1) + [(0, 8)])
    rows = []
    for wide_bias, table in ((wide_one, table_one), (wide_two, table_two)):
        table = jnp.pad(table, [(0, 0)] * len(lead) + [(0, 84)])
        pair = jnp.stack([wide_bias, table], axis=-2)
        rows.append(jnp.pad(pair, [(0, 0)] * len(lead) + [(0, 6), (0, 0)]))
    return jnp.concatenate([left, jnp.concatenate(rows, axis=-2)], axis=-1)


def whole(*shape):
    return pl.BlockSpec(shape, lambda r, *_: (0,) * len(shape))


def lane_masks(value):
    lane = lax.broadcasted_iota(jnp.int32, value.shape, 1)
    zero = jnp.zeros_like(value)
    return jnp.where(lane < HD, value, zero), jnp.where(lane < HD, zero, value)


def masked_scores(keys, query, bias, count):
    scores = mm(keys, query, NT) + wide(bias)
    size = scores.shape[0]
    head, tail = scores[: size - 128], scores[size - 128 :]
    row = lax.broadcasted_iota(jnp.int32, tail.shape, 0) + (size - 128)
    tail = jnp.where(row < count, tail, -1e30)
    return tail if size == 128 else jnp.concatenate([head, tail], axis=0)


def statistics(value):
    mean = jnp.mean(value, axis=-1, keepdims=True)
    centred = value - mean
    spread = jnp.mean(centred * centred, axis=-1, keepdims=True)
    rstd = lax.rsqrt(spread + EPS)
    return centred * rstd, rstd


def norm_pull(grad, unit, rstd):
    return rstd * (
        grad
        - jnp.mean(grad, axis=-1, keepdims=True)
        - unit * jnp.mean(grad * unit, axis=-1, keepdims=True)
    )


def column_sum(value):
    return jnp.sum(value, axis=0, keepdims=True)


def project_kernel(stride, count, len_ref, me_ref, x_ref, vec_ref, *refs):
    sources = refs[:count]
    refs = refs[count:]
    if stride == 2:
        pooled_ref, pooled_low_ref, *refs = refs
    q_ref, k_ref, v_ref, entry, sem = refs
    row = pl.program_id(0)
    keys = x_ref.shape[1]
    queries = q_ref.shape[1]

    @pl.when(row == 0)
    def _():
        start_load(me_ref[0], sources, entry, sem.at[0], place_entry)
        wait_load(entry, sem.at[0])

    length = len_ref[row]
    if stride == 2:
        place = lax.broadcasted_iota(jnp.int32, (queries, keys), 1)
        mine = lax.broadcasted_iota(jnp.int32, (queries, keys), 0)
        pair = jnp.where(lax.shift_right_logical(place, 1) == mine, 0.5, 0.0).astype(BF16)
        pooled = mm(pair, x_ref[0])
        pooled_ref[0] = pooled
        query_in = low(pooled)
        pooled_low_ref[0] = query_in
    else:
        query_in = x_ref[0]
    q_ref[0] = low(wide(low(mm(query_in, entry[0]) + vec_ref[0:1, :])) * HD**-0.5)
    for block in range(keys // 256):

        @pl.when(block * 256 < length)
        def _():
            rows = pl.ds(block * 256, 256)
            x = x_ref[0, rows, :]
            k_ref[0, rows, :] = low(mm(x, entry[1]))
            v_ref[0, rows, :] = low(mm(x, entry[2]) + vec_ref[1:2, :])


def project(stride, index, lengths, x, vectors, sources):
    rows, keys, _ = x.shape
    queries = keys // stride
    blk = lambda *shape: pl.BlockSpec((1,) + shape, lambda r, *_: (r,) + (0,) * len(shape))
    full = lambda *shape: pl.BlockSpec(shape, lambda r, *_: (0,) * len(shape))
    sds = jax.ShapeDtypeStruct
    outs = [
        (sds((rows, queries, D), BF16), blk(queries, D)),
        (sds((rows, keys, D), BF16), blk(keys, D)),
        (sds((rows, keys, D), BF16), blk(keys, D)),
    ]
    if stride == 2:
        outs = [
            (sds((rows, queries, D), F32), blk(queries, D)),
            (sds((rows, queries, D), BF16), blk(queries, D)),
        ] + outs
    return pl.pallas_call(
        partial(project_kernel, stride, len(sources)),
        grid_spec=pltpu.PrefetchScalarGridSpec(
            num_scalar_prefetch=2,
            grid=(rows,),
            in_specs=[blk(keys, D), full(8, D)] + [ANY] * len(sources),
            out_specs=[o[1] for o in outs],
            scratch_shapes=[pltpu.VMEM((3, D, D), BF16), pltpu.SemaphoreType.DMA((1,))],
        ),
        out_shape=[o[0] for o in outs],
        compiler_params=pltpu.CompilerParams(vmem_limit_bytes=VMEM_LIMIT),
        cost_estimate=pl.CostEstimate(
            flops=rows * keys * D * D * 4, bytes_accessed=20_000_000, transcendentals=0
        ),
        name="project",
    )(lengths, index, x, vectors, *sources)


def attend_kernel(base, len_ref, me_ref, q_ref, k_ref, v_ref, bias, *refs):
    ctx_ref, probs_ref, turned = refs[-3:]
    row = pl.program_id(0)
    keys = k_ref.shape[1]
    length = len_ref[row + base]

    def group_step(size, pairs, step, carry):
        made = []
        for p in range(pairs):
            lanes = pl.ds(pl.multiple_of((step * pairs + p) * 128, 128), 128)
            queries_low = lane_masks(q_ref[0, :, lanes])
            key = k_ref[0, :size, lanes]
            value = v_ref[0, :size, lanes].T
            for i in range(2):
                h = 2 * (step * pairs + p) + i
                scores = masked_scores(key, queries_low[i], bias[h, :size, :], length)
                made.append((h, scores, value[HD * i : HD * i + HD]))
        kept = []
        for h, scores, value in made:
            top = jnp.max(scores, axis=0, keepdims=True)
            probs = jnp.exp(scores - top)
            probs = low(probs * (1.0 / jnp.sum(probs, axis=0, keepdims=True)))
            probs_ref[0, h, :size, :] = probs
            kept.append((h, probs, value))
        for h, probs, value in kept:
            turned[pl.ds(pl.multiple_of(HD * h, HD), HD), :] = mm(value, probs)
        return carry

    blocks = lax.div(length + 127, 128)
    for w in range(1, keys // 128 + 1):

        @pl.when(blocks == w)
        def _():
            pairs = GROUPS[w - 1]
            lax.fori_loop(0, H // 2 // pairs, partial(group_step, 128 * w, pairs), 0)

    ctx_ref[0] = low(turned[...].T)


def attend(stride, index, lengths, q, k, v, table, base, count, before=()):
    rows, keys, _ = k.shape
    queries = keys // stride
    blk = lambda *shape: pl.BlockSpec((1,) + shape, lambda r, *_: (r + base,) + (0,) * len(shape))
    full = lambda *shape: pl.BlockSpec(shape, lambda r, *_: (0,) * len(shape))
    sds = jax.ShapeDtypeStruct
    return pl.pallas_call(
        partial(attend_kernel, base),
        grid_spec=pltpu.PrefetchScalarGridSpec(
            num_scalar_prefetch=2,
            grid=(count,),
            in_specs=[blk(queries, D), blk(keys, D), blk(keys, D), full(H, keys, queries)]
            + [ANY] * len(before),
            out_specs=[blk(queries, D), blk(H, keys, queries)],
            scratch_shapes=[pltpu.VMEM((D, queries), F32)],
        ),
        out_shape=[sds((rows, queries, D), BF16), sds((rows, H, keys, queries), BF16)],
        input_output_aliases={6 + i: i for i in range(len(before))},
        compiler_params=pltpu.CompilerParams(vmem_limit_bytes=VMEM_LIMIT),
        cost_estimate=pl.CostEstimate(
            flops=count * keys * queries * D * 8,
            bytes_accessed=20_000_000,
            transcendentals=count * H * keys * queries,
        ),
        name="attend",
    )(lengths, index, q, k, v, table, *before)


def expand_kernel(counts, me_ref, ctx_ref, resid_ref, vec_ref, bias_ref, *refs):
    c1, c2, c3 = counts
    leave_src, widen_src, narrow_src = refs[:c1], refs[c1 : c1 + c2], refs[c1 + c2 : c1 + c2 + c3]
    u_ref, act_ref, slope_ref, before_ref, out_ref, leave, widen, narrow, sem = refs[c1 + c2 + c3 :]
    first = pl.program_id(0) == 0

    @pl.when(first)
    def _():
        start_load(me_ref[0], leave_src, leave, sem.at[0], place_leave)
        start_load(me_ref[0], widen_src, widen, sem.at[1], place_widen)
        start_load(me_ref[0], narrow_src, narrow, sem.at[2], place_narrow)
        wait_load(leave, sem.at[0])

    u = wide(resid_ref[...]) + mm(ctx_ref[...], leave[...]) + vec_ref[2:3, :]
    u_ref[...] = u
    unit, _ = statistics(u)
    mixed = unit * vec_ref[3:4, :] + vec_ref[4:5, :]
    mixed_low = low(mixed)

    @pl.when(first)
    def _():
        wait_load(widen, sem.at[1])
        wait_load(narrow, sem.at[2])

    total = mixed + vec_ref[5:6, :]
    for j in range(4):
        cols = slice(D * j, D * j + D)
        h = mm(mixed_low, widen[j]) + bias_ref[0:1, cols]
        square = h * h
        gate = 0.5 + 0.5 * jnp.tanh(h * (GELU_A + GELU_A * GELU_B * square))
        act = h * gate
        slope = gate + act * (1.0 - gate) * (2.0 * GELU_A + 6.0 * GELU_A * GELU_B * square)
        slope_ref[:, cols] = low(slope)
        act = low(act)
        act_ref[:, cols] = act
        total = total + mm(act, narrow[16 * j : 16 * j + 16].reshape(D, D))
    before_ref[...] = total
    unit, _ = statistics(total)
    out_ref[...] = low(unit * vec_ref[6:7, :] + vec_ref[7:8, :])


def expand(index, ctx, resid, vectors, wide_bias, leave, widen, narrow):
    tokens = ctx.shape[0]
    tile = TILE_A
    blk = lambda width: pl.BlockSpec((tile, width), lambda r, *_: (r, 0))
    full = lambda *shape: pl.BlockSpec(shape, lambda r, *_: (0,) * len(shape))
    sds = jax.ShapeDtypeStruct
    sources = tuple(leave) + tuple(widen) + tuple(narrow)
    return pl.pallas_call(
        partial(expand_kernel, (len(leave), len(widen), len(narrow))),
        grid_spec=pltpu.PrefetchScalarGridSpec(
            num_scalar_prefetch=1,
            grid=(tokens // tile,),
            in_specs=[blk(D), blk(D), full(8, D), full(1, FF)] + [ANY] * len(sources),
            out_specs=[blk(D), blk(FF), blk(FF), blk(D), blk(D)],
            scratch_shapes=[
                pltpu.VMEM((D, D), BF16),
                pltpu.VMEM((4, D, D), BF16),
                pltpu.VMEM((64, 48, D), BF16),
                pltpu.SemaphoreType.DMA((3,)),
            ],
        ),
        out_shape=[
            sds((tokens, D), F32),
            sds((tokens, FF), BF16),
            sds((tokens, FF), BF16),
            sds((tokens, D), F32),
            sds((tokens, D), BF16),
        ],
        compiler_params=pltpu.CompilerParams(vmem_limit_bytes=VMEM_LIMIT),
        cost_estimate=pl.CostEstimate(
            flops=2 * tokens * D * (D + 2 * FF), bytes_accessed=30_000_000, transcendentals=tokens * FF
        ),
        name="expand",
    )(index, ctx, resid, vectors, wide_bias, *sources)


def contract_kernel(counts, me_ref, dz_ref, before_ref, slope_ref, u_ref, vec_ref, *refs):
    c1, c2, c3 = counts
    leave_src, widen_src, narrow_src = refs[:c1], refs[c1 : c1 + c2], refs[c1 + c2 : c1 + c2 + c3]
    refs = refs[c1 + c2 + c3 :]
    dback_ref, mixed_ref, dhid_ref, dattn_ref, dctx_ref, dvec_ref, dbias_ref = refs[:7]
    leave, widen, narrow, sem = refs[7:]
    first = pl.program_id(0) == 0

    @pl.when(first)
    def _():
        start_load(me_ref[0], narrow_src, narrow, sem.at[2], place_narrow)
        start_load(me_ref[0], widen_src, widen, sem.at[1], place_widen)
        start_load(me_ref[0], leave_src, leave, sem.at[0], place_leave)
        dvec_ref[...] = jnp.zeros_like(dvec_ref)
        dbias_ref[...] = jnp.zeros_like(dbias_ref)

    dz = wide(dz_ref[...])
    unit, rstd = statistics(before_ref[...])
    dvec_ref[6:7, :] += column_sum(dz * unit)
    dvec_ref[7:8, :] += column_sum(dz)
    dpre = norm_pull(dz * vec_ref[6:7, :], unit, rstd)
    dback = low(dpre)
    dback_ref[...] = dback
    dvec_ref[5:6, :] += column_sum(wide(dback))
    unit, rstd = statistics(u_ref[...])
    mixed_ref[...] = low(unit * vec_ref[3:4, :] + vec_ref[4:5, :])

    @pl.when(first)
    def _():
        wait_load(narrow, sem.at[2])
        wait_load(widen, sem.at[1])
        wait_load(leave, sem.at[0])

    dmixed = dpre
    for j in range(4):
        cols = slice(D * j, D * j + D)
        dact = mm(dback, narrow[16 * j : 16 * j + 16].reshape(D, D), NT)
        dhid = low(dact * wide(slope_ref[:, cols]))
        dhid_ref[:, cols] = dhid
        dbias_ref[:, cols] += column_sum(wide(dhid))
        dmixed = dmixed + mm(dhid, widen[j], NT)
    dvec_ref[3:4, :] += column_sum(dmixed * unit)
    dvec_ref[4:5, :] += column_sum(dmixed)
    du = norm_pull(dmixed * vec_ref[3:4, :], unit, rstd)
    dattn = low(du)
    dattn_ref[...] = dattn
    dvec_ref[2:3, :] += column_sum(wide(dattn))
    dctx_ref[...] = low(mm(dattn, leave[...], NT))


def contract(index, dz, before, hidden_units, u, vectors, leave, widen, narrow):
    tokens = dz.shape[0]
    tile = TILE_B
    blk = lambda width: pl.BlockSpec((tile, width), lambda r, *_: (r, 0))
    full = lambda *shape: pl.BlockSpec(shape, lambda r, *_: (0,) * len(shape))
    sds = jax.ShapeDtypeStruct
    sources = tuple(leave) + tuple(widen) + tuple(narrow)
    return pl.pallas_call(
        partial(contract_kernel, (len(leave), len(widen), len(narrow))),
        grid_spec=pltpu.PrefetchScalarGridSpec(
            num_scalar_prefetch=1,
            grid=(tokens // tile,),
            in_specs=[blk(D), blk(D), blk(FF), blk(D), full(8, D)] + [ANY] * len(sources),
            out_specs=[blk(D), blk(D), blk(FF), blk(D), blk(D), full(8, D), full(1, FF)],
            scratch_shapes=[
                pltpu.VMEM((D, D), BF16),
                pltpu.VMEM((4, D, D), BF16),
                pltpu.VMEM((64, 48, D), BF16),
                pltpu.SemaphoreType.DMA((3,)),
            ],
        ),
        out_shape=[
            sds((tokens, D), BF16),
            sds((tokens, D), BF16),
            sds((tokens, FF), BF16),
            sds((tokens, D), BF16),
            sds((tokens, D), BF16),
            sds((8, D), F32),
            sds((1, FF), F32),
        ],
        compiler_params=pltpu.CompilerParams(vmem_limit_bytes=VMEM_LIMIT),
        cost_estimate=pl.CostEstimate(
            flops=2 * tokens * D * (D + 2 * FF), bytes_accessed=50_000_000, transcendentals=tokens * FF
        ),
        name="contract",
    )(index, dz, before, hidden_units, u, vectors, *sources)


def halves(core, value, width):
    left, right = value[:, :width], value[:, width:]
    first = core == 0
    return jnp.where(first, right, left), jnp.where(first, left, right)


def flush(pairs, start, rows, sem):
    copies = [
        pltpu.make_async_copy(scratch, out_ref.at[:, start : start + rows, :], sem.at[i])
        for i, (scratch, out_ref) in enumerate(pairs)
    ]
    for copy in copies:
        copy.start()
    for copy in copies:
        copy.wait()


def sum_call(kernel, name, total_rows, start, rows, grid, prefetch, inputs, in_specs, scratch, before, flops):
    out = jax.ShapeDtypeStruct((UNITS, total_rows, HALF), BF16)
    return pl.pallas_call(
        partial(kernel, start, rows),
        grid_spec=pltpu.PrefetchScalarGridSpec(
            num_scalar_prefetch=len(prefetch),
            grid=grid,
            in_specs=in_specs + [ANY] * len(before),
            out_specs=[ANY, ANY],
            scratch_shapes=[
                pltpu.VMEM((UNITS, rows, HALF), BF16),
                pltpu.VMEM((UNITS, rows, HALF), BF16),
                pltpu.SemaphoreType.DMA((2,)),
            ]
            + scratch,
        ),
        out_shape=[out, out],
        input_output_aliases={len(prefetch) + len(inputs) + i: i for i in range(len(before))},
        compiler_params=pltpu.CompilerParams(vmem_limit_bytes=VMEM_LIMIT),
        cost_estimate=pl.CostEstimate(flops=flops, bytes_accessed=16_000_000, transcendentals=0),
        name=name,
    )(*prefetch, *inputs, *before)


def narrow_grad_kernel(start, rows, me_ref, act_ref, dback_ref, ctx_ref, dattn_ref, *refs):
    send_out, keep_out, send_ref, keep_ref, sem = refs[-5:]
    step = pl.program_id(0)
    core = jnp.bitwise_and(me_ref[0], 1)
    chip = lax.shift_right_logical(me_ref[0], 1)

    @pl.when(step < 4)
    def _():
        send, keep = halves(core, mm(act_ref[...], dback_ref[...], TN), HALF)
        for i in range(4):
            at = position(chip, step * 4 + i)
            send_ref[at, 0:192, :] = low(send[192 * i : 192 * i + 192])
            keep_ref[at, 0:192, :] = low(keep[192 * i : 192 * i + 192])

    @pl.when(step == 4)
    def _():
        send, keep = halves(core, mm(ctx_ref[...], dattn_ref[...], TN), HALF)
        for i in range(UNITS):
            at = position(chip, i)
            send_ref[at, 192:240, :] = low(send[48 * i : 48 * i + 48])
            keep_ref[at, 192:240, :] = low(keep[48 * i : 48 * i + 48])
        flush(((send_ref, send_out), (keep_ref, keep_out)), start, rows, sem)


def halves(core, value, width):
    left, right = value[:, :width], value[:, width:]
    first = core == 0
    return jnp.where(first, right, left), jnp.where(first, left, right)


def narrow_grad(total_rows, index, act, dback, ctx, dattn):
    tokens = act.shape[0]
    specs = [pl.BlockSpec((tokens, D), lambda r, *_: (0, jnp.minimum(r, 3)))] + [whole(tokens, D)] * 3
    return sum_call(
        narrow_grad_kernel, "narrow_grad", total_rows, 0, 240, (5,), (index,),
        (act, dback, ctx, dattn), specs, [], (), 2 * tokens * D * (D + FF),
    )


def widen_grad_kernel(start, rows, me_ref, mixed_ref, dhid_ref, *refs):
    send_out, keep_out, send_ref, keep_ref, sem, turned = refs[-6:]
    step = pl.program_id(0)
    core = jnp.bitwise_and(me_ref[0], 1)
    chip = lax.shift_right_logical(me_ref[0], 1)

    @pl.when(step == 0)
    def _():
        turned[...] = mixed_ref[...].T

    grad = low(mm(turned[...], dhid_ref[...]))
    mine = lax.div(step, 2) == core
    for part in range(2):

        @pl.when(lax.rem(step, 2) == part)
        def _():
            for wanted, out_ref in ((True, keep_ref), (False, send_ref)):

                @pl.when(mine == wanted)
                def _():
                    for i in range(UNITS):
                        at = position(chip, i)
                        for q in range(2):
                            line = 96 * part + 48 * q
                            out_ref[at, line : line + 48, :] = grad[
                                48 * i : 48 * i + 48, HALF * q : HALF * q + HALF
                            ]

    @pl.when(step == 3)
    def _():
        flush(((send_ref, send_out), (keep_ref, keep_out)), start, rows, sem)


def widen_grad(total_rows, index, mixed_low, dhid, before):
    start = 240 if before else 0
    tokens = mixed_low.shape[0]
    specs = [whole(tokens, D), pl.BlockSpec((tokens, D), lambda r, *_: (0, r))]
    return sum_call(
        widen_grad_kernel, "widen_grad", total_rows, start, 192, (4,), (index,),
        (mixed_low, dhid), specs, [pltpu.VMEM((D, tokens), BF16)], before, 2 * tokens * D * FF,
    )


def entry_grad_kernel(start, rows, len_ref, me_ref, a_ref, b_ref, dq_ref, dk_ref, dv_ref, vec_ref, *refs):
    send_out, keep_out, send_ref, keep_ref, sem, total = refs[-6:]
    row = pl.program_id(0)
    core = jnp.bitwise_and(me_ref[0], 1)
    chip = lax.shift_right_logical(me_ref[0], 1)
    keys = b_ref.shape[1]

    @pl.when(row == 0)
    def _():
        total[...] = jnp.zeros_like(total)

    total[0] += mm(a_ref[0], dq_ref[0], TN)
    for block in range(keys // 256):

        @pl.when(block * 256 < len_ref[row])
        def _():
            lines = pl.ds(block * 256, 256)
            b = b_ref[0, lines, :].T
            total[1] += mm(b, dk_ref[0, lines, :])
            total[2] += mm(b, dv_ref[0, lines, :])

    @pl.when(row == pl.num_programs(0) - 1)
    def _():
        for m in range(3):
            send, keep = halves(core, total[m], HALF)
            for i in range(UNITS):
                at = position(chip, i)
                send_ref[at, 48 * m : 48 * m + 48, :] = low(send[48 * i : 48 * i + 48])
                keep_ref[at, 48 * m : 48 * m + 48, :] = low(keep[48 * i : 48 * i + 48])
        for i in range(UNITS):
            at = position(chip, i)
            send_ref[at, 144:160, :] = vec_ref[i, 1 - core]
            keep_ref[at, 144:160, :] = vec_ref[i, core]
        flush(((send_ref, send_out), (keep_ref, keep_out)), start, rows, sem)


def entry_grad(total_rows, start, index, lengths, a, b, dq, dk, dv, vec, before):
    rows, keys, _ = b.shape
    queries = a.shape[1]
    blk = lambda *shape: pl.BlockSpec((1,) + shape, lambda r, *_: (r,) + (0,) * len(shape))
    specs = [blk(queries, D), blk(keys, D), blk(queries, D), blk(keys, D), blk(keys, D)]
    specs.append(whole(UNITS, 2, 16, HALF))
    return sum_call(
        entry_grad_kernel, "entry_grad", total_rows, start, 160, (rows,), (lengths, index),
        (a, b, dq, dk, dv, vec), specs, [pltpu.VMEM((3, D, D), F32)], before,
        2 * rows * (queries + keys) * D * D,
    )


def retrace_kernel(stride, base, len_ref, me_ref, q_ref, k_ref, v_ref, dctx_ref, probs_ref, *refs):
    dq_ref, dk_ref, dv_ref, dvec_ref, diag_ref, ends_ref, bias_sum, turned = refs[-8:]
    row = pl.program_id(0)
    keys = k_ref.shape[1]
    queries = q_ref.shape[1]
    length = len_ref[row + base]

    @pl.when(row == 0)
    def _():
        bias_sum[...] = jnp.zeros_like(bias_sum)
        dvec_ref[...] = jnp.zeros_like(dvec_ref)

    def group_step(size, pairs, step, carry):
        loaded = []
        for p in range(pairs):
            lanes = pl.ds(pl.multiple_of((step * pairs + p) * 128, 128), 128)
            dctx = lane_masks(dctx_ref[0, :, lanes])
            value = v_ref[0, :size, lanes]
            loaded.append((lanes, dctx, [mm(value, dctx[i], NT) for i in range(2)]))
        made = []
        for p, (lanes, dctx, dprobs) in enumerate(loaded):
            grads, probs = [], []
            for i in range(2):
                h = 2 * (step * pairs + p) + i
                kept = probs_ref[0, h, :size, :]
                prob = wide(kept)
                inner = jnp.sum(prob * dprobs[i], axis=0, keepdims=True)
                inner = inner / jnp.sum(prob, axis=0, keepdims=True)
                grad = low(prob * (dprobs[i] - inner))
                for lane in range(queries // 128):
                    bias_sum[lane, h, :size, :] += wide(grad[:, 128 * lane : 128 * lane + 128])
                grads.append(grad)
                probs.append(kept)
            made.append((lanes, dctx, grads, probs))
        for p, (lanes, dctx, grads, probs) in enumerate(made):
            query = lane_masks(q_ref[0, :, lanes])
            key = k_ref[0, :size, lanes].T
            for i in range(2):
                h = 2 * (step * pairs + p) + i
                turned[pl.ds(pl.multiple_of(HD * h, HD), HD), :] = (
                    mm(key[HD * i : HD * i + HD], grads[i]) * HD**-0.5
                )
            dv_ref[0, :size, lanes] = low(
                mm(jnp.concatenate(probs, axis=1), jnp.concatenate(dctx, axis=0))
            )
            dk_ref[0, :size, lanes] = low(
                mm(jnp.concatenate(grads, axis=1), jnp.concatenate(query, axis=0))
            )
        return carry

    blocks = lax.div(length + 127, 128)
    for w in range(1, keys // 128 + 1):

        @pl.when(blocks == w)
        def _():
            size, pairs = 128 * w, GROUPS[w - 1]
            lax.fori_loop(0, H // 2 // pairs, partial(group_step, size, pairs), 0)
            if size < keys:
                dk_ref[0, size:, :] = jnp.zeros((keys - size, D), BF16)
                dv_ref[0, size:, :] = jnp.zeros((keys - size, D), BF16)
            dvec_ref[1:2, :] += column_sum(wide(dv_ref[0, :size, :]))

    dquery = low(turned[...].T)
    dq_ref[0] = dquery
    dvec_ref[0:1, :] += column_sum(wide(dquery))

    @pl.when(row == pl.num_programs(0) - 1)
    def _():
        ends_ref[...] = jnp.zeros_like(ends_ref)

        def collect(h, carry):
            below = above = jnp.zeros((1, queries), F32)
            for part in range(stride):
                block = jnp.concatenate(
                    [
                        bias_sum[lane, h, pl.ds(part, queries, stride=stride), :]
                        for lane in range(queries // 128)
                    ],
                    axis=1,
                )
                col = lax.broadcasted_iota(jnp.int32, block.shape, 1)
                line = lax.broadcasted_iota(jnp.int32, block.shape, 0)
                place = stride * (line - col) + part
                zero = jnp.zeros_like(block)
                below = below + column_sum(jnp.where(place <= -(NB // 2), block, zero))
                above = above + column_sum(jnp.where(place >= NB // 2 - 1, block, zero))
                inside = jnp.where((place > -(NB // 2)) & (place < NB // 2 - 1), block, zero)
                partial_sum = inside[:8]
                for a in range(1, queries // 8):
                    partial_sum = partial_sum + pltpu.roll(inside[8 * a : 8 * a + 8], queries - 8 * a, 1)
                sub = lax.broadcasted_iota(jnp.int32, partial_sum.shape, 0)
                lined = jnp.where(sub == 0, partial_sum, 0.0)
                for b in range(1, 8):
                    lined = lined + jnp.where(sub == b, pltpu.roll(partial_sum, queries - b, 1), 0.0)
                diag_ref[h, part] = jnp.broadcast_to(column_sum(lined), (8, queries))
            ends_ref[h, 0] = jnp.broadcast_to(below, (8, queries))
            ends_ref[h, 1] = jnp.broadcast_to(above, (8, queries))
            return carry

        lax.fori_loop(0, H, collect, 0)


def retrace(stride, index, lengths, q, k, v, dctx, probs, base, count, before=()):
    rows, keys, _ = k.shape
    queries = q.shape[1]
    blk = lambda *shape: pl.BlockSpec((1,) + shape, lambda r, *_: (r + base,) + (0,) * len(shape))
    full = lambda *shape: pl.BlockSpec(shape, lambda r, *_: (0,) * len(shape))
    sds = jax.ShapeDtypeStruct
    return pl.pallas_call(
        partial(retrace_kernel, stride, base),
        grid_spec=pltpu.PrefetchScalarGridSpec(
            num_scalar_prefetch=2,
            grid=(count,),
            in_specs=[
                blk(queries, D),
                blk(keys, D),
                blk(keys, D),
                blk(queries, D),
                blk(H, keys, queries),
            ]
            + [ANY] * len(before),
            out_specs=[
                blk(queries, D),
                blk(keys, D),
                blk(keys, D),
                full(8, D),
                full(H, stride, 8, queries),
                full(H, 2, 8, queries),
            ],
            scratch_shapes=[
                pltpu.VMEM((queries // 128, H, keys, 128), F32),
                pltpu.VMEM((D, queries), F32),
            ],
        ),
        out_shape=[
            sds((rows, queries, D), BF16),
            sds((rows, keys, D), BF16),
            sds((rows, keys, D), BF16),
            sds((8, D), F32),
            sds((H, stride, 8, queries), F32),
            sds((H, 2, 8, queries), F32),
        ],
        input_output_aliases={7 + i: i for i in range(len(before))},
        compiler_params=pltpu.CompilerParams(vmem_limit_bytes=VMEM_LIMIT),
        cost_estimate=pl.CostEstimate(
            flops=count * keys * queries * D * 10, bytes_accessed=20_000_000, transcendentals=count * H * keys * queries
        ),
        name="retrace",
    )(lengths, index, q, k, v, dctx, probs, *before)


def table_grad(stride, diag, ends):
    queries = diag.shape[-1]
    columns = []
    for bucket in range(NB):
        place = bucket - NB // 2
        if bucket == 0:
            columns.append(jnp.sum(ends[:, 0, 0], axis=-1))
        elif bucket == NB - 1:
            columns.append(jnp.sum(ends[:, 1, 0], axis=-1))
        else:
            part = place % stride
            columns.append(diag[:, part, 0, ((part - place) // stride) % queries])
    return jnp.stack(columns, axis=1).reshape(-1)


def inputs_kernel(stride, base, count, len_ref, me_ref, dq_ref, dk_ref, dv_ref, du_ref, *refs):
    sources = refs[:count]
    out_ref, entry, sem = refs[-3:]
    row = pl.program_id(0)
    keys = dk_ref.shape[1]
    queries = dq_ref.shape[1]

    @pl.when(row == 0)
    def _():
        start_load(me_ref[0], sources, entry, sem.at[0], place_entry)
        wait_load(entry, sem.at[0])

    total = mm(dq_ref[0], entry[0], NT) + wide(du_ref[0])
    if stride == 1:
        out_ref[0] = total + mm(dk_ref[0], entry[1], NT) + mm(dv_ref[0], entry[2], NT)
        return
    total = 0.5 * total
    upper = low(total)
    lower = low(total - wide(upper))
    for block in range(keys // 256):
        rows = pl.ds(block * 256, 256)
        place = lax.broadcasted_iota(jnp.int32, (256, queries), 0) + 256 * block
        mine = lax.broadcasted_iota(jnp.int32, (256, queries), 1)
        pair = jnp.where(lax.shift_right_logical(place, 1) == mine, 1.0, 0.0).astype(BF16)
        spread = mm(pair, upper) + mm(pair, lower)

        @pl.when(block * 256 < len_ref[row + base])
        def _():
            out_ref[0, rows, :] = (
                spread + mm(dk_ref[0, rows, :], entry[1], NT) + mm(dv_ref[0, rows, :], entry[2], NT)
            )

        @pl.when(block * 256 >= len_ref[row + base])
        def _():
            out_ref[0, rows, :] = spread


def input_grads(stride, index, lengths, dq, dk, dv, du, sources, base, count, before=()):
    rows, keys, _ = dk.shape
    queries = dq.shape[1]
    blk = lambda *shape: pl.BlockSpec((1,) + shape, lambda r, *_: (r + base,) + (0,) * len(shape))
    return pl.pallas_call(
        partial(inputs_kernel, stride, base, len(sources)),
        grid_spec=pltpu.PrefetchScalarGridSpec(
            num_scalar_prefetch=2,
            grid=(count,),
            in_specs=[blk(queries, D), blk(keys, D), blk(keys, D), blk(queries, D)] + [ANY] * (len(sources) + len(before)),
            out_specs=blk(keys, D),
            scratch_shapes=[pltpu.VMEM((3, D, D), BF16), pltpu.SemaphoreType.DMA((1,))],
        ),
        out_shape=jax.ShapeDtypeStruct((rows, keys, D), F32),
        input_output_aliases={6 + len(sources) + i: i for i in range(len(before))},
        compiler_params=pltpu.CompilerParams(vmem_limit_bytes=VMEM_LIMIT),
        cost_estimate=pl.CostEstimate(
            flops=2 * count * (queries + keys) * D * D, bytes_accessed=20_000_000, transcendentals=0
        ),
        name="input_grads",
    )(lengths, index, dq, dk, dv, du, *sources, *before)


def vectors_by_unit(dvec, dbias, dtable):
    flat = vector_units(dvec, dbias, dtable, 32)
    return jnp.pad(low(flat), ((0, 0), (0, 16 * HALF - flat.shape[1]))).reshape(UNITS, 2, 16, HALF)


NARROW_CUTS = ((192, 96), (48, 24))
WIDEN_CUTS = ((48, 24),) * 4
FEED_CUTS = NARROW_CUTS + WIDEN_CUTS
ENTRY_CUTS = ((48, 24),) * 3


def join(left, right):
    return jnp.concatenate([left, right], axis=-1)


def feed_shards(left, right):
    widen = jnp.concatenate([left[120:216].reshape(4, 24, HALF), right[120:216].reshape(4, 24, HALF)])
    return (
        join(left[96:120], right[96:120]),
        widen.transpose(1, 0, 2).reshape(24, FF),
        join(left[:96], right[:96]),
    )


def entry_shards(left, right):
    return join(left, right).reshape(3, 24, D)


def absolute_units(pair):
    send, keep = pair
    merged = jnp.stack([keep, send], axis=2)
    rest = merged.shape[1:]
    merged = merged.reshape((4, 4) + rest).transpose(1, 0, 2, 3, 4)
    return wide(merged.reshape((UNITS,) + rest))


def plain_shards(feed, entry):
    feed, entry = absolute_units(feed), absolute_units(entry)
    narrow = feed[:, :192].reshape(FF, D)
    leave = feed[:, 192:240].reshape(D, D)
    widen = feed[:, 240:432].reshape(UNITS, 4, 48, 2, HALF).transpose(0, 2, 3, 1, 4).reshape(D, FF)
    vectors = entry[:, 144:].transpose(0, 2, 1, 3).reshape(32, -1)
    entry = entry[:, :144].reshape(UNITS, 3, 48, D).transpose(1, 0, 2, 3).reshape(3, D, D)
    scatter = lambda value, dim: lax.psum_scatter(value, AX, scatter_dimension=dim, tiled=True)
    rows = vectors.shape[0]
    cut, mid = 8 * D // rows, 8 * D // rows + FF // rows
    last = mid + H * NB // rows
    vec = vectors[:, :cut].reshape(rows, 8, -1).transpose(1, 0, 2).reshape(8, D)
    return (
        scatter(entry, 1),
        scatter(leave, 0),
        scatter(widen, 0),
        scatter(narrow, 0),
        scatter(vec, 1),
        scatter(vectors[:, cut:mid].reshape(-1), 0),
        scatter(vectors[:, mid:last].reshape(-1), 0),
    )


def plain_gather(entry, leave, widen, narrow):
    gather = lambda value, dim: lax.all_gather(value, AX, axis=dim, tiled=True)
    widen = gather(widen, 0).reshape(D, 4, D).transpose(1, 0, 2)
    return (
        (gather(entry, 1),),
        (gather(leave, 0),),
        (widen,),
        (gather(narrow, 0).reshape(64, 48, D),),
    )


def plain_vectors(*small):
    gather = lambda value, dim: lax.all_gather(value, AX, axis=dim, tiled=True)
    parts = []
    for value in small:
        full = gather(value, value.ndim - 1)
        if value.ndim == 2:
            parts.append(full.reshape(8, 32, 24).transpose(1, 0, 2))
        else:
            parts.append(full.reshape(32, -1))
    slabs = vector_slab(*parts).reshape(4, 4, 2, 16, 128).transpose(2, 1, 0, 3, 4)
    return slabs[0].reshape(UNITS, 16, 128), slabs[1].reshape(UNITS, 16, 128)


def on_device(
    devices,
    hidden,
    lengths,
    cotangent,
    inflow,
    outflow,
    widener,
    narrower,
    shifts,
    offsets,
    distance,
    intake,
    outtake,
    expander,
    squeezer,
    adjusts,
    leanings,
    spacing,
):
    rows, seq, width = hidden.shape
    half = seq // 2
    fast = devices == 32
    index = lax.axis_index(AX)
    core = index % 2
    halved = (lengths + 1) // 2
    layer_one = (inflow, outflow, widener, narrower)
    layer_two = (intake, outtake, expander, squeezer)

    small = (shifts, offsets, distance, adjusts, leanings, spacing)
    if fast:
        ticks = Ticks(index.astype(jnp.int32).reshape(1))
        tick = ticks.run
        vec = Job(vector_stages, vector_slab(*small))
        eo1, w1 = gather_jobs(core, (True, None), *layer_one)
        eo2, w2 = gather_jobs(core, (False, False), *layer_two)
        tick([eo1, vec, w1])
        tick([eo1, vec, w1])
        tick([eo1, vec, w1])
        prepared = tick([eo1, w1], lambda me: prepare(me, *vec.result, seq, half))
        tick([eo1, eo2, w2])
    else:
        ticks = Ticks(jnp.zeros((1,), jnp.int32))
        eo1 = w1 = eo2 = w2 = None
        plain_one, plain_two = plain_gather(*layer_one), plain_gather(*layer_two)
        prepared = prepare(ticks.me, *plain_vectors(*small), seq, half)

        def tick(jobs, kernel=None):
            return ticks.run([], kernel)

    def weights(layer, names):
        if fast:
            jobs = {"e": (eo1, eo2), "o": (eo1, eo2), "w": (w1, w2), "n": (w1, w2)}
            return [jobs[name][layer].result for name in names]
        return [(plain_one, plain_two)[layer]["eown".index(name)] for name in names]

    vec1, bias1, tab1, vec2, bias2, tab2 = prepared
    flatten = lambda value: value.reshape(-1, D)
    part = rows // 2

    def begin(stride, me, lens, x, vec_in, layer, tab):
        made = project(stride, me, lens, x, vec_in, *weights(layer, "e"))
        q, k, v = made[-3:]
        return made, attend(stride, me, lens, q, k, v, tab, 0, part)

    def finish(stride, me, lens, made, tab, head):
        return attend(stride, me, lens, *made[-3:], tab, part, rows - part, head)

    made1, head = tick([w1, eo2, w2], lambda me: begin(2, me, lengths, hidden, vec1, 0, tab1))
    ctx1, probs1 = tick([w1, eo2], lambda me: finish(2, me, lengths, made1, tab1, head))
    pooled, pooled_low, q1, k1, v1 = made1
    tick([w1])
    u1, act1, slope1, before1, first_out = tick(
        [eo2, w2],
        lambda me: expand(me, flatten(ctx1), flatten(pooled), vec1, bias1, *weights(0, "own")),
    )
    pooled_layer = first_out.reshape(rows, half, width)

    tick([eo2])
    tick([eo2])
    made2, head = tick([w2], lambda me: begin(1, me, halved, pooled_layer, vec2, 1, tab2))
    ctx2, probs2 = tick([w2], lambda me: finish(1, me, halved, made2, tab2, head))
    q2, k2, v2 = made2
    tick([w2])
    u2, act2, slope2, before2, second_out = tick(
        [], lambda me: expand(me, flatten(ctx2), first_out, vec2, bias2, *weights(1, "own"))
    )

    def reducing(pair, cuts, direct=False):
        return Job(reduce_stages, core, cuts, direct, *pair) if fast else pair

    dback, mixed_low, dhid, dattn, dctx, dvec, dbias = tick(
        [],
        lambda me: contract(me, cotangent.reshape(-1, D), before2, slope2, u2, vec2, *weights(1, "own")),
    )

    narrow2 = tick([], lambda me: narrow_grad(240, me, act2, dback, flatten(ctx2), dattn))
    sumn2 = reducing(narrow2, NARROW_CUTS)
    widen2 = tick([sumn2], lambda me: widen_grad(192, me, mixed_low, dhid, ()))
    sumw2 = reducing(widen2, WIDEN_CUTS)
    back = tick(
        [sumn2, sumw2],
        lambda me: retrace(1, me, halved, q2, k2, v2, dctx.reshape(q2.shape), probs2, 0, rows),
    )
    dq, dk, dv, dvec_top, diag, ends = back
    packed = vectors_by_unit(dvec + dvec_top, dbias, table_grad(1, diag, ends))

    def entry_end(me):
        made = entry_grad(160, 0, me, halved, pooled_layer, pooled_layer, dq, dk, dv, packed, ())
        parts = (dq, dk, dv, dattn.reshape(q2.shape), *weights(1, "e"))
        return made, input_grads(1, me, halved, *parts, 0, rows)

    entry2, dlayer = tick([sumn2, sumw2], entry_end)
    sume2 = reducing(entry2, ENTRY_CUTS)

    dback, mixed_low, dhid, dattn, dctx, dvec, dbias = tick(
        [sumw2, sumn2, sume2],
        lambda me: contract(me, flatten(dlayer), before1, slope1, u1, vec1, *weights(0, "own")),
    )
    narrow1 = tick(
        [sumw2, sumn2, sume2], lambda me: narrow_grad(240, me, act1, dback, flatten(ctx1), dattn)
    )
    sumn1 = reducing(narrow1, NARROW_CUTS)
    widen1 = tick([sumn1, sumw2, sume2], lambda me: widen_grad(192, me, mixed_low, dhid, ()))
    sumw1 = reducing(widen1, WIDEN_CUTS)
    parts = (q1, k1, v1, dctx.reshape(q1.shape), probs1)
    head = tick([sumn1, sumw1, sume2, sumn2], lambda me: retrace(2, me, lengths, *parts, 0, part))
    back = tick(
        [sumn1, sumw1, sume2], lambda me: retrace(2, me, lengths, *parts, part, rows - part, head[:3])
    )
    dq, dk, dv = back[:3]
    dvec_top, diag, ends = [one + two for one, two in zip(head[3:], back[3:])]
    packed = vectors_by_unit(dvec + dvec_top, dbias, table_grad(2, diag, ends))
    entry1 = tick(
        [sumw1, sumn1, sumw2],
        lambda me: entry_grad(160, 0, me, lengths, pooled_low, hidden, dq, dk, dv, packed, ()),
    )
    sume1 = reducing(entry1, ENTRY_CUTS, True)
    parts = (dq, dk, dv, dattn.reshape(q1.shape), *weights(0, "e"))
    ends = (0, 1, 2, rows) if rows > 2 else (0, rows)
    beside = ([sume1, sumn1, sume2], [sume1, sumn1], [sume1, sumw1])
    done = ()
    for first, last, jobs in zip(ends, ends[1:], beside):
        done = (
            tick(
                jobs,
                lambda me: input_grads(2, me, lengths, *parts, first, last - first, done),
            ),
        )
    (hidden_grad,) = done
    if fast:
        for job in (sume1, sumw1, sumn1, sumn2, sumw2, sume2):
            while job.result is None:
                tick([job, sumw1] if job is sume1 else [job])
        left, right, rest = sume2.result
        feed = [jnp.concatenate(sides) for sides in zip(sumn2.result[:2], sumw2.result[:2])]
        shards_two = (entry_shards(left, right),) + feed_shards(*feed)
        shards_two = shards_two + split_vectors(rest.reshape(-1), 32)
        left, right, rest = sume1.result
        feed = [jnp.concatenate(sides) for sides in zip(sumn1.result[:2], sumw1.result[:2])]
        shards_one = (entry_shards(left, right),) + feed_shards(*feed)
        shards_one = shards_one + split_vectors(rest.reshape(-1), 32)
    else:
        feed2 = [jnp.concatenate(sides, axis=1) for sides in zip(narrow2, widen2)]
        feed1 = [jnp.concatenate(sides, axis=1) for sides in zip(narrow1, widen1)]
        shards_one, shards_two = plain_shards(feed1, entry1), plain_shards(feed2, entry2)
    return (
        pooled_layer,
        second_out.reshape(rows, half, width),
        hidden_grad,
        *shards_one,
        *shards_two[:4],
        shards_two[4][1:],
        shards_two[5],
        shards_two[6],
        shards_two[4][0],
    )


def solution(mesh):
    both = ("wide", "narrow")
    rows = P(both, None, None)
    weights = (
        P(None, both, None),
        P(both, None),
        P(both, None),
        P(both, None),
        P(None, both),
        P(both),
        P(both),
    )
    return jax.shard_map(
        partial(on_device, mesh.size),
        mesh=mesh,
        in_specs=(rows, P(both), rows) + weights + weights,
        out_specs=(rows, rows, rows) + weights + weights + (P(both),),
        check_vma=False,
    )
```
